32 devices in a mesh: groups: 2 (over x), wide: 16 (over z, y, core).
Axes of the slice: x: 2, y: 2, z: 4, core: 2. Of those that a mesh axis runs over, the one named last changes fastest.
Arguments:
- tokens: bfloat16 [4096, 5120], P(('groups', 'wide')), parts along dimension 0, may hold values from -6 to 6
- query_output_gradient: bfloat16 [4096, 4096], P(('groups', 'wide')), parts along dimension 0, may hold values from -6 to 6
- down_factors: bfloat16 [5120, 4096], P('wide', 'groups'), parts along dimension 1, may hold values from -0.078125 to 0.078125
- up_factors_transposed: bfloat16 [4096, 4096], P('wide', 'groups'), parts along dimension 1, may hold values from -0.09375 to 0.09375
- tenant_of_block: int32 [32], P('groups'), parts along dimension 0, may hold values from 0 to 63
- device_tenant_list: int32 [32, 4], P(('groups', 'wide')), parts along dimension 0, may hold values from 0 to 63
- row_list_entry: int32 [128], P(('groups', 'wide')), parts along dimension 0, may hold values from 0 to 3
- hidden: bfloat16 [128, 5120], P(('groups', 'wide')), parts along dimension 0, may hold values from -6 to 6
- base_query_rows: bfloat16 [128, 4096], P(('groups', 'wide')), parts along dimension 0, may hold values from -6 to 6
- cached_key_rows: bfloat16 [128, 256, 512], P(('groups', 'wide')), parts along dimension 0, may hold values from -6 to 6
- cached_value_rows: bfloat16 [128, 256, 512], P(('groups', 'wide')), parts along dimension 0, may hold values from -6 to 6
- live_cache_length: int32 [128], P(('groups', 'wide')), parts along dimension 0, may hold values from 1 to 256, 10240 in all
Outputs:
- down_gradient: float32 [5120, 4096], P('wide', 'groups'), parts along dimension 1
- up_gradient: float32 [4096, 4096], P('wide', 'groups'), parts along dimension 1
- attended: bfloat16 [128, 4096], P(('groups', 'wide')), parts along dimension 0
The draws below stay inside these ranges and needn't reach their ends.
There are 2 independent parts, one for each index of `groups`. The reference program is written for one: setup_inputs(seed, part) draws one part's arguments, and reference() takes and returns one part's arrays. A program takes and returns all parts, laid end to end along the dimension named above; each array names one. Nothing has to cross between parts.
All inputs are finite; a program needn't handle non-finite values. No bound on the sum of `live_cache_length` on one device may be relied on, other than what follows from the above.
Results may differ from the reference program's by a relative error of at most 0.0056.
Values may be sent and summed in bfloat16 or wider, within the bound.
No kernel may reach another device: no remote copies, remote signals or barrier semaphores. Data moves between devices by JAX's collectives and lax.ppermute only.
A program may use at most 64 MiB of HBM per device.

```python
import math
import jax
import jax.numpy as jnp
import numpy as np
from jax import lax

MODEL_WIDTH = 5120
HEAD_DIM = 128
HEADS = 32
KV_HEADS = 4
RANK = 32
TENANTS = 64
BLOCK = 128
SLOTS = 4
ROWS_DEV = 4
CACHE = 256
QUERY_FEATURES = 4096
ALL_ADAPTER_COLS = 2048
TOKENS = 2048
BLOCKS = 16
ROWS = 64
SERVERS = 16


key_peak = 6.0


key_second = 5.9375


def aligned_layout(key):
    key_rows, key_kv, key_group, key_sign, key_size = jax.random.split(key, 5)
    row_index = jnp.arange(ROWS, dtype=jnp.int32)
    chosen = (jax.random.randint(key_rows, (ROWS,), 0, 4) == 0) | (row_index == 0)
    kv_index = jax.random.randint(key_kv, (ROWS,), 0, KV_HEADS)
    head_index = kv_index * (HEADS // KV_HEADS) + jax.random.randint(key_group, (ROWS,), 0, HEADS // KV_HEADS)
    sign_table = jnp.where(jax.random.bernoulli(key_sign, 0.5, (ROWS, HEAD_DIM)), 1.0, -1.0).astype(jnp.float32)
    target = jax.random.uniform(key_size, (ROWS,), jnp.float32, 130.0, 290.0)
    magnitude = jnp.minimum(target / (key_peak * jnp.sqrt(jnp.float32(HEAD_DIM))), 5.5)
    return (chosen, kv_index, head_index, sign_table, magnitude)


def draw_base_query_rows(key, part):
    chosen, kv_index, head_index, sign_table, magnitude = aligned_layout(key)
    key = jax.random.fold_in(key, 11)
    drawn = jnp.clip(jax.random.normal(key, (ROWS, QUERY_FEATURES), jnp.float32), -6.0, 6.0)
    per_head = drawn.reshape(ROWS, HEADS, HEAD_DIM)
    picked = chosen[:, None] & (jnp.arange(HEADS, dtype=jnp.int32)[None, :] == head_index[:, None])
    planted = magnitude[:, None, None] * sign_table[:, None, :]
    per_head = jnp.where(picked[:, :, None], planted, per_head)
    return per_head.reshape(ROWS, QUERY_FEATURES).astype(jnp.bfloat16)


def draw_cached_key_rows(key, part):
    chosen, kv_index, head_index, sign_table, magnitude = aligned_layout(key)
    key = jax.random.fold_in(key, 12)
    drawn = jnp.clip(jax.random.normal(key, (ROWS, CACHE, KV_HEADS, HEAD_DIM), jnp.float32), -6.0, 6.0)
    position = jnp.arange(CACHE, dtype=jnp.int32)
    height = jnp.where(position == 0, key_peak, jnp.where(position == 1, key_second, 0.0)).astype(jnp.float32)
    picked = chosen[:, None, None] & (position[None, :, None] < 2) & (jnp.arange(KV_HEADS, dtype=jnp.int32)[None, None, :] == kv_index[:, None, None])
    planted = height[None, :, None, None] * sign_table[:, None, None, :]
    mixed = jnp.where(picked[:, :, :, None], planted, drawn)
    return mixed.reshape(ROWS, CACHE, KV_HEADS * HEAD_DIM).astype(jnp.bfloat16)


def set_ends(drawn, rng, least, top_value):
    place = [jax.random.randint(jax.random.fold_in(rng, axis), (), 0, length) for axis, length in enumerate(drawn.shape)]
    main_axis = drawn.shape.index(max(drawn.shape))
    next_to = place[:main_axis] + [(place[main_axis] + 1) % drawn.shape[main_axis]] + place[main_axis + 1:]
    return drawn.at[tuple(place)].set(least).at[tuple(next_to)].set(top_value)


def block_scale(own_key, extent, pieces, low, high):
    gain, own = 1.0, jax.random.fold_in(own_key, 6)
    for dim, blocks in pieces:
        heights = jnp.exp(jax.random.uniform(jax.random.fold_in(own, dim), (blocks,), jnp.float32, low / len(pieces), high / len(pieces)))
        gain = gain * jnp.repeat(heights, extent[dim] // blocks).reshape([-1 if axis == dim else 1 for axis in range(len(extent))])
    return gain


def profile(amount, total, limit, skew):
    portions = [(1 << 20) // math.isqrt(standing ** skew) + 1 for standing in range(2, amount + 1)]
    surplus, given = total - limit - (amount - 1), [1] * (amount - 1)
    while surplus > 0:
        free = [i for i in range(amount - 1) if given[i] < limit]
        mass, remaining = sum([portions[i] for i in free]), surplus
        for i in free:
            extra = min(limit - given[i], max(1, remaining * portions[i] // mass), surplus)
            given[i] = given[i] + extra
            surplus = surplus - extra
    return np.array([limit] + given)


def uneven_parts(stream_key, number_of, total, reach, slope):
    if number_of == 2:
        one = jax.random.randint(stream_key, (), max(1, total - reach), min(reach, total - 1) + 1)
        return jnp.stack([one, total - one])
    lengths = jnp.asarray(profile(number_of, total, reach, slope), jnp.int32)
    twos = (number_of - 1) // 2
    donor, receiver = lengths[1:1 + 2 * twos:2], lengths[2:2 + 2 * twos:2]
    slack = jnp.minimum(donor - 1, reach - receiver)
    passed = jax.random.randint(jax.random.fold_in(stream_key, 1), (twos,), 0, 1 << 20) % (slack + 1)
    lengths = lengths.at[1:1 + 2 * twos:2].set(donor - passed).at[2:2 + 2 * twos:2].set(receiver + passed)
    return lengths[jax.random.permutation(jax.random.fold_in(stream_key, 2), number_of)]


def scatter_about(stream_key, shape, spread, limit, shards=(), held_as=jnp.bfloat16):
    factor_of = block_scale(stream_key, shape, shards, -0.22, 0.18) if shards else 1.0
    entries = jax.random.normal(stream_key, shape, jnp.float32) * spread * factor_of
    return jnp.minimum(jnp.maximum(entries, -limit), limit).astype(held_as)


def setup_inputs(seed: int = 0, part: int = 0) -> dict:
    arg_keys = jax.random.split(jax.random.key(seed), 13)
    part_keys = jax.random.split(jax.random.fold_in(arg_keys[12], part), 13)
    tokens = scatter_about(part_keys[0], (TOKENS, MODEL_WIDTH), 1.0, 6.0, ((0, 16),))
    query_output_gradient = scatter_about(part_keys[1], (TOKENS, QUERY_FEATURES), 1.0, 6.0, ((0, 16),))
    down_factors = scatter_about(part_keys[2], (MODEL_WIDTH, ALL_ADAPTER_COLS), MODEL_WIDTH ** -0.5, 0.078125, ((0, 16),))
    up_factors_transposed = scatter_about(part_keys[3], (QUERY_FEATURES, ALL_ADAPTER_COLS), QUERY_FEATURES ** -0.5, 0.09375, ((0, 16),))
    tenant_of_block = set_ends(jax.random.randint(part_keys[4], (BLOCKS,), 0, TENANTS), jax.random.fold_in(part_keys[4], 1), 0, TENANTS - 1).astype(jnp.int32)
    device_tenant_list = set_ends(jax.random.randint(part_keys[5], (SERVERS, SLOTS), 0, TENANTS), jax.random.fold_in(part_keys[5], 1), 0, TENANTS - 1).astype(jnp.int32)
    row_list_entry = set_ends(jax.random.randint(part_keys[6], (ROWS,), 0, SLOTS), jax.random.fold_in(part_keys[6], 1), 0, SLOTS - 1).astype(jnp.int32)
    hidden = scatter_about(part_keys[7], (ROWS, MODEL_WIDTH), 1.0, 6.0, ((0, 16),))
    base_query_rows = draw_base_query_rows(jax.random.fold_in(jax.random.fold_in(arg_keys[12], part), 71), part)
    cached_key_rows = draw_cached_key_rows(jax.random.fold_in(jax.random.fold_in(arg_keys[12], part), 71), part)
    cached_value_rows = scatter_about(part_keys[10], (ROWS, CACHE, KV_HEADS * HEAD_DIM), 1.0, 6.0, ((0, 16),))
    live_cache_length = uneven_parts(part_keys[11], ROWS, ROWS * CACHE * 5 // 8, CACHE, 2).astype(jnp.int32)
    return {"tokens": tokens, "query_output_gradient": query_output_gradient, "down_factors": down_factors, "up_factors_transposed": up_factors_transposed, "tenant_of_block": tenant_of_block, "device_tenant_list": device_tenant_list, "row_list_entry": row_list_entry, "hidden": hidden, "base_query_rows": base_query_rows, "cached_key_rows": cached_key_rows, "cached_value_rows": cached_value_rows, "live_cache_length": live_cache_length}


adapter_scale = 2.0
learning_rate = 0.0002

def pick_tenant_columns(table, tenants):
    grouped = table.reshape(table.shape[0], TENANTS, RANK)
    return jnp.take(grouped, tenants, axis=1)

def reference(tokens, query_output_gradient, down_factors, up_factors_transposed, tenant_of_block, device_tenant_list, row_list_entry, hidden, base_query_rows, cached_key_rows, cached_value_rows, live_cache_length):
    input_block = tokens.reshape(BLOCKS, BLOCK, MODEL_WIDTH).astype(jnp.float32)
    gb = query_output_gradient.reshape(BLOCKS, BLOCK, QUERY_FEATURES).astype(jnp.float32)
    selected_down = pick_tenant_columns(down_factors, tenant_of_block).astype(jnp.float32)
    selected_up = pick_tenant_columns(up_factors_transposed, tenant_of_block).astype(jnp.float32)
    down_projected = jnp.einsum('jwt,tjo->jwo', input_block, selected_down).astype(jnp.bfloat16)
    backward_input = jnp.einsum('bkq,qbr->bkr', gb, selected_up).astype(jnp.bfloat16)
    tenant_indicator = (tenant_of_block[:, None] == jnp.arange(TENANTS, dtype=jnp.int32)[None, :]).astype(jnp.float32)
    tenant_up_gradient = jnp.einsum('bkq,bkr->bqr', gb, down_projected.astype(jnp.float32))
    up_gradient = adapter_scale * jnp.einsum('pfx,pw->fwx', tenant_up_gradient, tenant_indicator, precision=lax.Precision.HIGHEST).reshape(QUERY_FEATURES, ALL_ADAPTER_COLS)
    tenant_down_gradient = jnp.einsum('vzu,vzh->vuh', input_block, backward_input.astype(jnp.float32))
    down_gradient = adapter_scale * jnp.einsum('xai,xk->aki', tenant_down_gradient, tenant_indicator, precision=lax.Precision.HIGHEST).reshape(MODEL_WIDTH, ALL_ADAPTER_COLS)
    updated_down = (down_factors.astype(jnp.float32) - learning_rate * down_gradient).astype(jnp.bfloat16)
    updated_up = (up_factors_transposed.astype(jnp.float32) - learning_rate * up_gradient).astype(jnp.bfloat16)
    owner = (jnp.arange(ROWS, dtype=jnp.int32) // ROWS_DEV).astype(jnp.int32)
    row_tenant = device_tenant_list[owner, row_list_entry].astype(jnp.int32)
    na_sel = pick_tenant_columns(updated_down, row_tenant).astype(jnp.float32)
    adapted_query = jnp.einsum('rd,drk->rk', hidden.astype(jnp.float32), na_sel).astype(jnp.bfloat16)
    selected_new_up = pick_tenant_columns(updated_up, row_tenant).astype(jnp.float32)
    query_change = adapter_scale * jnp.einsum('ez,jez->ej', adapted_query.astype(jnp.float32), selected_new_up)
    query = (base_query_rows.astype(jnp.float32) + query_change).astype(jnp.bfloat16)
    group = HEADS // KV_HEADS
    q_heads = query.reshape(ROWS, KV_HEADS, group, HEAD_DIM).astype(jnp.float32)
    keys = cached_key_rows.reshape(ROWS, CACHE, KV_HEADS, HEAD_DIM).astype(jnp.float32)
    values = cached_value_rows.reshape(ROWS, CACHE, KV_HEADS, HEAD_DIM).astype(jnp.float32)
    scores = jnp.einsum('rhgd,rphd->rhgp', q_heads, keys) / jnp.sqrt(jnp.float32(HEAD_DIM))
    live = jnp.arange(CACHE, dtype=jnp.int32)[None, :] < live_cache_length[:, None]
    scores = jnp.where(live[:, None, None, :], scores, jnp.float32(-1e+30))
    top = lax.optimization_barrier(jnp.max(scores, axis=-1, keepdims=True))
    expo = jnp.where(live[:, None, None, :], jnp.exp(scores - top), jnp.float32(0.0))
    weights = (expo / lax.optimization_barrier(jnp.sum(expo, axis=-1, keepdims=True))).astype(jnp.bfloat16)
    attended = jnp.einsum('rhgp,rphd->rhgd', weights.astype(jnp.float32), values)
    return (down_gradient, up_gradient, attended.reshape(ROWS, QUERY_FEATURES).astype(jnp.bfloat16))
```

```python
import functools

import jax
import jax.numpy as jnp
from jax import lax
from jax.experimental import pallas as pl
from jax.experimental.pallas import tpu as pltpu
from jax.sharding import PartitionSpec as P

HEAD_DIM = 128
HEADS = 32
KV_HEADS = 4
RANK = 32
TENANTS = 64
BLOCK = 128
ROWS_DEV = 4
LANES = 128
PER_TILE = LANES // RANK

adapter_scale = 2.0
learning_rate = 0.0002

F32 = jnp.float32
BF16 = jnp.bfloat16
VMEM_LIMIT = 40 * 1024 * 1024


def vmem():
    return pl.BlockSpec(memory_space=pltpu.VMEM)


def smem():
    return pl.BlockSpec(memory_space=pltpu.SMEM)


def call(kernel, out_shape, in_specs, scratch=(), flops=0, nbytes=0):
    single = not isinstance(out_shape, (list, tuple))
    return pl.pallas_call(
        kernel,
        out_shape=out_shape,
        in_specs=in_specs,
        out_specs=vmem() if single else [vmem()] * len(out_shape),
        scratch_shapes=list(scratch),
        compiler_params=pltpu.CompilerParams(vmem_limit_bytes=VMEM_LIMIT),
        cost_estimate=pl.CostEstimate(flops=flops, bytes_accessed=nbytes, transcendentals=0),
    )


def each(count, body):
    if count <= 16:
        for j in range(count):
            body(j)
    else:
        pl.loop(0, count)(body)


def dot(a, b, ca, cb):
    return lax.dot_general(a, b, (((ca,), (cb,)), ((), ())), preferred_element_type=F32)


def quarter_indicator(quarter, value):
    lane = lax.broadcasted_iota(jnp.int32, (RANK, LANES), 1)
    row = lax.broadcasted_iota(jnp.int32, (RANK, LANES), 0)
    return jnp.where(lane - row == quarter * RANK, value, 0.0).astype(BF16)


def tile_of(tenant):
    return pl.ds(pl.multiple_of((tenant // PER_TILE) * LANES, LANES), LANES)


def pick_kernel(t_ref, a_ref, b_ref, extra_ref, o_ref):
    fa, fb, w = a_ref.shape[0], b_ref.shape[0], extra_ref.shape[2]
    o_ref[...] = jnp.zeros_like(o_ref)

    def body(j):
        t = t_ref[j]
        pick = quarter_indicator(t % PER_TILE, 1.0)
        o_ref[j, :, :fb] = dot(pick, b_ref[:, tile_of(t)], 1, 1).astype(BF16)
        o_ref[j, :, fb : fb + fa] = dot(pick, a_ref[:, tile_of(t)], 1, 1).astype(BF16)
        o_ref[j, :, fb + fa : fb + fa + w] = extra_ref[j]

    each(t_ref.shape[0], body)


def block_kernel(x_ref, g_ref, r_ref, o_ref, wa_ref, wb_ref):
    n = r_ref.shape[0]
    fa, fb = x_ref.shape[1] // n, g_ref.shape[1] // n
    for d in range(n):
        wb_ref[:, d * fb : (d + 1) * fb] = r_ref[d, :, :fb]
        wa_ref[:, d * fa : (d + 1) * fa] = r_ref[d, :, fb : fb + fa]
    down = dot(wa_ref[...], x_ref[...], 1, 1).astype(BF16)
    back = dot(wb_ref[...], g_ref[...], 1, 1).astype(BF16)
    up_part = dot(down, g_ref[...], 1, 0).astype(BF16)
    down_part = dot(back, x_ref[...], 1, 0).astype(BF16)
    o_ref[...] = jnp.zeros_like(o_ref)
    for d in range(n):
        o_ref[d, :, :fb] = up_part[:, d * fb : (d + 1) * fb]
        o_ref[d, :, fb : fb + fa] = down_part[:, d * fa : (d + 1) * fa]


def sum_by_tenant(t_ref, part_ref, low, high, grad_ref):
    grad_ref[...] = jnp.zeros_like(grad_ref)

    def body(j):
        t = t_ref[j]
        place = quarter_indicator(t % PER_TILE, adapter_scale)
        grad_ref[:, tile_of(t)] += dot(part_ref[j, :, low:high], place, 0, 0)

    each(t_ref.shape[0], body)


def down_kernel(fb, t_ref, part_ref, a_ref, h_ref, u_ref, grad_ref, o_ref):
    fa = a_ref.shape[0]
    rows = h_ref.shape[0]
    sum_by_tenant(t_ref, part_ref, fb, fb + fa, grad_ref)
    new_a = (a_ref[...].astype(F32) - learning_rate * grad_ref[...]).astype(BF16)
    product = dot(h_ref[...], new_a, 1, 0)
    lane = lax.broadcasted_iota(jnp.int32, (rows, LANES), 1)
    tenant = u_ref[...]
    total = jnp.zeros((rows, LANES), F32)
    for c in range(TENANTS // PER_TILE):
        mine = tenant == c * PER_TILE + lane // RANK
        total = total + jnp.where(mine, product[:, c * LANES : (c + 1) * LANES], 0.0)
    half = total + pltpu.roll(total, 2 * RANK, 1)
    full = half + pltpu.roll(half, RANK, 1)
    quarter = rows // PER_TILE
    packed = jnp.zeros((quarter, LANES), F32)
    spot = lax.broadcasted_iota(jnp.int32, (quarter, LANES), 1) // RANK
    for q in range(PER_TILE):
        packed = packed + jnp.where(spot == q, full[q * quarter : (q + 1) * quarter], 0.0)
    for d in range(o_ref.shape[0]):
        o_ref[d] = packed


def up_kernel(t_ref, part_ref, b_ref, grad_ref, new_ref):
    sum_by_tenant(t_ref, part_ref, 0, b_ref.shape[0], grad_ref)
    new_ref[...] = (b_ref[...].astype(F32) - learning_rate * grad_ref[...]).astype(BF16)


def delta_kernel(p_ref, u_ref, new_ref, o_ref):
    n, quarter = p_ref.shape[0], p_ref.shape[1]
    total = p_ref[0]
    for d in range(1, n):
        total = total + p_ref[d]
    spot = lax.broadcasted_iota(jnp.int32, (quarter, LANES), 1) // RANK
    pieces = []
    for q in range(PER_TILE):
        one = jnp.where(spot == q, total, 0.0)
        half = one + pltpu.roll(one, 2 * RANK, 1)
        pieces.append(half + pltpu.roll(half, RANK, 1))
    adapted = jnp.concatenate(pieces, axis=0)
    rows = adapted.shape[0]
    lane = lax.broadcasted_iota(jnp.int32, (rows, LANES), 1)
    tenant = u_ref[...]
    spread = jnp.concatenate(
        [
            jnp.where(tenant == c * PER_TILE + lane // RANK, adapted, 0.0).astype(BF16)
            for c in range(TENANTS // PER_TILE)
        ],
        axis=1,
    )
    delta = adapter_scale * dot(spread, new_ref[...], 1, 1)
    for d in range(n):
        o_ref[d] = delta[d * ROWS_DEV : (d + 1) * ROWS_DEV]


def attention_kernel(len_ref, delta_ref, base_ref, k_ref, v_ref, o_ref):
    n = delta_ref.shape[0]
    delta = jnp.concatenate([delta_ref[d] for d in range(n)], axis=1)
    query = (base_ref[...] + delta).astype(BF16).astype(F32)
    group = HEADS // KV_HEADS
    cache = k_ref.shape[1]
    many = group * ROWS_DEV
    row_p = lax.broadcasted_iota(jnp.int32, (many, cache), 0) % ROWS_DEV
    row_d = lax.broadcasted_iota(jnp.int32, (many, HEAD_DIM), 0) % ROWS_DEV
    position = lax.broadcasted_iota(jnp.int32, (many, cache), 1)
    length = jnp.zeros((many, cache), jnp.int32)
    for r in range(ROWS_DEV):
        length = jnp.where(row_p == r, len_ref[r], length)
    live = position < length
    outs = []
    for g in range(KV_HEADS):
        cols = slice(g * HEAD_DIM, (g + 1) * HEAD_DIM)
        heads = jnp.concatenate(
            [query[:, (g * group + i) * HEAD_DIM : (g * group + i + 1) * HEAD_DIM] for i in range(group)],
            axis=0,
        ).astype(BF16)
        scores = jnp.zeros((many, cache), F32)
        for r in range(ROWS_DEV):
            scores = jnp.where(row_p == r, dot(heads, k_ref[r, :, cols], 1, 1), scores)
        scores = scores / jnp.sqrt(F32(HEAD_DIM))
        scores = jnp.where(live, scores, F32(-1e30))
        top = jnp.max(scores, axis=-1, keepdims=True)
        expo = jnp.where(live, jnp.exp(scores - top), 0.0)
        weights = (expo / jnp.sum(expo, axis=-1, keepdims=True)).astype(BF16)
        mixed = jnp.zeros((many, HEAD_DIM), F32)
        for r in range(ROWS_DEV):
            mixed = jnp.where(row_d == r, dot(weights, v_ref[r, :, cols], 1, 0), mixed)
        outs.extend(mixed[i * ROWS_DEV : (i + 1) * ROWS_DEV] for i in range(group))
    o_ref[...] = jnp.concatenate(outs, axis=1).astype(BF16)


def exchange(x):
    return lax.all_to_all(x, "wide", split_axis=0, concat_axis=0, tiled=True)


def per_device(
    tokens,
    query_output_gradient,
    down_factors,
    up_factors_transposed,
    tenant_of_block,
    device_tenant_list,
    row_list_entry,
    hidden,
    base_query_rows,
    cached_key_rows,
    cached_value_rows,
    live_cache_length,
):
    n = lax.axis_size("wide")
    fa, cols = down_factors.shape
    fb = up_factors_transposed.shape[0]
    local_rows = hidden.shape[0]
    rows = local_rows * n
    assert tokens.shape[0] == BLOCK and tenant_of_block.shape[0] == n
    wide = -(-(fa + fb + 1) // LANES) * LANES
    room = wide - fa - fb
    w = max(k for k in range(1, room + 1) if fa % k == 0)
    pieces = fa // w
    assert local_rows * (pieces + 1) <= RANK

    slot = row_list_entry[:, None] == jnp.arange(device_tenant_list.shape[1], dtype=jnp.int32)[None, :]
    row_tenant = jnp.sum(jnp.where(slot, device_tenant_list, 0), axis=1)
    slices = hidden.reshape(local_rows, n, pieces, w).transpose(1, 2, 0, 3).reshape(n, pieces * local_rows, w)
    marks = jnp.broadcast_to(row_tenant.astype(BF16)[None, :, None], (n, local_rows, w))
    extra = jnp.concatenate([slices, marks], axis=1)
    extra = jnp.pad(extra, ((0, 0), (0, RANK - extra.shape[1]), (0, 0)))

    packed = call(
        pick_kernel,
        jax.ShapeDtypeStruct((n, RANK, wide), BF16),
        [smem(), vmem(), vmem(), vmem()],
        flops=2 * RANK * LANES * n * (fa + fb),
        nbytes=2 * cols * (fa + fb),
    )(tenant_of_block, down_factors, up_factors_transposed, extra)
    got = exchange(packed)

    parts = call(
        block_kernel,
        jax.ShapeDtypeStruct((n, RANK, wide), BF16),
        [vmem(), vmem(), vmem()],
        scratch=[
            pltpu.VMEM((RANK, tokens.shape[1]), BF16),
            pltpu.VMEM((RANK, query_output_gradient.shape[1]), BF16),
        ],
        flops=4 * RANK * BLOCK * n * (fa + fb),
        nbytes=2 * BLOCK * n * (fa + fb),
    )(tokens, query_output_gradient, got)
    shares = exchange(parts)

    tail = got[:, :, fa + fb : fa + fb + w]
    h_cols = (
        tail[:, : pieces * local_rows]
        .reshape(n, pieces, local_rows, w)
        .transpose(0, 2, 1, 3)
        .reshape(rows, fa)
    )
    tenants = tail[:, pieces * local_rows : (pieces + 1) * local_rows, 0].reshape(rows, 1)
    tenants = jnp.broadcast_to(tenants.astype(jnp.int32), (rows, LANES))

    down_gradient, low_rank = call(
        functools.partial(down_kernel, fb),
        [
            jax.ShapeDtypeStruct((fa, cols), F32),
            jax.ShapeDtypeStruct((n, rows // PER_TILE, LANES), F32),
        ],
        [smem(), vmem(), vmem(), vmem(), vmem()],
        flops=2 * rows * fa * cols,
        nbytes=6 * cols * fa,
    )(tenant_of_block, shares, down_factors, h_cols, tenants)
    low_rank = exchange(low_rank)
    up_gradient, new_up = call(
        up_kernel,
        [jax.ShapeDtypeStruct((fb, cols), F32), jax.ShapeDtypeStruct((fb, cols), BF16)],
        [smem(), vmem(), vmem()],
        flops=2 * n * RANK * fb * LANES,
        nbytes=8 * cols * fb,
    )(tenant_of_block, shares, up_factors_transposed)
    delta = call(
        delta_kernel,
        jax.ShapeDtypeStruct((n, local_rows, fb), F32),
        [vmem(), vmem(), vmem()],
        flops=2 * rows * cols * fb,
        nbytes=2 * cols * fb,
    )(low_rank, tenants, new_up)
    delta = exchange(delta)
    attended = call(
        attention_kernel,
        jax.ShapeDtypeStruct((local_rows, HEADS * HEAD_DIM), BF16),
        [smem(), vmem(), vmem(), vmem(), vmem()],
        flops=4 * HEADS * local_rows * cached_key_rows.shape[1] * HEAD_DIM,
        nbytes=4 * cached_key_rows.size,
    )(live_cache_length, delta, base_query_rows.astype(F32), cached_key_rows, cached_value_rows)
    return down_gradient, up_gradient, attended


def solution(mesh):
    placed = (
        P(("groups", "wide"), None),
        P(("groups", "wide"), None),
        P("wide", "groups"),
        P("wide", "groups"),
        P("groups"),
        P(("groups", "wide"), None),
        P(("groups", "wide")),
        P(("groups", "wide"), None),
        P(("groups", "wide"), None),
        P(("groups", "wide"), None, None),
        P(("groups", "wide"), None, None),
        P(("groups", "wide")),
    )
    return jax.shard_map(
        per_device,
        mesh=mesh,
        in_specs=placed,
        out_specs=(P("wide", "groups"), P("wide", "groups"), P(("groups", "wide"), None)),
        check_vma=False,
    )
```

```python
import functools

import jax
import jax.numpy as jnp
from jax import lax
from jax.experimental import pallas as pl
from jax.experimental.pallas import tpu as pltpu
from jax.sharding import PartitionSpec as P

HEAD_DIM = 128
HEADS = 32
KV_HEADS = 4
RANK = 32
TENANTS = 64
BLOCK = 128
ROWS_DEV = 4
LANES = 128
PER_TILE = LANES // RANK

adapter_scale = 2.0
learning_rate = 0.0002

F32 = jnp.float32
BF16 = jnp.bfloat16
VMEM_LIMIT = 40 * 1024 * 1024


def vmem():
    return pl.BlockSpec(memory_space=pltpu.VMEM)


def smem():
    return pl.BlockSpec(memory_space=pltpu.SMEM)


def hbm():
    return pl.BlockSpec(memory_space=pltpu.HBM)


def call(kernel, out_shape, in_specs, out_specs, scratch=(), flops=0, nbytes=0):
    return pl.pallas_call(
        kernel,
        out_shape=out_shape,
        in_specs=in_specs,
        out_specs=out_specs,
        scratch_shapes=list(scratch),
        compiler_params=pltpu.CompilerParams(vmem_limit_bytes=VMEM_LIMIT),
        cost_estimate=pl.CostEstimate(flops=flops, bytes_accessed=nbytes, transcendentals=0),
    )


def each(count, body):
    if count <= 16:
        for j in range(count):
            body(j)
    else:
        pl.loop(0, count)(body)


def dot(a, b, ca, cb):
    return lax.dot_general(a, b, (((ca,), (cb,)), ((), ())), preferred_element_type=F32)


def quarter_indicator(quarter, value):
    lane = lax.broadcasted_iota(jnp.int32, (RANK, LANES), 1)
    row = lax.broadcasted_iota(jnp.int32, (RANK, LANES), 0)
    return jnp.where(lane - row == quarter * RANK, value, 0.0).astype(BF16)


def tile_of(tenant):
    return pl.ds(pl.multiple_of((tenant // PER_TILE) * LANES, LANES), LANES)


HALF = RANK // 2


def up_half(h, fa, fb):
    return slice(h * fb, (h + 1) * fb)


def down_half(h, fa, fb):
    return slice(2 * fb + h * fa, 2 * fb + (h + 1) * fa)


def halves(part, cut, fa, fb):
    return jnp.concatenate([part[:, cut(h, fa, fb)] for h in range(2)], axis=0)


def pick_kernel(t_ref, a_ref, b_ref, o_ref, a_buf, b_buf, o_buf, sem_a, sem_b, sem_o):
    n = t_ref.shape[0]
    fa, fb = a_ref.shape[0], b_ref.shape[0]

    def copies(j):
        cols = tile_of(t_ref[j])
        return (
            pltpu.make_async_copy(b_ref.at[:, cols], b_buf.at[j], sem_b.at[j]),
            pltpu.make_async_copy(a_ref.at[:, cols], a_buf.at[j], sem_a.at[j]),
        )

    def start(j):
        for copy in copies(j):
            copy.start()

    def body(j):
        for copy in copies(j):
            copy.wait()
        pick = quarter_indicator(t_ref[j] % PER_TILE, 1.0)
        up = dot(pick, b_buf[j], 1, 1).astype(BF16)
        down = dot(pick, a_buf[j], 1, 1).astype(BF16)
        for h in range(2):
            o_buf[j, :, up_half(h, fa, fb)] = up[h * HALF : (h + 1) * HALF]
            o_buf[j, :, down_half(h, fa, fb)] = down[h * HALF : (h + 1) * HALF]
        pltpu.make_async_copy(o_buf.at[j], o_ref.at[j], sem_o.at[j]).start()

    def finish(j):
        pltpu.make_async_copy(o_buf.at[j], o_ref.at[j], sem_o.at[j]).wait()

    each(n, start)
    each(n, body)
    each(n, finish)


def fold_rows(product, tenant):
    rows = product.shape[0]
    lane = lax.broadcasted_iota(jnp.int32, (rows, LANES), 1)
    total = jnp.zeros((rows, LANES), F32)
    for c in range(TENANTS // PER_TILE):
        mine = tenant == c * PER_TILE + lane // RANK
        total = total + jnp.where(mine, product[:, c * LANES : (c + 1) * LANES], 0.0)
    half = total + pltpu.roll(total, 2 * RANK, 1)
    return half + pltpu.roll(half, RANK, 1)


def rows_kernel(h_ref, x_ref, a_ref, hc_ref, u_ref, hx_ref, base_ref):
    hx_ref[...] = dot(h_ref[:, : x_ref.shape[1]], x_ref[...], 1, 1)
    base_ref[...] = fold_rows(dot(hc_ref[...], a_ref[...], 1, 0), u_ref[...])


def block_kernel(x_ref, g_ref, r_ref, o_ref, back_ref, wa_ref, wb_ref, o_buf, sem):
    n = r_ref.shape[0]
    fa, fb = x_ref.shape[1] // n, g_ref.shape[1] // n
    for d in range(n):
        for h in range(2):
            rank = slice(h * HALF, (h + 1) * HALF)
            wb_ref[rank, d * fb : (d + 1) * fb] = r_ref[d, :, up_half(h, fa, fb)]
            wa_ref[rank, d * fa : (d + 1) * fa] = r_ref[d, :, down_half(h, fa, fb)]
    down = dot(wa_ref[...], x_ref[...], 1, 1).astype(BF16)
    back = dot(wb_ref[...], g_ref[...], 1, 1).astype(BF16)
    back_ref[...] = back
    up_part = dot(down, g_ref[...], 1, 0).astype(BF16)
    down_part = dot(back, x_ref[...], 1, 0).astype(BF16)
    copies = []
    for d in range(n):
        for h in range(2):
            rank = slice(h * HALF, (h + 1) * HALF)
            o_buf[d, :, up_half(h, fa, fb)] = up_part[rank, d * fb : (d + 1) * fb]
            o_buf[d, :, down_half(h, fa, fb)] = down_part[rank, d * fa : (d + 1) * fa]
        copy = pltpu.make_async_copy(o_buf.at[d], o_ref.at[d], sem.at[d])
        copy.start()
        copies.append(copy)
    for copy in copies:
        copy.wait()


def share_kernel(t_ref, hx_ref, back_ref, base_ref, u_ref, o_ref):
    hx = hx_ref[...]
    high = hx.astype(BF16)
    low = (hx - high.astype(F32)).astype(BF16)
    back = jnp.concatenate([back_ref[...]] * PER_TILE, axis=0)
    change = dot(high, back, 1, 1) + dot(low, back, 1, 1)
    mine = u_ref[...] == t_ref[0]
    full = base_ref[...] - jnp.where(mine, learning_rate * (adapter_scale * change), 0.0)
    quarter = full.shape[0] // PER_TILE
    spot = lax.broadcasted_iota(jnp.int32, (quarter, LANES), 1) // RANK
    packed = jnp.zeros((quarter, LANES), F32)
    for q in range(PER_TILE):
        packed = packed + jnp.where(spot == q, full[q * quarter : (q + 1) * quarter], 0.0)
    o_ref[...] = packed


def sum_by_tenant(t_ref, part_ref, cut, fa, fb, grad_ref):
    grad_ref[...] = jnp.zeros_like(grad_ref)

    def body(j):
        t = t_ref[j]
        place = quarter_indicator(t % PER_TILE, adapter_scale)
        grad_ref[:, tile_of(t)] += dot(halves(part_ref.at[j], cut, fa, fb), place, 0, 0)

    each(t_ref.shape[0], body)


def delta_kernel(fa, t_ref, part_ref, b_ref, p_ref, u_ref, o_ref, grad_ref):
    n, fb = part_ref.shape[0], b_ref.shape[0]
    sum_by_tenant(t_ref, part_ref, up_half, fa, fb, grad_ref)
    new_b = (b_ref[...].astype(F32) - learning_rate * grad_ref[...]).astype(BF16)
    total = p_ref[...]
    spot = lax.broadcasted_iota(jnp.int32, total.shape, 1) // RANK
    pieces = []
    for q in range(PER_TILE):
        one = jnp.where(spot == q, total, 0.0)
        half = one + pltpu.roll(one, 2 * RANK, 1)
        pieces.append(half + pltpu.roll(half, RANK, 1))
    adapted = jnp.concatenate(pieces, axis=0)
    lane = lax.broadcasted_iota(jnp.int32, adapted.shape, 1)
    tenant = u_ref[...]
    spread = jnp.concatenate(
        [
            jnp.where(tenant == c * PER_TILE + lane // RANK, adapted, 0.0).astype(BF16)
            for c in range(TENANTS // PER_TILE)
        ],
        axis=1,
    )
    delta = adapter_scale * dot(spread, new_b, 1, 1)
    for d in range(n):
        o_ref[d] = delta[d * ROWS_DEV : (d + 1) * ROWS_DEV]


def gradient_kernel(t_ref, part_ref, down_ref, up_ref):
    fa, fb = down_ref.shape[0], up_ref.shape[0]
    sum_by_tenant(t_ref, part_ref, down_half, fa, fb, down_ref)
    sum_by_tenant(t_ref, part_ref, up_half, fa, fb, up_ref)


def attention_kernel(len_ref, delta_ref, base_ref, k_ref, v_ref, o_ref):
    n = delta_ref.shape[0]
    delta = jnp.concatenate([delta_ref[d] for d in range(n)], axis=1)
    query = (base_ref[...] + delta).astype(BF16).astype(F32)
    group = HEADS // KV_HEADS
    cache = k_ref.shape[1]
    many = group * ROWS_DEV
    row_p = lax.broadcasted_iota(jnp.int32, (many, cache), 0) % ROWS_DEV
    row_d = lax.broadcasted_iota(jnp.int32, (many, HEAD_DIM), 0) % ROWS_DEV
    position = lax.broadcasted_iota(jnp.int32, (many, cache), 1)
    length = jnp.zeros((many, cache), jnp.int32)
    for r in range(ROWS_DEV):
        length = jnp.where(row_p == r, len_ref[r], length)
    live = position < length
    outs = []
    for g in range(KV_HEADS):
        cols = slice(g * HEAD_DIM, (g + 1) * HEAD_DIM)
        heads = jnp.concatenate(
            [query[:, (g * group + i) * HEAD_DIM : (g * group + i + 1) * HEAD_DIM] for i in range(group)],
            axis=0,
        ).astype(BF16)
        scores = jnp.zeros((many, cache), F32)
        for r in range(ROWS_DEV):
            scores = jnp.where(row_p == r, dot(heads, k_ref[r, :, cols], 1, 1), scores)
        scores = scores / jnp.sqrt(F32(HEAD_DIM))
        scores = jnp.where(live, scores, F32(-1e30))
        top = jnp.max(scores, axis=-1, keepdims=True)
        expo = jnp.where(live, jnp.exp(scores - top), 0.0)
        weights = (expo / jnp.sum(expo, axis=-1, keepdims=True)).astype(BF16)
        mixed = jnp.zeros((many, HEAD_DIM), F32)
        for r in range(ROWS_DEV):
            mixed = jnp.where(row_d == r, dot(weights, v_ref[r, :, cols], 1, 0), mixed)
        outs.extend(mixed[i * ROWS_DEV : (i + 1) * ROWS_DEV] for i in range(group))
    o_ref[...] = jnp.concatenate(outs, axis=1).astype(BF16)


def exchange(x):
    return lax.all_to_all(x, "wide", split_axis=0, concat_axis=0, tiled=True)


def partner(x, bit):
    n = lax.axis_size("wide")
    return lax.ppermute(x, "wide", [(i, i ^ bit) for i in range(n)])


def gather_rows(x):
    n = lax.axis_size("wide")
    me = lax.axis_index("wide")
    held = x[None]
    bit = n // 2
    while bit:
        other = partner(held, bit)
        second = (me & bit) != 0
        pair = [jnp.where(second, other, held), jnp.where(second, held, other)]
        held = jnp.stack(pair, axis=1).reshape((2 * held.shape[0],) + x.shape)
        bit //= 2
    return held.reshape((n * x.shape[0],) + x.shape[1:])


def sum_all(x):
    bit = lax.axis_size("wide") // 2
    while bit:
        x = x + partner(x, bit)
        bit //= 2
    return x


def per_device(
    tokens,
    query_output_gradient,
    down_factors,
    up_factors_transposed,
    tenant_of_block,
    device_tenant_list,
    row_list_entry,
    hidden,
    base_query_rows,
    cached_key_rows,
    cached_value_rows,
    live_cache_length,
):
    n = lax.axis_size("wide")
    me = lax.axis_index("wide")
    fa, cols = down_factors.shape
    fb = up_factors_transposed.shape[0]
    local_rows = hidden.shape[0]
    rows = local_rows * n
    width = tokens.shape[1]
    assert tokens.shape[0] == BLOCK and tenant_of_block.shape[0] == n and n & (n - 1) == 0
    block_shape = (n, HALF, 2 * (fa + fb))

    packed = call(
        pick_kernel,
        jax.ShapeDtypeStruct(block_shape, BF16),
        [smem(), hbm(), hbm()],
        hbm(),
        scratch=[
            pltpu.VMEM((n, fa, LANES), BF16),
            pltpu.VMEM((n, fb, LANES), BF16),
            pltpu.VMEM(block_shape, BF16),
            pltpu.SemaphoreType.DMA((n,)),
            pltpu.SemaphoreType.DMA((n,)),
            pltpu.SemaphoreType.DMA((n,)),
        ],
        flops=2 * RANK * LANES * n * (fa + fb),
        nbytes=2 * cols * (fa + fb),
    )(tenant_of_block, down_factors, up_factors_transposed)
    got = exchange(packed)

    slot = row_list_entry[:, None] == jnp.arange(device_tenant_list.shape[1], dtype=jnp.int32)[None, :]
    row_tenant = jnp.sum(jnp.where(slot, device_tenant_list, 0), axis=1)
    marks = jnp.broadcast_to(row_tenant.astype(BF16)[:, None], (local_rows, LANES))
    everyone = gather_rows(jnp.concatenate([hidden, marks], axis=1))
    tenants = everyone[:, width:].astype(jnp.int32)
    h_cols = lax.dynamic_slice(everyone, (0, me * fa), (rows, fa))
    hx, base_low_rank = call(
        rows_kernel,
        [jax.ShapeDtypeStruct((rows, BLOCK), F32), jax.ShapeDtypeStruct((rows, LANES), F32)],
        [vmem()] * 5,
        [vmem()] * 2,
        flops=2 * rows * BLOCK * width + 2 * rows * fa * cols,
        nbytes=2 * BLOCK * width + 2 * fa * cols,
    )(everyone, tokens, down_factors, h_cols, tenants)

    parts, back = call(
        block_kernel,
        [jax.ShapeDtypeStruct(block_shape, BF16), jax.ShapeDtypeStruct((RANK, BLOCK), BF16)],
        [vmem(), vmem(), vmem()],
        [hbm(), vmem()],
        scratch=[
            pltpu.VMEM((RANK, width), BF16),
            pltpu.VMEM((RANK, query_output_gradient.shape[1]), BF16),
            pltpu.VMEM(block_shape, BF16),
            pltpu.SemaphoreType.DMA((n,)),
        ],
        flops=4 * RANK * BLOCK * n * (fa + fb),
        nbytes=2 * BLOCK * n * (fa + fb),
    )(tokens, query_output_gradient, got)
    shares = exchange(parts)

    my_tenant = lax.dynamic_slice(tenant_of_block, (me,), (1,))
    low_rank = call(
        share_kernel,
        jax.ShapeDtypeStruct((rows // PER_TILE, LANES), F32),
        [smem(), vmem(), vmem(), vmem(), vmem()],
        vmem(),
        flops=4 * rows * BLOCK * LANES,
        nbytes=12 * rows * LANES,
    )(my_tenant, hx, back, base_low_rank, tenants)
    low_rank = sum_all(low_rank)

    delta = call(
        functools.partial(delta_kernel, fa),
        jax.ShapeDtypeStruct((n, local_rows, fb), F32),
        [smem(), vmem(), vmem(), vmem(), vmem()],
        vmem(),
        scratch=[pltpu.VMEM((fb, cols), F32)],
        flops=2 * rows * cols * fb,
        nbytes=2 * cols * fb,
    )(tenant_of_block, shares, up_factors_transposed, low_rank, tenants)
    delta = exchange(delta)

    down_gradient, up_gradient = call(
        gradient_kernel,
        [jax.ShapeDtypeStruct((fa, cols), F32), jax.ShapeDtypeStruct((fb, cols), F32)],
        [smem(), vmem()],
        [vmem(), vmem()],
        flops=2 * n * RANK * (fa + fb) * LANES,
        nbytes=4 * cols * (fa + fb),
    )(tenant_of_block, shares)
    attended = call(
        attention_kernel,
        jax.ShapeDtypeStruct((local_rows, HEADS * HEAD_DIM), BF16),
        [smem(), vmem(), vmem(), vmem(), vmem()],
        vmem(),
        flops=4 * HEADS * local_rows * cached_key_rows.shape[1] * HEAD_DIM,
        nbytes=4 * cached_key_rows.size,
    )(live_cache_length, delta, base_query_rows.astype(F32), cached_key_rows, cached_value_rows)
    return down_gradient, up_gradient, attended


def solution(mesh):
    placed = (
        P(("groups", "wide"), None),
        P(("groups", "wide"), None),
        P("wide", "groups"),
        P("wide", "groups"),
        P("groups"),
        P(("groups", "wide"), None),
        P(("groups", "wide")),
        P(("groups", "wide"), None),
        P(("groups", "wide"), None),
        P(("groups", "wide"), None, None),
        P(("groups", "wide"), None, None),
        P(("groups", "wide")),
    )
    return jax.shard_map(
        per_device,
        mesh=mesh,
        in_specs=placed,
        out_specs=(P("wide", "groups"), P("wide", "groups"), P(("groups", "wide"), None)),
        check_vma=False,
    )
```

```python
import functools

import jax
import jax.numpy as jnp
from jax import lax
from jax.experimental import pallas as pl
from jax.experimental.pallas import tpu as pltpu
from jax.sharding import PartitionSpec as P

HEAD_DIM = 128
HEADS = 32
KV_HEADS = 4
RANK = 32
TENANTS = 64
BLOCK = 128
ROWS_DEV = 4
LANES = 128
PER_TILE = LANES // RANK

adapter_scale = 2.0
learning_rate = 0.0002

F32 = jnp.float32
BF16 = jnp.bfloat16
VMEM_LIMIT = 40 * 1024 * 1024
ALL_VMEM = 60 * 1024 * 1024


def vmem():
    return pl.BlockSpec(memory_space=pltpu.VMEM)


def smem():
    return pl.BlockSpec(memory_space=pltpu.SMEM)


def hbm():
    return pl.BlockSpec(memory_space=pltpu.HBM)


def call(kernel, out_shape, in_specs, out_specs, scratch=(), flops=0, nbytes=0, limit=VMEM_LIMIT):
    return pl.pallas_call(
        kernel,
        out_shape=out_shape,
        in_specs=in_specs,
        out_specs=out_specs,
        scratch_shapes=list(scratch),
        compiler_params=pltpu.CompilerParams(vmem_limit_bytes=limit),
        cost_estimate=pl.CostEstimate(flops=flops, bytes_accessed=nbytes, transcendentals=0),
    )


def each(count, body):
    if count <= 16:
        for j in range(count):
            body(j)
    else:
        pl.loop(0, count)(body)


def dot(a, b, ca, cb):
    return lax.dot_general(a, b, (((ca,), (cb,)), ((), ())), preferred_element_type=F32)


def quarter_indicator(quarter, value):
    lane = lax.broadcasted_iota(jnp.int32, (RANK, LANES), 1)
    row = lax.broadcasted_iota(jnp.int32, (RANK, LANES), 0)
    return jnp.where(lane - row == quarter * RANK, value, 0.0).astype(BF16)


def tile_of(tenant):
    return pl.ds(pl.multiple_of((tenant // PER_TILE) * LANES, LANES), LANES)


HALF = RANK // 2


def pick_kernel(t_ref, table_ref, *refs):
    extra_ref = refs[0] if len(refs) == 6 else None
    o_ref, table, o_buf, sem_in, sem_out = refs[-5:]
    n, f = t_ref.shape[0], table_ref.shape[0]
    chunks = sem_in.shape[0]
    step = f // chunks
    loads = []
    for c in range(chunks):
        rows = slice(c * step, (c + 1) * step)
        load = pltpu.make_async_copy(table_ref.at[rows], table.at[rows], sem_in.at[c])
        load.start()
        loads.append(load)
    for load in loads:
        load.wait()

    def body(j):
        t = t_ref[j]
        got = dot(quarter_indicator(t % PER_TILE, 1.0), table[:, tile_of(t)], 1, 1).astype(BF16)
        if extra_ref is None:
            o_buf[j] = got
        else:
            o_buf[j, :, :f] = got[:HALF]
            o_buf[j, :, f : 2 * f] = got[HALF:]
            o_buf[j, :, o_buf.shape[2] - LANES :] = extra_ref[j]
        pltpu.make_async_copy(o_buf.at[j], o_ref.at[j], sem_out.at[j]).start()

    def finish(j):
        pltpu.make_async_copy(o_buf.at[j], o_ref.at[j], sem_out.at[j]).wait()

    each(n, body)
    each(n, finish)


def back_kernel(g_ref, x_ref, r_ref, o_ref, w_ref):
    n, fb = r_ref.shape[0], r_ref.shape[2]
    fa = x_ref.shape[1] // n
    for d in range(n):
        w_ref[:, d * fb : (d + 1) * fb] = r_ref[d]
    back = dot(w_ref[...], g_ref[...], 1, 1).astype(BF16)
    part = dot(back, x_ref[...], 1, 0).astype(BF16)
    for d in range(n):
        for h in range(2):
            o_ref[d, :, h * fa : (h + 1) * fa] = part[h * HALF : (h + 1) * HALF, d * fa : (d + 1) * fa]


def down_kernel(x_ref, g_ref, r_ref, o_ref, w_ref):
    n, fb = o_ref.shape[0], o_ref.shape[2]
    fa = x_ref.shape[1] // n
    for d in range(n):
        for h in range(2):
            w_ref[h * HALF : (h + 1) * HALF, d * fa : (d + 1) * fa] = r_ref[d, :, h * fa : (h + 1) * fa]
    down = dot(w_ref[...], x_ref[...], 1, 1).astype(BF16)
    part = dot(down, g_ref[...], 1, 0).astype(BF16)
    for d in range(n):
        o_ref[d] = part[:, d * fb : (d + 1) * fb]


def sum_by_tenant(t_ref, part_ref, grad_ref):
    f = grad_ref.shape[0]
    grad_ref[...] = jnp.zeros_like(grad_ref)

    def body(j):
        t = t_ref[j]
        part = part_ref[j]
        if part.shape[0] == HALF:
            part = jnp.concatenate([part[:, :f], part[:, f:]], axis=0)
        place = quarter_indicator(t % PER_TILE, adapter_scale)
        grad_ref[:, tile_of(t)] += dot(part, place, 0, 0)

    each(t_ref.shape[0], body)


def updated(table_ref, grad_ref):
    return (table_ref[...].astype(F32) - learning_rate * grad_ref[...]).astype(BF16)


def fold_rows(product, tenant):
    rows = product.shape[0]
    lane = lax.broadcasted_iota(jnp.int32, (rows, LANES), 1)
    total = jnp.zeros((rows, LANES), F32)
    for c in range(TENANTS // PER_TILE):
        mine = tenant == c * PER_TILE + lane // RANK
        total = total + jnp.where(mine, product[:, c * LANES : (c + 1) * LANES], 0.0)
    half = total + pltpu.roll(total, 2 * RANK, 1)
    return half + pltpu.roll(half, RANK, 1)


def share_kernel(t_ref, part_ref, a_ref, h_ref, u_ref, o_ref, grad_ref):
    sum_by_tenant(t_ref, part_ref, grad_ref)
    full = fold_rows(dot(h_ref[...], updated(a_ref, grad_ref), 1, 0), u_ref[...])
    quarter = full.shape[0] // PER_TILE
    spot = lax.broadcasted_iota(jnp.int32, (quarter, LANES), 1) // RANK
    packed = jnp.zeros((quarter, LANES), F32)
    for q in range(PER_TILE):
        packed = packed + jnp.where(spot == q, full[q * quarter : (q + 1) * quarter], 0.0)
    for d in range(o_ref.shape[0]):
        o_ref[d] = packed


def up_kernel(t_ref, part_ref, b_ref, grad_ref, new_ref):
    sum_by_tenant(t_ref, part_ref, grad_ref)
    new_ref[...] = updated(b_ref, grad_ref)


def delta_kernel(p_ref, u_ref, new_ref, o_ref):
    n, quarter = p_ref.shape[0], p_ref.shape[1]
    total = p_ref[0]
    for d in range(1, n):
        total = total + p_ref[d]
    spot = lax.broadcasted_iota(jnp.int32, (quarter, LANES), 1) // RANK
    pieces = []
    for q in range(PER_TILE):
        one = jnp.where(spot == q, total, 0.0)
        half = one + pltpu.roll(one, 2 * RANK, 1)
        pieces.append(half + pltpu.roll(half, RANK, 1))
    adapted = jnp.concatenate(pieces, axis=0)
    lane = lax.broadcasted_iota(jnp.int32, adapted.shape, 1)
    tenant = u_ref[...]
    spread = jnp.concatenate(
        [
            jnp.where(tenant == c * PER_TILE + lane // RANK, adapted, 0.0).astype(BF16)
            for c in range(TENANTS // PER_TILE)
        ],
        axis=1,
    )
    delta = adapter_scale * dot(spread, new_ref[...], 1, 1)
    for d in range(n):
        o_ref[d] = delta[d * ROWS_DEV : (d + 1) * ROWS_DEV]


def attention_kernel(len_ref, delta_ref, base_ref, k_ref, v_ref, o_ref):
    n = delta_ref.shape[0]
    delta = jnp.concatenate([delta_ref[d] for d in range(n)], axis=1)
    query = (base_ref[...] + delta).astype(BF16).astype(F32)
    group = HEADS // KV_HEADS
    cache = k_ref.shape[1]
    many = group * ROWS_DEV
    row_p = lax.broadcasted_iota(jnp.int32, (many, cache), 0) % ROWS_DEV
    row_d = lax.broadcasted_iota(jnp.int32, (many, HEAD_DIM), 0) % ROWS_DEV
    position = lax.broadcasted_iota(jnp.int32, (many, cache), 1)
    length = jnp.zeros((many, cache), jnp.int32)
    for r in range(ROWS_DEV):
        length = jnp.where(row_p == r, len_ref[r], length)
    live = position < length
    outs = []
    for g in range(KV_HEADS):
        cols = slice(g * HEAD_DIM, (g + 1) * HEAD_DIM)
        heads = jnp.concatenate(
            [query[:, (g * group + i) * HEAD_DIM : (g * group + i + 1) * HEAD_DIM] for i in range(group)],
            axis=0,
        ).astype(BF16)
        scores = jnp.zeros((many, cache), F32)
        for r in range(ROWS_DEV):
            scores = jnp.where(row_p == r, dot(heads, k_ref[r, :, cols], 1, 1), scores)
        scores = scores / jnp.sqrt(F32(HEAD_DIM))
        scores = jnp.where(live, scores, F32(-1e30))
        top = jnp.max(scores, axis=-1, keepdims=True)
        expo = jnp.where(live, jnp.exp(scores - top), 0.0)
        weights = (expo / jnp.sum(expo, axis=-1, keepdims=True)).astype(BF16)
        mixed = jnp.zeros((many, HEAD_DIM), F32)
        for r in range(ROWS_DEV):
            mixed = jnp.where(row_d == r, dot(weights, v_ref[r, :, cols], 1, 0), mixed)
        outs.extend(mixed[i * ROWS_DEV : (i + 1) * ROWS_DEV] for i in range(group))
    o_ref[...] = jnp.concatenate(outs, axis=1).astype(BF16)


def exchange(x):
    return lax.all_to_all(x, "wide", split_axis=0, concat_axis=0, tiled=True)


def per_device(
    tokens,
    query_output_gradient,
    down_factors,
    up_factors_transposed,
    tenant_of_block,
    device_tenant_list,
    row_list_entry,
    hidden,
    base_query_rows,
    cached_key_rows,
    cached_value_rows,
    live_cache_length,
):
    n = lax.axis_size("wide")
    fa, cols = down_factors.shape
    fb = up_factors_transposed.shape[0]
    local_rows = hidden.shape[0]
    rows = local_rows * n
    width = tokens.shape[1]
    features = query_output_gradient.shape[1]
    pieces = -(-fa // LANES)
    assert tokens.shape[0] == BLOCK and tenant_of_block.shape[0] == n and local_rows * (pieces + 1) <= HALF

    def pick(table, extra):
        f = table.shape[0]
        chunks = 4 if f % 64 == 0 else 1
        lanes = -(-2 * f // LANES) * LANES + LANES
        shape = (n, RANK, f) if extra is None else (n, HALF, lanes)
        return call(
            pick_kernel,
            jax.ShapeDtypeStruct(shape, BF16),
            [smem(), hbm()] + ([] if extra is None else [vmem()]),
            hbm(),
            scratch=[
                pltpu.VMEM(table.shape, BF16),
                pltpu.VMEM(shape, BF16),
                pltpu.SemaphoreType.DMA((chunks,)),
                pltpu.SemaphoreType.DMA((n,)),
            ],
            flops=2 * RANK * LANES * n * f,
            nbytes=2 * cols * f,
            limit=ALL_VMEM,
        )(tenant_of_block, table, *([] if extra is None else [extra]))

    got_up = exchange(pick(up_factors_transposed, None))

    slot = row_list_entry[:, None] == jnp.arange(device_tenant_list.shape[1], dtype=jnp.int32)[None, :]
    row_tenant = jnp.sum(jnp.where(slot, device_tenant_list, 0), axis=1)
    slices = jnp.pad(hidden.reshape(local_rows, n, fa), ((0, 0), (0, 0), (0, pieces * LANES - fa)))
    slices = slices.reshape(local_rows, n, pieces, LANES).transpose(1, 2, 0, 3).reshape(n, pieces * local_rows, LANES)
    marks = jnp.broadcast_to(row_tenant.astype(BF16)[None, :, None], (n, local_rows, LANES))
    extra = jnp.concatenate([slices, marks], axis=1)
    extra = jnp.pad(extra, ((0, 0), (0, HALF - extra.shape[1]), (0, 0)))
    got_down = exchange(pick(down_factors, extra))

    down_parts = call(
        back_kernel,
        jax.ShapeDtypeStruct((n, HALF, 2 * fa), BF16),
        [vmem()] * 3,
        vmem(),
        scratch=[pltpu.VMEM((RANK, features), BF16)],
        flops=2 * RANK * BLOCK * (width + features),
        nbytes=2 * BLOCK * (width + features),
    )(query_output_gradient, tokens, got_up)
    down_parts = exchange(down_parts)

    up_parts = call(
        down_kernel,
        jax.ShapeDtypeStruct((n, RANK, fb), BF16),
        [vmem()] * 3,
        vmem(),
        scratch=[pltpu.VMEM((RANK, width), BF16)],
        flops=2 * RANK * BLOCK * (width + features),
        nbytes=2 * BLOCK * (width + features),
    )(tokens, query_output_gradient, got_down)
    up_parts = exchange(up_parts)

    tail = got_down[:, :, got_down.shape[2] - LANES :]
    h_cols = tail[:, : pieces * local_rows].reshape(n, pieces, local_rows, LANES).transpose(0, 2, 1, 3)
    h_cols = h_cols.reshape(rows, pieces * LANES)[:, :fa]
    tenants = tail[:, pieces * local_rows : (pieces + 1) * local_rows].astype(jnp.int32).reshape(rows, LANES)
    low_rank = call(
        share_kernel,
        jax.ShapeDtypeStruct((n, rows // PER_TILE, LANES), F32),
        [smem(), vmem(), vmem(), vmem(), vmem()],
        vmem(),
        scratch=[pltpu.VMEM((fa, cols), F32)],
        flops=2 * rows * fa * cols,
        nbytes=2 * cols * fa,
    )(tenant_of_block, down_parts, down_factors, h_cols, tenants)
    low_rank = exchange(low_rank)

    up_gradient, new_up = call(
        up_kernel,
        [jax.ShapeDtypeStruct((fb, cols), F32), jax.ShapeDtypeStruct((fb, cols), BF16)],
        [smem(), vmem(), vmem()],
        [vmem()] * 2,
        flops=2 * n * RANK * fb * LANES,
        nbytes=8 * cols * fb,
    )(tenant_of_block, up_parts, up_factors_transposed)
    delta = call(
        delta_kernel,
        jax.ShapeDtypeStruct((n, local_rows, fb), F32),
        [vmem()] * 3,
        vmem(),
        flops=2 * rows * cols * fb,
        nbytes=2 * cols * fb,
    )(low_rank, tenants, new_up)
    delta = exchange(delta)

    down_gradient = call(
        sum_by_tenant,
        jax.ShapeDtypeStruct((fa, cols), F32),
        [smem(), vmem()],
        vmem(),
        flops=2 * n * RANK * fa * LANES,
        nbytes=4 * cols * fa,
    )(tenant_of_block, down_parts)
    attended = call(
        attention_kernel,
        jax.ShapeDtypeStruct((local_rows, HEADS * HEAD_DIM), BF16),
        [smem(), vmem(), vmem(), vmem(), vmem()],
        vmem(),
        flops=4 * HEADS * local_rows * cached_key_rows.shape[1] * HEAD_DIM,
        nbytes=4 * cached_key_rows.size,
    )(live_cache_length, delta, base_query_rows.astype(F32), cached_key_rows, cached_value_rows)
    return down_gradient, up_gradient, attended


def solution(mesh):
    placed = (
        P(("groups", "wide"), None),
        P(("groups", "wide"), None),
        P("wide", "groups"),
        P("wide", "groups"),
        P("groups"),
        P(("groups", "wide"), None),
        P(("groups", "wide")),
        P(("groups", "wide"), None),
        P(("groups", "wide"), None),
        P(("groups", "wide"), None, None),
        P(("groups", "wide"), None, None),
        P(("groups", "wide")),
    )
    return jax.shard_map(
        per_device,
        mesh=mesh,
        in_specs=placed,
        out_specs=(P("wide", "groups"), P("wide", "groups"), P(("groups", "wide"), None)),
        check_vma=False,
    )
```

```python
import functools

import jax
import jax.numpy as jnp
from jax import lax
from jax.experimental import pallas as pl
from jax.experimental.pallas import tpu as pltpu
from jax.sharding import PartitionSpec as P

HEAD_DIM = 128
HEADS = 32
KV_HEADS = 4
RANK = 32
TENANTS = 64
BLOCK = 128
ROWS_DEV = 4
LANES = 128
PER_TILE = LANES // RANK

adapter_scale = 2.0
learning_rate = 0.0002

F32 = jnp.float32
BF16 = jnp.bfloat16
VMEM_LIMIT = 40 * 1024 * 1024
ALL_VMEM = 60 * 1024 * 1024


def vmem():
    return pl.BlockSpec(memory_space=pltpu.VMEM)


def smem():
    return pl.BlockSpec(memory_space=pltpu.SMEM)


def hbm():
    return pl.BlockSpec(memory_space=pltpu.HBM)


def call(kernel, out_shape, in_specs, out_specs, scratch=(), flops=0, nbytes=0, limit=VMEM_LIMIT):
    return pl.pallas_call(
        kernel,
        out_shape=out_shape,
        in_specs=in_specs,
        out_specs=out_specs,
        scratch_shapes=list(scratch),
        compiler_params=pltpu.CompilerParams(vmem_limit_bytes=limit),
        cost_estimate=pl.CostEstimate(flops=flops, bytes_accessed=nbytes, transcendentals=0),
    )


def each(count, body):
    if count <= 16:
        for j in range(count):
            body(j)
    else:
        pl.loop(0, count)(body)


def dot(a, b, ca, cb):
    return lax.dot_general(a, b, (((ca,), (cb,)), ((), ())), preferred_element_type=F32)


def quarter_indicator(quarter, value):
    lane = lax.broadcasted_iota(jnp.int32, (RANK, LANES), 1)
    row = lax.broadcasted_iota(jnp.int32, (RANK, LANES), 0)
    return jnp.where(lane - row == quarter * RANK, value, 0.0).astype(BF16)


def tile_of(tenant):
    return pl.ds(pl.multiple_of((tenant // PER_TILE) * LANES, LANES), LANES)


HALF = RANK // 2


def up_half(h, fa, fb):
    return slice(h * fb, (h + 1) * fb)


def down_half(h, fa, fb):
    return slice(2 * fb + h * fa, 2 * fb + (h + 1) * fa)


def pick_kernel(t_ref, b_ref, a_ref, o_ref, b_tab, a_tab, o_buf, sem_b, sem_a, sem_o):
    n = t_ref.shape[0]
    fa, fb = a_ref.shape[0], b_ref.shape[0]

    def loads(src, dst, sem):
        step = src.shape[0] // sem.shape[0]
        parts = [slice(c * step, (c + 1) * step) for c in range(sem.shape[0])]
        return [pltpu.make_async_copy(src.at[r], dst.at[r], sem.at[c]) for c, r in enumerate(parts)]

    first, second = loads(b_ref, b_tab, sem_b), loads(a_ref, a_tab, sem_a)
    for load in first + second:
        load.start()

    def picked(j, table):
        t = t_ref[j]
        return dot(quarter_indicator(t % PER_TILE, 1.0), table[:, tile_of(t)], 1, 1).astype(BF16)

    def up_body(j):
        up = picked(j, b_tab)
        for h in range(2):
            o_buf[j, :, up_half(h, fa, fb)] = up[h * HALF : (h + 1) * HALF]

    def down_body(j):
        down = picked(j, a_tab)
        for h in range(2):
            o_buf[j, :, down_half(h, fa, fb)] = down[h * HALF : (h + 1) * HALF]
        pltpu.make_async_copy(o_buf.at[j], o_ref.at[j], sem_o.at[j]).start()

    def finish(j):
        pltpu.make_async_copy(o_buf.at[j], o_ref.at[j], sem_o.at[j]).wait()

    for load in first:
        load.wait()
    each(n, up_body)
    for load in second:
        load.wait()
    each(n, down_body)
    each(n, finish)


def block_kernel(x_ref, g_ref, extra_ref, r_ref, o_ref, wa_ref, wb_ref):
    n = r_ref.shape[0]
    fa, fb = x_ref.shape[1] // n, g_ref.shape[1] // n
    for d in range(n):
        for h in range(2):
            rank = slice(h * HALF, (h + 1) * HALF)
            wb_ref[rank, d * fb : (d + 1) * fb] = r_ref[d, :, up_half(h, fa, fb)]
            wa_ref[rank, d * fa : (d + 1) * fa] = r_ref[d, :, down_half(h, fa, fb)]
    down = dot(wa_ref[...], x_ref[...], 1, 1).astype(BF16)
    back = dot(wb_ref[...], g_ref[...], 1, 1).astype(BF16)
    up_part = dot(down, g_ref[...], 1, 0).astype(BF16)
    down_part = dot(back, x_ref[...], 1, 0).astype(BF16)
    for d in range(n):
        for h in range(2):
            rank = slice(h * HALF, (h + 1) * HALF)
            o_ref[d, :, up_half(h, fa, fb)] = up_part[rank, d * fb : (d + 1) * fb]
            o_ref[d, :, down_half(h, fa, fb)] = down_part[rank, d * fa : (d + 1) * fa]
        o_ref[d, :, o_ref.shape[2] - LANES :] = extra_ref[d]


def sum_by_tenant(t_ref, part_ref, cut, fa, fb, grad_ref):
    grad_ref[...] = jnp.zeros_like(grad_ref)

    def body(j):
        t = t_ref[j]
        part = jnp.concatenate([part_ref[j, :, cut(h, fa, fb)] for h in range(2)], axis=0)
        place = quarter_indicator(t % PER_TILE, adapter_scale)
        grad_ref[:, tile_of(t)] += dot(part, place, 0, 0)

    each(t_ref.shape[0], body)


def updated(table_ref, grad_ref):
    return (table_ref[...].astype(F32) - learning_rate * grad_ref[...]).astype(BF16)


def fold_rows(product, tenant):
    rows = product.shape[0]
    lane = lax.broadcasted_iota(jnp.int32, (rows, LANES), 1)
    total = jnp.zeros((rows, LANES), F32)
    for c in range(TENANTS // PER_TILE):
        mine = tenant == c * PER_TILE + lane // RANK
        total = total + jnp.where(mine, product[:, c * LANES : (c + 1) * LANES], 0.0)
    half = total + pltpu.roll(total, 2 * RANK, 1)
    return half + pltpu.roll(half, RANK, 1)


def share_kernel(fb, t_ref, part_ref, a_ref, o_ref, u_ref, grad_ref):
    n, fa = part_ref.shape[0], a_ref.shape[0]
    pieces = -(-fa // LANES)
    sum_by_tenant(t_ref, part_ref, down_half, fa, fb, grad_ref)
    ride = [part_ref[d, :, part_ref.shape[2] - LANES :].astype(F32) for d in range(n)]

    def gathered(p):
        return jnp.concatenate([e[p * ROWS_DEV : (p + 1) * ROWS_DEV] for e in ride], axis=0)

    h_cols = jnp.concatenate([gathered(p) for p in range(pieces)], axis=1)[:, :fa].astype(BF16)
    tenant = gathered(pieces).astype(jnp.int32)
    u_ref[...] = tenant
    full = fold_rows(dot(h_cols, updated(a_ref, grad_ref), 1, 0), tenant)
    quarter = full.shape[0] // PER_TILE
    spot = lax.broadcasted_iota(jnp.int32, (quarter, LANES), 1) // RANK
    packed = jnp.zeros((quarter, LANES), F32)
    for q in range(PER_TILE):
        packed = packed + jnp.where(spot == q, full[q * quarter : (q + 1) * quarter], 0.0)
    o_ref[...] = packed


def up_kernel(fa, t_ref, part_ref, b_ref, grad_ref, new_ref):
    sum_by_tenant(t_ref, part_ref, up_half, fa, b_ref.shape[0], grad_ref)
    new_ref[...] = updated(b_ref, grad_ref)


def down_kernel(fb, t_ref, part_ref, grad_ref):
    sum_by_tenant(t_ref, part_ref, down_half, grad_ref.shape[0], fb, grad_ref)


def delta_kernel(shares, me_ref, u_ref, new_ref, *refs):
    p_refs, o_refs, term = refs[:shares], refs[shares:-1], refs[-1]
    total = p_refs[0][...]
    for p_ref in p_refs[1:]:
        total = total + p_ref[...]
    spot = lax.broadcasted_iota(jnp.int32, total.shape, 1) // RANK
    pieces = []
    for q in range(PER_TILE):
        one = jnp.where(spot == q, total, 0.0)
        half = one + pltpu.roll(one, 2 * RANK, 1)
        pieces.append(half + pltpu.roll(half, RANK, 1))
    adapted = jnp.concatenate(pieces, axis=0)
    lane = lax.broadcasted_iota(jnp.int32, adapted.shape, 1)
    tenant = u_ref[...]
    spread = jnp.concatenate(
        [
            jnp.where(tenant == c * PER_TILE + lane // RANK, adapted, 0.0).astype(BF16)
            for c in range(TENANTS // PER_TILE)
        ],
        axis=1,
    )
    delta = adapter_scale * dot(spread, new_ref[...], 1, 1)
    dest = o_refs[0] if len(o_refs) == 1 else term
    for d in range(dest.shape[0]):
        dest[d] = delta[d * ROWS_DEV : (d + 1) * ROWS_DEV]
    if len(o_refs) > 1:
        for s, o_ref in enumerate(o_refs):
            o_ref[...] = term[me_ref[0] ^ s]


def attention_kernel(len_ref, me_ref, base_ref, k_ref, v_ref, *refs):
    delta_refs, o_ref, term = refs[:-2], refs[-2], refs[-1]
    n = term.shape[0]
    if len(delta_refs) == 1:
        term[...] = delta_refs[0][...]
    else:
        for s in range(n):
            term[me_ref[0] ^ s] = delta_refs[s][...]
    delta = jnp.concatenate([term[d] for d in range(n)], axis=1)
    query = (base_ref[...] + delta).astype(BF16).astype(F32)
    group = HEADS // KV_HEADS
    cache = k_ref.shape[1]
    many = group * ROWS_DEV
    row_p = lax.broadcasted_iota(jnp.int32, (many, cache), 0) % ROWS_DEV
    row_d = lax.broadcasted_iota(jnp.int32, (many, HEAD_DIM), 0) % ROWS_DEV
    position = lax.broadcasted_iota(jnp.int32, (many, cache), 1)
    length = jnp.zeros((many, cache), jnp.int32)
    for r in range(ROWS_DEV):
        length = jnp.where(row_p == r, len_ref[r], length)
    live = position < length
    outs = []
    for g in range(KV_HEADS):
        cols = slice(g * HEAD_DIM, (g + 1) * HEAD_DIM)
        heads = jnp.concatenate(
            [query[:, (g * group + i) * HEAD_DIM : (g * group + i + 1) * HEAD_DIM] for i in range(group)],
            axis=0,
        ).astype(BF16)
        scores = jnp.zeros((many, cache), F32)
        for r in range(ROWS_DEV):
            scores = jnp.where(row_p == r, dot(heads, k_ref[r, :, cols], 1, 1), scores)
        scores = scores / jnp.sqrt(F32(HEAD_DIM))
        scores = jnp.where(live, scores, F32(-1e30))
        top = jnp.max(scores, axis=-1, keepdims=True)
        expo = jnp.where(live, jnp.exp(scores - top), 0.0)
        weights = (expo / jnp.sum(expo, axis=-1, keepdims=True)).astype(BF16)
        mixed = jnp.zeros((many, HEAD_DIM), F32)
        for r in range(ROWS_DEV):
            mixed = jnp.where(row_d == r, dot(weights, v_ref[r, :, cols], 1, 0), mixed)
        outs.extend(mixed[i * ROWS_DEV : (i + 1) * ROWS_DEV] for i in range(group))
    o_ref[...] = jnp.concatenate(outs, axis=1).astype(BF16)


def exchange(x):
    return lax.all_to_all(x, "wide", split_axis=0, concat_axis=0, tiled=True)


def partner(x, mask):
    return lax.ppermute(x, "wide", [(i, i ^ mask) for i in range(lax.axis_size("wide"))])


def per_device(
    tokens,
    query_output_gradient,
    down_factors,
    up_factors_transposed,
    tenant_of_block,
    device_tenant_list,
    row_list_entry,
    hidden,
    base_query_rows,
    cached_key_rows,
    cached_value_rows,
    live_cache_length,
):
    n = lax.axis_size("wide")
    me = lax.axis_index("wide").astype(jnp.int32)[None]
    direct = n == 16
    fa, cols = down_factors.shape
    fb = up_factors_transposed.shape[0]
    local_rows = hidden.shape[0]
    rows = local_rows * n
    width = tokens.shape[1]
    features = query_output_gradient.shape[1]
    pieces = -(-fa // LANES)
    assert tokens.shape[0] == BLOCK and tenant_of_block.shape[0] == n and local_rows * (pieces + 1) <= HALF

    shape = (n, HALF, 2 * (fa + fb))
    chunks = 4 if fa % 64 == 0 and fb % 64 == 0 else 1
    packed = call(
        pick_kernel,
        jax.ShapeDtypeStruct(shape, BF16),
        [smem(), hbm(), hbm()],
        hbm(),
        scratch=[
            pltpu.VMEM(up_factors_transposed.shape, BF16),
            pltpu.VMEM(down_factors.shape, BF16),
            pltpu.VMEM(shape, BF16),
            pltpu.SemaphoreType.DMA((chunks,)),
            pltpu.SemaphoreType.DMA((chunks,)),
            pltpu.SemaphoreType.DMA((n,)),
        ],
        flops=2 * RANK * LANES * n * (fa + fb),
        nbytes=2 * cols * (fa + fb),
        limit=ALL_VMEM,
    )(tenant_of_block, up_factors_transposed, down_factors)
    got = exchange(packed)

    slot = row_list_entry[:, None] == jnp.arange(device_tenant_list.shape[1], dtype=jnp.int32)[None, :]
    row_tenant = jnp.sum(jnp.where(slot, device_tenant_list, 0), axis=1)
    slices = jnp.pad(hidden.reshape(local_rows, n, fa), ((0, 0), (0, 0), (0, pieces * LANES - fa)))
    slices = slices.reshape(local_rows, n, pieces, LANES).transpose(1, 2, 0, 3).reshape(n, pieces * local_rows, LANES)
    marks = jnp.broadcast_to(row_tenant.astype(BF16)[None, :, None], (n, local_rows, LANES))
    extra = jnp.concatenate([slices, marks], axis=1)
    extra = jnp.pad(extra, ((0, 0), (0, HALF - extra.shape[1]), (0, 0)))

    parts = call(
        block_kernel,
        jax.ShapeDtypeStruct((n, HALF, -(-2 * (fa + fb) // LANES) * LANES + LANES), BF16),
        [vmem()] * 4,
        vmem(),
        scratch=[pltpu.VMEM((RANK, width), BF16), pltpu.VMEM((RANK, features), BF16)],
        flops=4 * RANK * BLOCK * n * (fa + fb),
        nbytes=2 * BLOCK * n * (fa + fb),
    )(tokens, query_output_gradient, extra, got)
    parts = exchange(parts)

    low_rank, tenants = call(
        functools.partial(share_kernel, fb),
        [
            jax.ShapeDtypeStruct((rows // PER_TILE, LANES), F32),
            jax.ShapeDtypeStruct((rows, LANES), jnp.int32),
        ],
        [smem(), vmem(), vmem()],
        [vmem()] * 2,
        scratch=[pltpu.VMEM((fa, cols), F32)],
        flops=2 * rows * fa * cols,
        nbytes=2 * cols * fa,
    )(tenant_of_block, parts, down_factors)
    if direct:
        low_rank = low_rank + partner(low_rank, 1)
        low_rank = [low_rank] + [partner(low_rank, 2 * s) for s in range(1, n // 2)]
    else:
        low_rank = [lax.psum(low_rank, "wide")]

    up_gradient, new_up = call(
        functools.partial(up_kernel, fa),
        [jax.ShapeDtypeStruct((fb, cols), F32), jax.ShapeDtypeStruct((fb, cols), BF16)],
        [smem(), vmem(), vmem()],
        [vmem()] * 2,
        flops=2 * n * RANK * fb * LANES,
        nbytes=8 * cols * fb,
    )(tenant_of_block, parts, up_factors_transposed)
    if direct:
        shapes = [jax.ShapeDtypeStruct((local_rows, fb), F32)] * n
    else:
        shapes = [jax.ShapeDtypeStruct((n, local_rows, fb), F32)]
    delta = call(
        functools.partial(delta_kernel, len(low_rank)),
        shapes,
        [smem()] + [vmem()] * (2 + len(low_rank)),
        [vmem()] * len(shapes),
        scratch=[pltpu.VMEM((n, local_rows, fb), F32)],
        flops=2 * rows * cols * fb,
        nbytes=2 * cols * fb,
    )(me, tenants, new_up, *low_rank)
    if direct:
        delta = [partner(d, s) if s else d for s, d in enumerate(delta)]
    else:
        delta = [exchange(delta[0])]

    down_gradient = call(
        functools.partial(down_kernel, fb),
        jax.ShapeDtypeStruct((fa, cols), F32),
        [smem(), vmem()],
        vmem(),
        flops=2 * n * RANK * fa * LANES,
        nbytes=4 * cols * fa,
    )(tenant_of_block, parts)
    attended = call(
        attention_kernel,
        jax.ShapeDtypeStruct((local_rows, HEADS * HEAD_DIM), BF16),
        [smem(), smem()] + [vmem()] * (3 + len(delta)),
        vmem(),
        scratch=[pltpu.VMEM((n, local_rows, fb), F32)],
        flops=4 * HEADS * local_rows * cached_key_rows.shape[1] * HEAD_DIM,
        nbytes=4 * cached_key_rows.size,
    )(live_cache_length, me, base_query_rows.astype(F32), cached_key_rows, cached_value_rows, *delta)
    return down_gradient, up_gradient, attended


def solution(mesh):
    placed = (
        P(("groups", "wide"), None),
        P(("groups", "wide"), None),
        P("wide", "groups"),
        P("wide", "groups"),
        P("groups"),
        P(("groups", "wide"), None),
        P(("groups", "wide")),
        P(("groups", "wide"), None),
        P(("groups", "wide"), None),
        P(("groups", "wide"), None, None),
        P(("groups", "wide"), None, None),
        P(("groups", "wide")),
    )
    return jax.shard_map(
        per_device,
        mesh=mesh,
        in_specs=placed,
        out_specs=(P("wide", "groups"), P("wide", "groups"), P(("groups", "wide"), None)),
        check_vma=False,
    )
```

```python
import functools

import jax
import jax.numpy as jnp
from jax import lax
from jax.experimental import pallas as pl
from jax.experimental.pallas import tpu as pltpu
from jax.sharding import PartitionSpec as P

HEAD_DIM = 128
HEADS = 32
KV_HEADS = 4
RANK = 32
TENANTS = 64
BLOCK = 128
ROWS_DEV = 4
LANES = 128
PER_TILE = LANES // RANK

adapter_scale = 2.0
learning_rate = 0.0002

F32 = jnp.float32
BF16 = jnp.bfloat16
VMEM_LIMIT = 40 * 1024 * 1024
ALL_VMEM = 60 * 1024 * 1024


def vmem():
    return pl.BlockSpec(memory_space=pltpu.VMEM)


def smem():
    return pl.BlockSpec(memory_space=pltpu.SMEM)


def hbm():
    return pl.BlockSpec(memory_space=pltpu.HBM)


def call(kernel, out_shape, in_specs, out_specs, scratch=(), flops=0, nbytes=0, limit=VMEM_LIMIT):
    return pl.pallas_call(
        kernel,
        out_shape=out_shape,
        in_specs=in_specs,
        out_specs=out_specs,
        scratch_shapes=list(scratch),
        compiler_params=pltpu.CompilerParams(vmem_limit_bytes=limit),
        cost_estimate=pl.CostEstimate(flops=flops, bytes_accessed=nbytes, transcendentals=0),
    )


def each(count, body):
    if count <= 16:
        for j in range(count):
            body(j)
    else:
        pl.loop(0, count)(body)


def dot(a, b, ca, cb):
    return lax.dot_general(a, b, (((ca,), (cb,)), ((), ())), preferred_element_type=F32)


def quarter_indicator(quarter, value):
    lane = lax.broadcasted_iota(jnp.int32, (RANK, LANES), 1)
    row = lax.broadcasted_iota(jnp.int32, (RANK, LANES), 0)
    return jnp.where(lane - row == quarter * RANK, value, 0.0).astype(BF16)


def tile_of(tenant):
    return pl.ds(pl.multiple_of((tenant // PER_TILE) * LANES, LANES), LANES)


HALF = RANK // 2
CHUNKS = HALF // ROWS_DEV


def up_half(h, fa, fb):
    return slice(h * fb, (h + 1) * fb)


def down_half(h, fa, fb):
    return slice(2 * fb + h * fa, 2 * fb + (h + 1) * fa)


def pick_kernel(t_ref, b_ref, a_ref, o_ref, b_tab, a_tab, o_buf, sem_b, sem_a, sem_o):
    n = t_ref.shape[0]
    fa, fb = a_ref.shape[0], b_ref.shape[0]

    def loads(src, dst, sem):
        step = src.shape[0] // sem.shape[0]
        parts = [slice(c * step, (c + 1) * step) for c in range(sem.shape[0])]
        return [pltpu.make_async_copy(src.at[r], dst.at[r], sem.at[c]) for c, r in enumerate(parts)]

    first, second = loads(b_ref, b_tab, sem_b), loads(a_ref, a_tab, sem_a)
    for load in first + second:
        load.start()

    def picked(j, table):
        t = t_ref[j]
        return dot(quarter_indicator(t % PER_TILE, 1.0), table[:, tile_of(t)], 1, 1).astype(BF16)

    def up_body(j):
        up = picked(j, b_tab)
        for h in range(2):
            o_buf[j, :, up_half(h, fa, fb)] = up[h * HALF : (h + 1) * HALF]

    def down_body(j):
        down = picked(j, a_tab)
        for h in range(2):
            o_buf[j, :, down_half(h, fa, fb)] = down[h * HALF : (h + 1) * HALF]
        pltpu.make_async_copy(o_buf.at[j], o_ref.at[j], sem_o.at[j]).start()

    def finish(j):
        pltpu.make_async_copy(o_buf.at[j], o_ref.at[j], sem_o.at[j]).wait()

    for load in first:
        load.wait()
    each(n, up_body)
    for load in second:
        load.wait()
    each(n, down_body)
    each(n, finish)


def rows_pack_kernel(list_ref, slot_ref, hidden_ref, o_ref):
    hidden = hidden_ref[...].astype(F32)
    size = hidden.shape[1] // CHUNKS
    main = jnp.concatenate([hidden[:, p * size : (p + 1) * size] for p in range(CHUNKS)], axis=0)
    row = lax.broadcasted_iota(jnp.int32, (HALF, LANES), 0) % ROWS_DEV
    mark = jnp.zeros((HALF, LANES), jnp.int32)
    for r in range(ROWS_DEV):
        mark = jnp.where(row == r, list_ref[0, slot_ref[r]], mark)
    o_ref[...] = jnp.concatenate([main, mark.astype(F32)], axis=1).astype(BF16)


def fold_rows(product, tenant):
    rows = product.shape[0]
    lane = lax.broadcasted_iota(jnp.int32, (rows, LANES), 1)
    total = jnp.zeros((rows, LANES), F32)
    for c in range(TENANTS // PER_TILE):
        mine = tenant == c * PER_TILE + lane // RANK
        total = total + jnp.where(mine, product[:, c * LANES : (c + 1) * LANES], 0.0)
    half = total + pltpu.roll(total, 2 * RANK, 1)
    return half + pltpu.roll(half, RANK, 1)


def rows_kernel(masks, me_ref, h0_ref, h1_ref, x_ref, a_ref, hx_ref, base_ref, u_ref, sel, sx, sb, su):
    tiles = len(masks)
    h = jnp.concatenate([r[k] for r in (h0_ref, h1_ref) for k in range(tiles // 2)], axis=0)
    size = h.shape[1] - LANES
    fa = a_ref.shape[0]
    part = lax.broadcasted_iota(jnp.int32, (h.shape[0], LANES), 0) % HALF // ROWS_DEV
    hx = jnp.zeros((h.shape[0], LANES), F32)
    for p in range(CHUNKS):
        hx = jnp.where(part == p, dot(h[:, :size], x_ref[:, p * size : (p + 1) * size], 1, 1), hx)
    per_chunk = size // fa
    for m in range(per_chunk):

        @pl.when(me_ref[0] % per_chunk == m)
        def _():
            sel[...] = h[:, m * fa : (m + 1) * fa]

    tenant = h[:, size:].astype(F32).astype(jnp.int32)
    base = fold_rows(dot(sel[...], a_ref[...], 1, 0), tenant)
    base = jnp.where(part == me_ref[0] // per_chunk, base, 0.0)
    for k, mask in enumerate(masks):
        d = me_ref[0] ^ mask
        for value, dest in ((hx, sx), (base, sb)):
            eight = value[k * HALF : k * HALF + 8] + value[k * HALF + 8 : (k + 1) * HALF]
            dest[d] = eight[:ROWS_DEV] + eight[ROWS_DEV:]
        su[d] = tenant[k * HALF : k * HALF + ROWS_DEV]
    for src, dest in ((sx, hx_ref), (sb, base_ref), (su, u_ref)):
        dest[...] = jnp.concatenate([src[d] for d in range(tiles)], axis=0)


def plain_rows_kernel(h_ref, x_ref, a_ref, hc_ref, u_ref, hx_ref, base_ref):
    hx_ref[...] = dot(h_ref[...], x_ref[...], 1, 1)
    base_ref[...] = fold_rows(dot(hc_ref[...], a_ref[...], 1, 0), u_ref[...])


def block_kernel(ride, t_ref, x_ref, g_ref, hx_ref, base_ref, u_ref, r_ref, o_ref, *refs):
    wa_ref, wb_ref = refs[-2:]
    n = r_ref.shape[0]
    fa, fb = x_ref.shape[1] // n, g_ref.shape[1] // n
    for d in range(n):
        for h in range(2):
            rank = slice(h * HALF, (h + 1) * HALF)
            wb_ref[rank, d * fb : (d + 1) * fb] = r_ref[d, :, up_half(h, fa, fb)]
            wa_ref[rank, d * fa : (d + 1) * fa] = r_ref[d, :, down_half(h, fa, fb)]
    back = dot(wb_ref[...], g_ref[...], 1, 1).astype(BF16)
    down = dot(wa_ref[...], x_ref[...], 1, 1).astype(BF16)

    hx = hx_ref[...]
    high = hx.astype(BF16)
    low = (hx - high.astype(F32)).astype(BF16)
    wide_back = jnp.concatenate([back] * PER_TILE, axis=0)
    change = dot(high, wide_back, 1, 1) + dot(low, wide_back, 1, 1)
    mine = u_ref[...] == t_ref[0]
    full = base_ref[...] - jnp.where(mine, learning_rate * (adapter_scale * change), 0.0)
    quarter = full.shape[0] // PER_TILE
    spot = lax.broadcasted_iota(jnp.int32, (quarter, LANES), 1) // RANK
    packed = jnp.zeros((quarter, LANES), F32)
    for q in range(PER_TILE):
        packed = packed + jnp.where(spot == q, full[q * quarter : (q + 1) * quarter], 0.0)
    if not ride:
        refs[0][...] = packed

    down_part = dot(back, x_ref[...], 1, 0).astype(BF16)
    up_part = dot(down, g_ref[...], 1, 0).astype(BF16)
    for d in range(n):
        for h in range(2):
            rank = slice(h * HALF, (h + 1) * HALF)
            o_ref[d, :, up_half(h, fa, fb)] = up_part[rank, d * fb : (d + 1) * fb]
            o_ref[d, :, down_half(h, fa, fb)] = down_part[rank, d * fa : (d + 1) * fa]
        if ride:
            o_ref[d, :, 2 * (fa + fb) :] = packed.astype(BF16)


def sum_by_tenant(t_ref, part_ref, cut, fa, fb, grad_ref):
    grad_ref[...] = jnp.zeros_like(grad_ref)

    def body(j):
        t = t_ref[j]
        part = jnp.concatenate([part_ref[j, :, cut(h, fa, fb)] for h in range(2)], axis=0)
        place = quarter_indicator(t % PER_TILE, adapter_scale)
        grad_ref[:, tile_of(t)] += dot(part, place, 0, 0)

    each(t_ref.shape[0], body)


def updated(table_ref, grad_ref):
    return (table_ref[...].astype(F32) - learning_rate * grad_ref[...]).astype(BF16)


def gradient_kernel(t_ref, part_ref, down_ref, up_ref):
    fa, fb = down_ref.shape[0], up_ref.shape[0]
    sum_by_tenant(t_ref, part_ref, down_half, fa, fb, down_ref)
    sum_by_tenant(t_ref, part_ref, up_half, fa, fb, up_ref)


def delta_kernel(fa, t_ref, part_ref, b_ref, u_ref, *refs):
    o_ref, grad_ref = refs[-2:]
    n, fb = part_ref.shape[0], b_ref.shape[0]
    if len(refs) == 3:
        total = refs[0][...]
    else:
        total = part_ref[0, :, 2 * (fa + fb) :].astype(F32)
        for d in range(1, n):
            total = total + part_ref[d, :, 2 * (fa + fb) :].astype(F32)
    spot = lax.broadcasted_iota(jnp.int32, total.shape, 1) // RANK
    pieces = []
    for q in range(PER_TILE):
        one = jnp.where(spot == q, total, 0.0)
        half = one + pltpu.roll(one, 2 * RANK, 1)
        pieces.append(half + pltpu.roll(half, RANK, 1))
    adapted = jnp.concatenate(pieces, axis=0)
    lane = lax.broadcasted_iota(jnp.int32, adapted.shape, 1)
    tenant = u_ref[...]
    spread = jnp.concatenate(
        [
            jnp.where(tenant == c * PER_TILE + lane // RANK, adapted, 0.0).astype(BF16)
            for c in range(TENANTS // PER_TILE)
        ],
        axis=1,
    )
    sum_by_tenant(t_ref, part_ref, up_half, fa, fb, grad_ref)
    delta = adapter_scale * dot(spread, updated(b_ref, grad_ref), 1, 1)
    for d in range(n):
        o_ref[d] = delta[d * ROWS_DEV : (d + 1) * ROWS_DEV]


def attention_kernel(len_ref, delta_ref, base_ref, k_ref, v_ref, o_ref):
    n = delta_ref.shape[0]
    delta = jnp.concatenate([delta_ref[d] for d in range(n)], axis=1)
    query = (base_ref[...] + delta).astype(BF16).astype(F32)
    group = HEADS // KV_HEADS
    cache = k_ref.shape[1]
    many = group * ROWS_DEV
    row_p = lax.broadcasted_iota(jnp.int32, (many, cache), 0) % ROWS_DEV
    row_d = lax.broadcasted_iota(jnp.int32, (many, HEAD_DIM), 0) % ROWS_DEV
    position = lax.broadcasted_iota(jnp.int32, (many, cache), 1)
    length = jnp.zeros((many, cache), jnp.int32)
    for r in range(ROWS_DEV):
        length = jnp.where(row_p == r, len_ref[r], length)
    live = position < length
    outs = []
    for g in range(KV_HEADS):
        cols = slice(g * HEAD_DIM, (g + 1) * HEAD_DIM)
        heads = jnp.concatenate(
            [query[:, (g * group + i) * HEAD_DIM : (g * group + i + 1) * HEAD_DIM] for i in range(group)],
            axis=0,
        ).astype(BF16)
        scores = jnp.zeros((many, cache), F32)
        for r in range(ROWS_DEV):
            scores = jnp.where(row_p == r, dot(heads, k_ref[r, :, cols], 1, 1), scores)
        scores = scores / jnp.sqrt(F32(HEAD_DIM))
        scores = jnp.where(live, scores, F32(-1e30))
        top = jnp.max(scores, axis=-1, keepdims=True)
        expo = jnp.where(live, jnp.exp(scores - top), 0.0)
        weights = (expo / jnp.sum(expo, axis=-1, keepdims=True)).astype(BF16)
        mixed = jnp.zeros((many, HEAD_DIM), F32)
        for r in range(ROWS_DEV):
            mixed = jnp.where(row_d == r, dot(weights, v_ref[r, :, cols], 1, 0), mixed)
        outs.extend(mixed[i * ROWS_DEV : (i + 1) * ROWS_DEV] for i in range(group))
    o_ref[...] = jnp.concatenate(outs, axis=1).astype(BF16)


def exchange(x):
    return lax.all_to_all(x, "wide", split_axis=0, concat_axis=0, tiled=True)


def partner(x, mask):
    return lax.ppermute(x, "wide", [(i, i ^ mask) for i in range(lax.axis_size("wide"))])


def per_device(
    tokens,
    query_output_gradient,
    down_factors,
    up_factors_transposed,
    tenant_of_block,
    device_tenant_list,
    row_list_entry,
    hidden,
    base_query_rows,
    cached_key_rows,
    cached_value_rows,
    live_cache_length,
):
    n = lax.axis_size("wide")
    me = lax.axis_index("wide").astype(jnp.int32)
    small = n == 16
    fa, cols = down_factors.shape
    fb = up_factors_transposed.shape[0]
    local_rows = hidden.shape[0]
    rows = local_rows * n
    quarter = rows // PER_TILE
    width = tokens.shape[1]
    features = query_output_gradient.shape[1]
    assert tokens.shape[0] == BLOCK and tenant_of_block.shape[0] == n

    shape = (n, HALF, 2 * (fa + fb))
    chunks = 4 if fa % 64 == 0 and fb % 64 == 0 else 1
    packed = call(
        pick_kernel,
        jax.ShapeDtypeStruct(shape, BF16),
        [smem(), hbm(), hbm()],
        hbm(),
        scratch=[
            pltpu.VMEM(up_factors_transposed.shape, BF16),
            pltpu.VMEM(down_factors.shape, BF16),
            pltpu.VMEM(shape, BF16),
            pltpu.SemaphoreType.DMA((chunks,)),
            pltpu.SemaphoreType.DMA((chunks,)),
            pltpu.SemaphoreType.DMA((n,)),
        ],
        flops=2 * RANK * LANES * n * (fa + fb),
        nbytes=2 * cols * (fa + fb),
        limit=ALL_VMEM,
    )(tenant_of_block, up_factors_transposed, down_factors)

    if small:
        held = call(
            rows_pack_kernel,
            jax.ShapeDtypeStruct((HALF, width // CHUNKS + LANES), BF16),
            [smem(), smem(), vmem()],
            vmem(),
            nbytes=4 * local_rows * width,
        )(device_tenant_list, row_list_entry, hidden)[None]
        held = jnp.concatenate([held, partner(held, n // 2)], axis=0)
        held, packed = lax.optimization_barrier((held, packed))
        got = exchange(packed)
        masks = [0, n // 2]
        bit = n // 4
        while bit > 1:
            held = jnp.concatenate([held, partner(held, bit)], axis=0)
            masks = masks + [m ^ bit for m in masks]
            bit //= 2
        masks = masks + [m ^ 1 for m in masks]
        shapes = [(rows, BLOCK, F32), (rows, LANES, F32), (rows, LANES, jnp.int32)]
        hx, base_low_rank, tenants = call(
            functools.partial(rows_kernel, masks),
            [jax.ShapeDtypeStruct((r, c), t) for r, c, t in shapes],
            [smem()] + [vmem()] * 4,
            [vmem()] * 3,
            scratch=[
                pltpu.VMEM((n * HALF, fa), BF16),
                pltpu.VMEM((n, local_rows, LANES), F32),
                pltpu.VMEM((n, local_rows, LANES), F32),
                pltpu.VMEM((n, local_rows, LANES), jnp.int32),
            ],
            flops=8 * rows * BLOCK * width + 8 * rows * fa * cols,
            nbytes=2 * BLOCK * width + 2 * fa * cols,
        )(me[None], held, partner(held, 1), tokens, down_factors)
    else:
        got = exchange(packed)
        slot = row_list_entry[:, None] == jnp.arange(device_tenant_list.shape[1], dtype=jnp.int32)[None, :]
        row_tenant = jnp.sum(jnp.where(slot, device_tenant_list, 0), axis=1)
        everyone = lax.all_gather(hidden, "wide", axis=0, tiled=True)
        tenants = lax.all_gather(row_tenant, "wide", axis=0, tiled=True)
        tenants = jnp.broadcast_to(tenants[:, None], (rows, LANES))
        hx, base_low_rank = call(
            plain_rows_kernel,
            [jax.ShapeDtypeStruct((rows, BLOCK), F32), jax.ShapeDtypeStruct((rows, LANES), F32)],
            [vmem()] * 5,
            [vmem()] * 2,
        )(everyone, tokens, down_factors, lax.dynamic_slice(everyone, (0, me * fa), (rows, fa)), tenants)

    part_shape = (n, HALF, 2 * (fa + fb) + (LANES if small else 0))
    my_tenant = lax.dynamic_slice(tenant_of_block, (me,), (1,))
    parts = call(
        functools.partial(block_kernel, small),
        [jax.ShapeDtypeStruct(part_shape, BF16)]
        + ([] if small else [jax.ShapeDtypeStruct((quarter, LANES), F32)]),
        [smem()] + [vmem()] * 6,
        [vmem()] * (1 if small else 2),
        scratch=[pltpu.VMEM((RANK, width), BF16), pltpu.VMEM((RANK, features), BF16)],
        flops=4 * RANK * BLOCK * n * (fa + fb),
        nbytes=2 * BLOCK * n * (fa + fb),
    )(my_tenant, tokens, query_output_gradient, hx, base_low_rank, tenants, got)
    low_rank = [lax.psum(p, "wide") for p in parts[1:]]
    parts = exchange(parts[0])

    delta = call(
        functools.partial(delta_kernel, fa),
        jax.ShapeDtypeStruct((n, local_rows, fb), F32),
        [smem()] + [vmem()] * (3 + len(low_rank)),
        vmem(),
        scratch=[pltpu.VMEM((fb, cols), F32)],
        flops=2 * rows * cols * fb,
        nbytes=2 * cols * fb,
    )(tenant_of_block, parts, up_factors_transposed, tenants, *low_rank)
    delta = exchange(delta)

    down_gradient, up_gradient = call(
        gradient_kernel,
        [jax.ShapeDtypeStruct((fa, cols), F32), jax.ShapeDtypeStruct((fb, cols), F32)],
        [smem(), vmem()],
        [vmem()] * 2,
        flops=2 * n * RANK * (fa + fb) * LANES,
        nbytes=4 * cols * (fa + fb),
    )(tenant_of_block, parts)
    attended = call(
        attention_kernel,
        jax.ShapeDtypeStruct((local_rows, HEADS * HEAD_DIM), BF16),
        [smem(), vmem(), vmem(), vmem(), vmem()],
        vmem(),
        flops=4 * HEADS * local_rows * cached_key_rows.shape[1] * HEAD_DIM,
        nbytes=4 * cached_key_rows.size,
    )(live_cache_length, delta, base_query_rows.astype(F32), cached_key_rows, cached_value_rows)
    return down_gradient, up_gradient, attended


def solution(mesh):
    placed = (
        P(("groups", "wide"), None),
        P(("groups", "wide"), None),
        P("wide", "groups"),
        P("wide", "groups"),
        P("groups"),
        P(("groups", "wide"), None),
        P(("groups", "wide")),
        P(("groups", "wide"), None),
        P(("groups", "wide"), None),
        P(("groups", "wide"), None, None),
        P(("groups", "wide"), None, None),
        P(("groups", "wide")),
    )
    return jax.shard_map(
        per_device,
        mesh=mesh,
        in_specs=placed,
        out_specs=(P("wide", "groups"), P("wide", "groups"), P(("groups", "wide"), None)),
        check_vma=False,
    )
```

```python
import functools

import jax
import jax.numpy as jnp
from jax import lax
from jax.experimental import pallas as pl
from jax.experimental.pallas import tpu as pltpu
from jax.sharding import PartitionSpec as P

HEAD_DIM = 128
HEADS = 32
KV_HEADS = 4
RANK = 32
TENANTS = 64
BLOCK = 128
ROWS_DEV = 4
LANES = 128
PER_TILE = LANES // RANK

adapter_scale = 2.0
learning_rate = 0.0002

F32 = jnp.float32
BF16 = jnp.bfloat16
VMEM_LIMIT = 24 * 1024 * 1024
ALL_VMEM = 60 * 1024 * 1024


def vmem():
    return pl.BlockSpec(memory_space=pltpu.VMEM)


def smem():
    return pl.BlockSpec(memory_space=pltpu.SMEM)


def hbm():
    return pl.BlockSpec(memory_space=pltpu.HBM)


def call(kernel, out_shape, in_specs, out_specs, scratch=(), flops=0, nbytes=0, limit=VMEM_LIMIT):
    return pl.pallas_call(
        kernel,
        out_shape=out_shape,
        in_specs=in_specs,
        out_specs=out_specs,
        scratch_shapes=list(scratch),
        compiler_params=pltpu.CompilerParams(vmem_limit_bytes=limit),
        cost_estimate=pl.CostEstimate(flops=flops, bytes_accessed=nbytes, transcendentals=0),
    )


def each(count, body):
    if count <= 16:
        for j in range(count):
            body(j)
    else:
        pl.loop(0, count)(body)


def dot(a, b, ca, cb):
    return lax.dot_general(a, b, (((ca,), (cb,)), ((), ())), preferred_element_type=F32)


def quarter_indicator(quarter, value):
    lane = lax.broadcasted_iota(jnp.int32, (RANK, LANES), 1)
    row = lax.broadcasted_iota(jnp.int32, (RANK, LANES), 0)
    return jnp.where(lane - row == quarter * RANK, value, 0.0).astype(BF16)


def tile_of(tenant):
    return pl.ds(pl.multiple_of((tenant // PER_TILE) * LANES, LANES), LANES)


HALF = RANK // 2
CHUNKS = HALF // ROWS_DEV


def up_half(h, fa, fb):
    return slice(h * fb, (h + 1) * fb)


def down_half(h, fa, fb):
    return slice(2 * fb + h * fa, 2 * fb + (h + 1) * fa)


def pick_kernel(tenant_ref, b_ref, a_ref, o_ref, b_tab, a_tab, o_buf, t_ref, sem_t, sem_b, sem_a, sem_o):
    n = t_ref.shape[0]
    fa, fb = a_ref.shape[0], b_ref.shape[0]

    def loads(src, dst, sem):
        step = src.shape[0] // sem.shape[0]
        parts = [slice(c * step, (c + 1) * step) for c in range(sem.shape[0])]
        return [pltpu.make_async_copy(src.at[r], dst.at[r], sem.at[c]) for c, r in enumerate(parts)]

    first, second = loads(b_ref, b_tab, sem_b), loads(a_ref, a_tab, sem_a)
    tenants = pltpu.make_async_copy(tenant_ref, t_ref, sem_t)
    for load in [tenants] + first + second:
        load.start()

    def picked(j, table):
        t = t_ref[j]
        return dot(quarter_indicator(t % PER_TILE, 1.0), table[:, tile_of(t)], 1, 1).astype(BF16)

    def up_body(j):
        up = picked(j, b_tab)
        for h in range(2):
            o_buf[j, :, up_half(h, fa, fb)] = up[h * HALF : (h + 1) * HALF]

    def down_body(j):
        down = picked(j, a_tab)
        for h in range(2):
            o_buf[j, :, down_half(h, fa, fb)] = down[h * HALF : (h + 1) * HALF]
        pltpu.make_async_copy(o_buf.at[j], o_ref.at[j], sem_o.at[j]).start()

    def finish(j):
        pltpu.make_async_copy(o_buf.at[j], o_ref.at[j], sem_o.at[j]).wait()

    for load in [tenants] + first:
        load.wait()
    each(n, up_body)
    for load in second:
        load.wait()
    each(n, down_body)
    each(n, finish)


def rows_pack_kernel(list_ref, slot_ref, hidden_ref, o_ref):
    hidden = hidden_ref[...].astype(F32)
    size = hidden.shape[1] // CHUNKS
    main = jnp.concatenate([hidden[:, p * size : (p + 1) * size] for p in range(CHUNKS)], axis=0)
    row = lax.broadcasted_iota(jnp.int32, (HALF, LANES), 0) % ROWS_DEV
    mark = jnp.zeros((HALF, LANES), jnp.int32)
    for r in range(ROWS_DEV):
        mark = jnp.where(row == r, list_ref[0, slot_ref[r]], mark)
    o_ref[...] = jnp.concatenate([main, mark.astype(F32)], axis=1).astype(BF16)


def fold_rows(product, tenant):
    rows = product.shape[0]
    lane = lax.broadcasted_iota(jnp.int32, (rows, LANES), 1)
    total = jnp.zeros((rows, LANES), F32)
    for c in range(TENANTS // PER_TILE):
        mine = tenant == c * PER_TILE + lane // RANK
        total = total + jnp.where(mine, product[:, c * LANES : (c + 1) * LANES], 0.0)
    half = total + pltpu.roll(total, 2 * RANK, 1)
    return half + pltpu.roll(half, RANK, 1)


def rows_kernel(count, me_ref, *refs):
    h_refs, (x_ref, a_ref, hx_ref, base_ref, u_ref, sel) = refs[:count], refs[count:]
    h = jnp.concatenate([r[k] for r in h_refs for k in range(r.shape[0])], axis=0)
    size = h.shape[1] - LANES
    fa = a_ref.shape[0]
    part = lax.broadcasted_iota(jnp.int32, (h.shape[0], LANES), 0) % HALF // ROWS_DEV
    hx = jnp.zeros((h.shape[0], LANES), F32)
    for p in range(CHUNKS):
        hx = jnp.where(part == p, dot(h[:, :size], x_ref[:, p * size : (p + 1) * size], 1, 1), hx)
    per_chunk = size // fa
    for m in range(per_chunk):

        @pl.when(me_ref[0] % per_chunk == m)
        def _():
            sel[...] = h[:, m * fa : (m + 1) * fa]

    tenant = h[:, size:].astype(F32).astype(jnp.int32)
    base = fold_rows(dot(sel[...], a_ref[...], 1, 0), tenant)
    base = jnp.where(part == me_ref[0] // per_chunk, base, 0.0)
    for k in range(h.shape[0] // HALF):
        for value, dest in ((hx, hx_ref), (base, base_ref)):
            eight = value[k * HALF : k * HALF + 8] + value[k * HALF + 8 : (k + 1) * HALF]
            dest[k] = eight[:ROWS_DEV] + eight[ROWS_DEV:]
        u_ref[k] = tenant[k * HALF : k * HALF + ROWS_DEV]


def plain_rows_kernel(h_ref, x_ref, a_ref, hc_ref, u_ref, hx_ref, base_ref):
    hx = dot(h_ref[...], x_ref[...], 1, 1)
    base = fold_rows(dot(hc_ref[...], a_ref[...], 1, 0), u_ref[...])
    for d in range(hx_ref.shape[0]):
        hx_ref[d] = hx[d * ROWS_DEV : (d + 1) * ROWS_DEV]
        base_ref[d] = base[d * ROWS_DEV : (d + 1) * ROWS_DEV]


def block_kernel(ride, masks, t_ref, me_ref, x_ref, g_ref, r_ref, *refs):
    sets = (len(refs) - (7 if ride else 8)) // 3
    hx_sets, base_sets, u_sets = (refs[i * sets : (i + 1) * sets] for i in range(3))
    o_ref, u_ref = refs[3 * sets : 3 * sets + 2]
    wa_ref, wb_ref, sx, sb, su = refs[-5:]
    n = r_ref.shape[0]
    fa, fb = x_ref.shape[1] // n, g_ref.shape[1] // n
    for d in range(n):
        for h in range(2):
            rank = slice(h * HALF, (h + 1) * HALF)
            wb_ref[rank, d * fb : (d + 1) * fb] = r_ref[d, :, up_half(h, fa, fb)]
            wa_ref[rank, d * fa : (d + 1) * fa] = r_ref[d, :, down_half(h, fa, fb)]
    back = dot(wb_ref[...], g_ref[...], 1, 1).astype(BF16)
    down = dot(wa_ref[...], x_ref[...], 1, 1).astype(BF16)

    k = 0
    for hx_ref, base_ref, tile_ref in zip(hx_sets, base_sets, u_sets):
        for i in range(hx_ref.shape[0]):
            d = me_ref[0] ^ masks[k] if masks else i
            sx[d], sb[d], su[d] = hx_ref[i], base_ref[i], tile_ref[i]
            k += 1
    hx, base, tenant = (jnp.concatenate([v[d] for d in range(n)], axis=0) for v in (sx, sb, su))
    u_ref[...] = tenant
    high = hx.astype(BF16)
    low = (hx - high.astype(F32)).astype(BF16)
    wide_back = jnp.concatenate([back] * PER_TILE, axis=0)
    change = dot(high, wide_back, 1, 1) + dot(low, wide_back, 1, 1)
    mine = tenant == t_ref[0]
    full = base - jnp.where(mine, learning_rate * (adapter_scale * change), 0.0)
    quarter = full.shape[0] // PER_TILE
    spot = lax.broadcasted_iota(jnp.int32, (quarter, LANES), 1) // RANK
    packed = jnp.zeros((quarter, LANES), F32)
    for q in range(PER_TILE):
        packed = packed + jnp.where(spot == q, full[q * quarter : (q + 1) * quarter], 0.0)
    if not ride:
        refs[3 * sets + 2][...] = packed

    down_part = dot(back, x_ref[...], 1, 0).astype(BF16)
    up_part = dot(down, g_ref[...], 1, 0).astype(BF16)
    for d in range(n):
        for h in range(2):
            rank = slice(h * HALF, (h + 1) * HALF)
            o_ref[d, :, up_half(h, fa, fb)] = up_part[rank, d * fb : (d + 1) * fb]
            o_ref[d, :, down_half(h, fa, fb)] = down_part[rank, d * fa : (d + 1) * fa]
        if ride:
            o_ref[d, :, 2 * (fa + fb) :] = packed.astype(BF16)


def sum_by_tenant(t_ref, part_ref, cut, fa, fb, grad_ref):
    grad_ref[...] = jnp.zeros_like(grad_ref)

    def body(j):
        t = t_ref[j]
        part = jnp.concatenate([part_ref[j, :, cut(h, fa, fb)] for h in range(2)], axis=0)
        place = quarter_indicator(t % PER_TILE, adapter_scale)
        grad_ref[:, tile_of(t)] += dot(part, place, 0, 0)

    each(t_ref.shape[0], body)


def gradient_kernel(t_ref, part_ref, down_ref, up_ref):
    fa, fb = down_ref.shape[0], up_ref.shape[0]
    sum_by_tenant(t_ref, part_ref, down_half, fa, fb, down_ref)
    sum_by_tenant(t_ref, part_ref, up_half, fa, fb, up_ref)


def mask_kernel(u_ref, o_ref):
    tenant = u_ref[...]
    lane = lax.broadcasted_iota(jnp.int32, tenant.shape, 1)
    for c in range(TENANTS // PER_TILE):
        mine = tenant == c * PER_TILE + lane // RANK
        o_ref[:, c * LANES : (c + 1) * LANES] = jnp.where(mine, 1.0, 0.0).astype(BF16)


def delta_kernel(fa, t_ref, part_ref, b_ref, u_ref, mask_ref, *refs):
    o_ref = refs[-1]
    n, fb = part_ref.shape[0], b_ref.shape[0]
    if len(refs) == 2:
        total = refs[0][...]
    else:
        total = part_ref[0, :, 2 * (fa + fb) :].astype(F32)
        for d in range(1, n):
            total = total + part_ref[d, :, 2 * (fa + fb) :].astype(F32)
    spot = lax.broadcasted_iota(jnp.int32, total.shape, 1) // RANK
    pieces = []
    for q in range(PER_TILE):
        one = jnp.where(spot == q, total, 0.0)
        half = one + pltpu.roll(one, 2 * RANK, 1)
        pieces.append(half + pltpu.roll(half, RANK, 1))
    adapted = jnp.concatenate(pieces, axis=0)
    rounded = adapted.astype(BF16)
    spread = jnp.concatenate([rounded] * (TENANTS // PER_TILE), axis=1) * mask_ref[...]
    old = dot(spread, b_ref[...], 1, 1)
    quarter = lax.broadcasted_iota(jnp.int32, adapted.shape, 1) // RANK
    tenant = u_ref[...]
    matched = []
    for c in range(n // PER_TILE):
        block = jnp.zeros(adapted.shape, jnp.int32)
        for i in range(PER_TILE):
            block = jnp.where(quarter == i, t_ref[c * PER_TILE + i], block)
        matched.append(jnp.where(tenant == block, adapted, 0.0).astype(BF16))
    up = [part_ref[j, :, up_half(h, fa, fb)] for j in range(n) for h in range(2)]
    change = dot(jnp.concatenate(matched, axis=1), jnp.concatenate(up, axis=0), 1, 0)
    delta = adapter_scale * (old - learning_rate * (adapter_scale * change))
    for d in range(n):
        o_ref[d] = delta[d * ROWS_DEV : (d + 1) * ROWS_DEV]


def attention_kernel(len_ref, delta_ref, base_ref, k_ref, v_ref, o_ref):
    n = delta_ref.shape[0]
    delta = jnp.concatenate([delta_ref[d] for d in range(n)], axis=1)
    query = (base_ref[...] + delta).astype(BF16).astype(F32)
    group = HEADS // KV_HEADS
    cache = k_ref.shape[1]
    many = HEADS * ROWS_DEV
    empty = jnp.zeros((group * ROWS_DEV, HEAD_DIM), F32)
    heads = []
    for g in range(KV_HEADS):
        mine = [query[:, h * HEAD_DIM : (h + 1) * HEAD_DIM] for h in range(g * group, (g + 1) * group)]
        lanes = [empty] * KV_HEADS
        lanes[g] = jnp.concatenate(mine, axis=0)
        heads.append(jnp.concatenate(lanes, axis=1))
    heads = jnp.concatenate(heads, axis=0).astype(BF16)
    row = lax.broadcasted_iota(jnp.int32, (many, cache), 0) % ROWS_DEV
    length = jnp.zeros((many, cache), jnp.int32)
    scores = jnp.zeros((many, cache), F32)
    for r in range(ROWS_DEV):
        length = jnp.where(row == r, len_ref[r], length)
        scores = jnp.where(row == r, dot(heads, k_ref[r], 1, 1), scores)
    live = lax.broadcasted_iota(jnp.int32, (many, cache), 1) < length
    scores = jnp.where(live, scores / jnp.sqrt(F32(HEAD_DIM)), F32(-1e30))
    top = jnp.max(scores, axis=-1, keepdims=True)
    expo = jnp.where(live, jnp.exp(scores - top), 0.0)
    weights = (expo / jnp.sum(expo, axis=-1, keepdims=True)).astype(BF16)
    mixed = [dot(weights, v_ref[r], 1, 0) for r in range(ROWS_DEV)]
    outs = []
    rows = group * ROWS_DEV
    row = lax.broadcasted_iota(jnp.int32, (rows, HEAD_DIM), 0) % ROWS_DEV
    for g in range(KV_HEADS):
        part = jnp.zeros((rows, HEAD_DIM), F32)
        for r in range(ROWS_DEV):
            part = jnp.where(
                row == r, mixed[r][g * rows : (g + 1) * rows, g * HEAD_DIM : (g + 1) * HEAD_DIM], part
            )
        outs.extend(part[i * ROWS_DEV : (i + 1) * ROWS_DEV] for i in range(group))
    o_ref[...] = jnp.concatenate(outs, axis=1).astype(BF16)


def exchange(x):
    return lax.all_to_all(x, "wide", split_axis=0, concat_axis=0, tiled=True)


def partner(x, mask):
    return lax.ppermute(x, "wide", [(i, i ^ mask) for i in range(lax.axis_size("wide"))])


def per_device(
    tokens,
    query_output_gradient,
    down_factors,
    up_factors_transposed,
    tenant_of_block,
    device_tenant_list,
    row_list_entry,
    hidden,
    base_query_rows,
    cached_key_rows,
    cached_value_rows,
    live_cache_length,
):
    n = lax.axis_size("wide")
    me = lax.axis_index("wide").astype(jnp.int32)
    small = n == 16
    fa, cols = down_factors.shape
    fb = up_factors_transposed.shape[0]
    local_rows = hidden.shape[0]
    rows = local_rows * n
    quarter = rows // PER_TILE
    width = tokens.shape[1]
    features = query_output_gradient.shape[1]
    assert tokens.shape[0] == BLOCK and tenant_of_block.shape[0] == n

    shape = (n, HALF, 2 * (fa + fb))
    chunks = 4 if fa % 64 == 0 and fb % 64 == 0 else 1
    packed = call(
        pick_kernel,
        jax.ShapeDtypeStruct(shape, BF16),
        [hbm(), hbm(), hbm()],
        hbm(),
        scratch=[
            pltpu.VMEM(up_factors_transposed.shape, BF16),
            pltpu.VMEM(down_factors.shape, BF16),
            pltpu.VMEM(shape, BF16),
            pltpu.SMEM((n,), jnp.int32),
            pltpu.SemaphoreType.DMA,
            pltpu.SemaphoreType.DMA((chunks,)),
            pltpu.SemaphoreType.DMA((chunks,)),
            pltpu.SemaphoreType.DMA((n,)),
        ],
        flops=2 * RANK * LANES * n * (fa + fb),
        nbytes=2 * cols * (fa + fb),
        limit=ALL_VMEM,
    )(tenant_of_block, up_factors_transposed, down_factors)

    if small:
        held = call(
            rows_pack_kernel,
            jax.ShapeDtypeStruct((HALF, width // CHUNKS + LANES), BF16),
            [smem(), smem(), vmem()],
            vmem(),
            nbytes=4 * local_rows * width,
            limit=ALL_VMEM,
        )(device_tenant_list, row_list_entry, hidden)[None]
        held = jnp.concatenate([held, partner(held, n // 2)], axis=0)
        held, packed = lax.optimization_barrier((held, packed))
        got = exchange(packed)
        held = jnp.concatenate([held, partner(held, n // 4)], axis=0)
        beside = partner(held, n // 8)

        def rows_call(*tiles):
            count = sum(t.shape[0] for t in tiles)
            shapes = [jax.ShapeDtypeStruct((count, local_rows, LANES), t) for t in (F32, F32, jnp.int32)]
            return call(
                functools.partial(rows_kernel, len(tiles)),
                shapes,
                [smem()] + [vmem()] * (2 + len(tiles)),
                [vmem()] * 3,
                scratch=[pltpu.VMEM((count * HALF, fa), BF16)],
                flops=8 * count * local_rows * (BLOCK * width + fa * cols),
                nbytes=2 * BLOCK * width + 2 * fa * cols,
            )(me[None], *tiles, tokens, down_factors)

        near = [0, n // 2, n // 4, n // 2 + n // 4]
        masks = near + [m ^ 1 for m in near] + [m ^ n // 8 for m in near] + [m ^ n // 8 ^ 1 for m in near]
        found = [rows_call(held, partner(held, 1)), rows_call(beside), rows_call(partner(beside, 1))]
        hx, base_low_rank, tenants = zip(*found)
    else:
        got = exchange(packed)
        slot = row_list_entry[:, None] == jnp.arange(device_tenant_list.shape[1], dtype=jnp.int32)[None, :]
        row_tenant = jnp.sum(jnp.where(slot, device_tenant_list, 0), axis=1)
        everyone = lax.all_gather(hidden, "wide", axis=0, tiled=True)
        tenants = lax.all_gather(row_tenant, "wide", axis=0, tiled=True)
        tenants = jnp.broadcast_to(tenants[:, None], (rows, LANES))
        hx, base_low_rank = call(
            plain_rows_kernel,
            [jax.ShapeDtypeStruct((n, local_rows, LANES), F32)] * 2,
            [vmem()] * 5,
            [vmem()] * 2,
        )(everyone, tokens, down_factors, lax.dynamic_slice(everyone, (0, me * fa), (rows, fa)), tenants)

    if not small:
        masks, hx, base_low_rank = None, (hx,), (base_low_rank,)
        tenants = (tenants.reshape(n, local_rows, LANES),)
    part_shape = (n, HALF, 2 * (fa + fb) + (LANES if small else 0))
    my_tenant = lax.dynamic_slice(tenant_of_block, (me,), (1,))
    parts, tenants, *low_rank = call(
        functools.partial(block_kernel, small, masks),
        [jax.ShapeDtypeStruct(part_shape, BF16), jax.ShapeDtypeStruct((rows, LANES), jnp.int32)]
        + ([] if small else [jax.ShapeDtypeStruct((quarter, LANES), F32)]),
        [smem(), smem()] + [vmem()] * (3 + 3 * len(hx)),
        [vmem()] * (2 if small else 3),
        scratch=[pltpu.VMEM((RANK, width), BF16), pltpu.VMEM((RANK, features), BF16)]
        + [pltpu.VMEM((n, local_rows, LANES), t) for t in (F32, F32, jnp.int32)],
        flops=4 * RANK * BLOCK * n * (fa + fb),
        nbytes=2 * BLOCK * n * (fa + fb),
    )(my_tenant, me[None], tokens, query_output_gradient, got, *hx, *base_low_rank, *tenants)
    low_rank = [lax.psum(p, "wide") for p in low_rank]
    parts = exchange(parts)
    mask = call(
        mask_kernel,
        jax.ShapeDtypeStruct((rows, cols), BF16),
        [vmem()],
        vmem(),
        flops=rows * cols,
        nbytes=2 * rows * cols,
    )(tenants)

    delta = call(
        functools.partial(delta_kernel, fa),
        jax.ShapeDtypeStruct((n, local_rows, fb), F32),
        [smem()] + [vmem()] * (4 + len(low_rank)),
        vmem(),
        flops=2 * rows * cols * fb,
        nbytes=2 * cols * fb,
    )(tenant_of_block, parts, up_factors_transposed, tenants, mask, *low_rank)
    delta = exchange(delta)

    down_gradient, up_gradient = call(
        gradient_kernel,
        [jax.ShapeDtypeStruct((fa, cols), F32), jax.ShapeDtypeStruct((fb, cols), F32)],
        [smem(), vmem()],
        [vmem()] * 2,
        flops=2 * n * RANK * (fa + fb) * LANES,
        nbytes=4 * cols * (fa + fb),
    )(tenant_of_block, parts)
    attended = call(
        attention_kernel,
        jax.ShapeDtypeStruct((local_rows, HEADS * HEAD_DIM), BF16),
        [smem(), vmem(), vmem(), vmem(), vmem()],
        vmem(),
        flops=4 * HEADS * local_rows * cached_key_rows.shape[1] * HEAD_DIM,
        nbytes=4 * cached_key_rows.size,
    )(live_cache_length, delta, base_query_rows.astype(F32), cached_key_rows, cached_value_rows)
    return down_gradient, up_gradient, attended


def solution(mesh):
    placed = (
        P(("groups", "wide"), None),
        P(("groups", "wide"), None),
        P("wide", "groups"),
        P("wide", "groups"),
        P("groups"),
        P(("groups", "wide"), None),
        P(("groups", "wide")),
        P(("groups", "wide"), None),
        P(("groups", "wide"), None),
        P(("groups", "wide"), None, None),
        P(("groups", "wide"), None, None),
        P(("groups", "wide")),
    )
    return jax.shard_map(
        per_device,
        mesh=mesh,
        in_specs=placed,
        out_specs=(P("wide", "groups"), P("wide", "groups"), P(("groups", "wide"), None)),
        check_vma=False,
    )
```

```python
import functools

import jax
import jax.numpy as jnp
from jax import lax
from jax.experimental import pallas as pl
from jax.experimental.pallas import tpu as pltpu
from jax.sharding import PartitionSpec as P

HEAD_DIM = 128
HEADS = 32
KV_HEADS = 4
RANK = 32
TENANTS = 64
BLOCK = 128
ROWS_DEV = 4
LANES = 128
PER_TILE = LANES // RANK

adapter_scale = 2.0
learning_rate = 0.0002

F32 = jnp.float32
BF16 = jnp.bfloat16
VMEM_LIMIT = 24 * 1024 * 1024
ALL_VMEM = 60 * 1024 * 1024


def vmem():
    return pl.BlockSpec(memory_space=pltpu.VMEM)


def smem():
    return pl.BlockSpec(memory_space=pltpu.SMEM)


def hbm():
    return pl.BlockSpec(memory_space=pltpu.HBM)


def call(kernel, out_shape, in_specs, out_specs, scratch=(), flops=0, nbytes=0, limit=VMEM_LIMIT):
    return pl.pallas_call(
        kernel,
        out_shape=out_shape,
        in_specs=in_specs,
        out_specs=out_specs,
        scratch_shapes=list(scratch),
        compiler_params=pltpu.CompilerParams(vmem_limit_bytes=limit),
        cost_estimate=pl.CostEstimate(flops=flops, bytes_accessed=nbytes, transcendentals=0),
    )


def each(count, body):
    if count <= 16:
        for j in range(count):
            body(j)
    else:
        pl.loop(0, count)(body)


def dot(a, b, ca, cb):
    return lax.dot_general(a, b, (((ca,), (cb,)), ((), ())), preferred_element_type=F32)


def quarter_indicator(quarter, value):
    lane = lax.broadcasted_iota(jnp.int32, (RANK, LANES), 1)
    row = lax.broadcasted_iota(jnp.int32, (RANK, LANES), 0)
    return jnp.where(lane - row == quarter * RANK, value, 0.0).astype(BF16)


def tile_of(tenant):
    return pl.ds(pl.multiple_of((tenant // PER_TILE) * LANES, LANES), LANES)


HALF = RANK // 2
CHUNKS = HALF // ROWS_DEV


def up_half(h, fa, fb):
    return slice(h * fb, (h + 1) * fb)


def down_half(h, fa, fb):
    return slice(2 * fb + h * fa, 2 * fb + (h + 1) * fa)


def pick_kernel(tenant_ref, b_ref, a_ref, o_ref, b_tab, a_tab, o_buf, t_ref, sem_t, sem_b, sem_a, sem_o):
    n = t_ref.shape[0]
    fa, fb = a_ref.shape[0], b_ref.shape[0]

    def loads(src, dst, sem):
        step = src.shape[0] // sem.shape[0]
        parts = [slice(c * step, (c + 1) * step) for c in range(sem.shape[0])]
        return [pltpu.make_async_copy(src.at[r], dst.at[r], sem.at[c]) for c, r in enumerate(parts)]

    first, second = loads(b_ref, b_tab, sem_b), loads(a_ref, a_tab, sem_a)
    tenants = pltpu.make_async_copy(tenant_ref, t_ref, sem_t)
    for load in [tenants] + first + second:
        load.start()

    def picked(j, table):
        t = t_ref[j]
        return dot(quarter_indicator(t % PER_TILE, 1.0), table[:, tile_of(t)], 1, 1).astype(BF16)

    def up_body(j):
        up = picked(j, b_tab)
        for h in range(2):
            o_buf[j, :, up_half(h, fa, fb)] = up[h * HALF : (h + 1) * HALF]

    def down_body(j):
        down = picked(j, a_tab)
        for h in range(2):
            o_buf[j, :, down_half(h, fa, fb)] = down[h * HALF : (h + 1) * HALF]
        pltpu.make_async_copy(o_buf.at[j], o_ref.at[j], sem_o.at[j]).start()

    def finish(j):
        pltpu.make_async_copy(o_buf.at[j], o_ref.at[j], sem_o.at[j]).wait()

    for load in [tenants] + first:
        load.wait()
    each(n, up_body)
    for load in second:
        load.wait()
    each(n, down_body)
    each(n, finish)


def rows_pack_kernel(list_ref, slot_ref, hidden_ref, o_ref):
    hidden = hidden_ref[...].astype(F32)
    size = hidden.shape[1] // CHUNKS
    main = jnp.concatenate([hidden[:, p * size : (p + 1) * size] for p in range(CHUNKS)], axis=0)
    row = lax.broadcasted_iota(jnp.int32, (HALF, LANES), 0) % ROWS_DEV
    mark = jnp.zeros((HALF, LANES), jnp.int32)
    for r in range(ROWS_DEV):
        mark = jnp.where(row == r, list_ref[0, slot_ref[r]], mark)
    o_ref[...] = jnp.concatenate([main, mark.astype(F32)], axis=1).astype(BF16)


def fold_rows(product, tenant):
    rows = product.shape[0]
    lane = lax.broadcasted_iota(jnp.int32, (rows, LANES), 1)
    total = jnp.zeros((rows, LANES), F32)
    for c in range(TENANTS // PER_TILE):
        mine = tenant == c * PER_TILE + lane // RANK
        total = total + jnp.where(mine, product[:, c * LANES : (c + 1) * LANES], 0.0)
    half = total + pltpu.roll(total, 2 * RANK, 1)
    return half + pltpu.roll(half, RANK, 1)


def rows_kernel(me_ref, h0_ref, h1_ref, x_ref, a_ref, _, hx_ref, base_ref, u_ref, sel):
    h = jnp.concatenate([r[k] for r in (h0_ref, h1_ref) for k in range(r.shape[0])], axis=0)
    size = h.shape[1] - LANES
    fa = a_ref.shape[0]
    part = lax.broadcasted_iota(jnp.int32, (h.shape[0], LANES), 0) % HALF // ROWS_DEV
    hx = jnp.zeros((h.shape[0], LANES), F32)
    for p in range(CHUNKS):
        hx = jnp.where(part == p, dot(h[:, :size], x_ref[:, p * size : (p + 1) * size], 1, 1), hx)
    per_chunk = size // fa
    for m in range(per_chunk):

        @pl.when(me_ref[0] % per_chunk == m)
        def _():
            sel[...] = h[:, m * fa : (m + 1) * fa]

    tenant = h[:, size:].astype(F32).astype(jnp.int32)
    base = fold_rows(dot(sel[...], a_ref[...], 1, 0), tenant)
    base = jnp.where(part == me_ref[0] // per_chunk, base, 0.0)
    for k in range(h.shape[0] // HALF):
        for value, dest in ((hx, hx_ref), (base, base_ref)):
            eight = value[k * HALF : k * HALF + 8] + value[k * HALF + 8 : (k + 1) * HALF]
            dest[k] = eight[:ROWS_DEV] + eight[ROWS_DEV:]
        u_ref[k] = tenant[k * HALF : k * HALF + ROWS_DEV]


def plain_rows_kernel(h_ref, x_ref, a_ref, hc_ref, u_ref, hx_ref, base_ref):
    hx = dot(h_ref[...], x_ref[...], 1, 1)
    base = fold_rows(dot(hc_ref[...], a_ref[...], 1, 0), u_ref[...])
    for d in range(hx_ref.shape[0]):
        hx_ref[d] = hx[d * ROWS_DEV : (d + 1) * ROWS_DEV]
        base_ref[d] = base[d * ROWS_DEV : (d + 1) * ROWS_DEV]


def block_kernel(ride, masks, t_ref, me_ref, x_ref, g_ref, r_ref, *refs):
    sets = (len(refs) - (7 if ride else 8)) // 3
    hx_sets, base_sets, u_sets = (refs[i * sets : (i + 1) * sets] for i in range(3))
    o_ref, u_ref = refs[3 * sets : 3 * sets + 2]
    wa_ref, wb_ref, sx, sb, su = refs[-5:]
    n = r_ref.shape[0]
    fa, fb = x_ref.shape[1] // n, g_ref.shape[1] // n
    for d in range(n):
        for h in range(2):
            rank = slice(h * HALF, (h + 1) * HALF)
            wb_ref[rank, d * fb : (d + 1) * fb] = r_ref[d, :, up_half(h, fa, fb)]
            wa_ref[rank, d * fa : (d + 1) * fa] = r_ref[d, :, down_half(h, fa, fb)]
    back = dot(wb_ref[...], g_ref[...], 1, 1).astype(BF16)
    down = dot(wa_ref[...], x_ref[...], 1, 1).astype(BF16)

    k = 0
    for hx_ref, base_ref, tile_ref in zip(hx_sets, base_sets, u_sets):
        for i in range(hx_ref.shape[0]):
            d = me_ref[0] ^ masks[k] if masks else i
            sx[d], sb[d], su[d] = hx_ref[i], base_ref[i], tile_ref[i]
            k += 1
    hx, base, tenant = (jnp.concatenate([v[d] for d in range(n)], axis=0) for v in (sx, sb, su))
    u_ref[...] = tenant
    high = hx.astype(BF16)
    low = (hx - high.astype(F32)).astype(BF16)
    wide_back = jnp.concatenate([back] * PER_TILE, axis=0)
    change = dot(high, wide_back, 1, 1) + dot(low, wide_back, 1, 1)
    mine = tenant == t_ref[0]
    full = base - jnp.where(mine, learning_rate * (adapter_scale * change), 0.0)
    quarter = full.shape[0] // PER_TILE
    spot = lax.broadcasted_iota(jnp.int32, (quarter, LANES), 1) // RANK
    packed = jnp.zeros((quarter, LANES), F32)
    for q in range(PER_TILE):
        packed = packed + jnp.where(spot == q, full[q * quarter : (q + 1) * quarter], 0.0)
    if not ride:
        refs[3 * sets + 2][...] = packed

    down_part = dot(back, x_ref[...], 1, 0).astype(BF16)
    up_part = dot(down, g_ref[...], 1, 0).astype(BF16)
    for d in range(n):
        for h in range(2):
            rank = slice(h * HALF, (h + 1) * HALF)
            o_ref[d, :, up_half(h, fa, fb)] = up_part[rank, d * fb : (d + 1) * fb]
            o_ref[d, :, down_half(h, fa, fb)] = down_part[rank, d * fa : (d + 1) * fa]
        if ride:
            o_ref[d, :, 2 * (fa + fb) :] = packed.astype(BF16)


def sum_by_tenant(t_ref, part_ref, cut, fa, fb, grad_ref):
    grad_ref[...] = jnp.zeros_like(grad_ref)

    def body(j):
        t = t_ref[j]
        part = jnp.concatenate([part_ref[j, :, cut(h, fa, fb)] for h in range(2)], axis=0)
        place = quarter_indicator(t % PER_TILE, adapter_scale)
        grad_ref[:, tile_of(t)] += dot(part, place, 0, 0)

    each(t_ref.shape[0], body)


def gradient_kernel(t_ref, part_ref, down_ref, up_ref):
    fa, fb = down_ref.shape[0], up_ref.shape[0]
    sum_by_tenant(t_ref, part_ref, down_half, fa, fb, down_ref)
    sum_by_tenant(t_ref, part_ref, up_half, fa, fb, up_ref)


def delta_kernel(fa, t_ref, part_ref, b_ref, u_ref, *refs):
    o_ref = refs[-1]
    n, fb = part_ref.shape[0], b_ref.shape[0]
    if len(refs) == 2:
        total = refs[0][...]
    else:
        total = part_ref[0, :, 2 * (fa + fb) :].astype(F32)
        for d in range(1, n):
            total = total + part_ref[d, :, 2 * (fa + fb) :].astype(F32)
    spot = lax.broadcasted_iota(jnp.int32, total.shape, 1) // RANK
    pieces = []
    for q in range(PER_TILE):
        one = jnp.where(spot == q, total, 0.0)
        half = one + pltpu.roll(one, 2 * RANK, 1)
        pieces.append(half + pltpu.roll(half, RANK, 1))
    adapted = jnp.concatenate(pieces, axis=0)
    quarter = lax.broadcasted_iota(jnp.int32, adapted.shape, 1) // RANK
    tenant = u_ref[...]
    spread = [
        jnp.where(tenant == c * PER_TILE + quarter, adapted, 0.0).astype(BF16) for c in range(TENANTS // PER_TILE)
    ]
    old = dot(jnp.concatenate(spread, axis=1), b_ref[...], 1, 1)
    matched = []
    for c in range(n // PER_TILE):
        block = jnp.zeros(adapted.shape, jnp.int32)
        for i in range(PER_TILE):
            block = jnp.where(quarter == i, t_ref[c * PER_TILE + i], block)
        matched.append(jnp.where(tenant == block, adapted, 0.0).astype(BF16))
    up = [part_ref[j, :, up_half(h, fa, fb)] for j in range(n) for h in range(2)]
    change = dot(jnp.concatenate(matched, axis=1), jnp.concatenate(up, axis=0), 1, 0)
    delta = adapter_scale * (old - learning_rate * (adapter_scale * change))
    for d in range(n):
        o_ref[d] = delta[d * ROWS_DEV : (d + 1) * ROWS_DEV]


def attention_kernel(len_ref, delta_ref, base_ref, k_ref, v_ref, o_ref):
    n = delta_ref.shape[0]
    delta = jnp.concatenate([delta_ref[d] for d in range(n)], axis=1)
    query = (base_ref[...] + delta).astype(BF16).astype(F32)
    group = HEADS // KV_HEADS
    cache = k_ref.shape[1]
    many = HEADS * ROWS_DEV
    empty = jnp.zeros((group * ROWS_DEV, HEAD_DIM), F32)
    heads = []
    for g in range(KV_HEADS):
        mine = [query[:, h * HEAD_DIM : (h + 1) * HEAD_DIM] for h in range(g * group, (g + 1) * group)]
        lanes = [empty] * KV_HEADS
        lanes[g] = jnp.concatenate(mine, axis=0)
        heads.append(jnp.concatenate(lanes, axis=1))
    heads = jnp.concatenate(heads, axis=0).astype(BF16)
    row = lax.broadcasted_iota(jnp.int32, (many, cache), 0) % ROWS_DEV
    length = jnp.zeros((many, cache), jnp.int32)
    scores = jnp.zeros((many, cache), F32)
    for r in range(ROWS_DEV):
        length = jnp.where(row == r, len_ref[r], length)
        scores = jnp.where(row == r, dot(heads, k_ref[r], 1, 1), scores)
    live = lax.broadcasted_iota(jnp.int32, (many, cache), 1) < length
    scores = jnp.where(live, scores / jnp.sqrt(F32(HEAD_DIM)), F32(-1e30))
    top = jnp.max(scores, axis=-1, keepdims=True)
    expo = jnp.where(live, jnp.exp(scores - top), 0.0)
    weights = (expo / jnp.sum(expo, axis=-1, keepdims=True)).astype(BF16)
    mixed = [dot(weights, v_ref[r], 1, 0) for r in range(ROWS_DEV)]
    outs = []
    rows = group * ROWS_DEV
    row = lax.broadcasted_iota(jnp.int32, (rows, HEAD_DIM), 0) % ROWS_DEV
    for g in range(KV_HEADS):
        part = jnp.zeros((rows, HEAD_DIM), F32)
        for r in range(ROWS_DEV):
            part = jnp.where(
                row == r, mixed[r][g * rows : (g + 1) * rows, g * HEAD_DIM : (g + 1) * HEAD_DIM], part
            )
        outs.extend(part[i * ROWS_DEV : (i + 1) * ROWS_DEV] for i in range(group))
    o_ref[...] = jnp.concatenate(outs, axis=1).astype(BF16)


def exchange(x):
    return lax.all_to_all(x, "wide", split_axis=0, concat_axis=0, tiled=True)


def partner(x, mask):
    return lax.ppermute(x, "wide", [(i, i ^ mask) for i in range(lax.axis_size("wide"))])


def per_device(
    tokens,
    query_output_gradient,
    down_factors,
    up_factors_transposed,
    tenant_of_block,
    device_tenant_list,
    row_list_entry,
    hidden,
    base_query_rows,
    cached_key_rows,
    cached_value_rows,
    live_cache_length,
):
    n = lax.axis_size("wide")
    me = lax.axis_index("wide").astype(jnp.int32)
    small = n == 16
    fa, cols = down_factors.shape
    fb = up_factors_transposed.shape[0]
    local_rows = hidden.shape[0]
    rows = local_rows * n
    quarter = rows // PER_TILE
    width = tokens.shape[1]
    features = query_output_gradient.shape[1]
    assert tokens.shape[0] == BLOCK and tenant_of_block.shape[0] == n

    shape = (n, HALF, 2 * (fa + fb))
    chunks = 4 if fa % 64 == 0 and fb % 64 == 0 else 1
    packed = call(
        pick_kernel,
        jax.ShapeDtypeStruct(shape, BF16),
        [hbm(), hbm(), hbm()],
        hbm(),
        scratch=[
            pltpu.VMEM(up_factors_transposed.shape, BF16),
            pltpu.VMEM(down_factors.shape, BF16),
            pltpu.VMEM(shape, BF16),
            pltpu.SMEM((n,), jnp.int32),
            pltpu.SemaphoreType.DMA,
            pltpu.SemaphoreType.DMA((chunks,)),
            pltpu.SemaphoreType.DMA((chunks,)),
            pltpu.SemaphoreType.DMA((n,)),
        ],
        flops=2 * RANK * LANES * n * (fa + fb),
        nbytes=2 * cols * (fa + fb),
        limit=ALL_VMEM,
    )(tenant_of_block, up_factors_transposed, down_factors)

    if small:
        held = call(
            rows_pack_kernel,
            jax.ShapeDtypeStruct((HALF, width // CHUNKS + LANES), BF16),
            [smem(), smem(), vmem()],
            vmem(),
            nbytes=4 * local_rows * width,
            limit=ALL_VMEM,
        )(device_tenant_list, row_list_entry, hidden)[None]
        held = jnp.concatenate([held, partner(held, n // 2)], axis=0)
        held, packed = lax.optimization_barrier((held, packed))
        got = exchange(packed)
        masks = [0, n // 2]
        bit = n // 4
        while bit > 1:
            held = jnp.concatenate([held, partner(held, bit)], axis=0)
            masks = masks + [m ^ bit for m in masks]
            bit //= 2
        masks = masks + [m ^ 1 for m in masks]
        found = call(
            rows_kernel,
            [jax.ShapeDtypeStruct((n, local_rows, LANES), t) for t in (F32, F32, jnp.int32)],
            [smem()] + [vmem()] * 5,
            [vmem()] * 3,
            scratch=[pltpu.VMEM((n * HALF, fa), BF16)],
            flops=8 * rows * (BLOCK * width + fa * cols),
            nbytes=2 * BLOCK * width + 2 * fa * cols,
        )(me[None], held, partner(held, 1), tokens, down_factors, query_output_gradient)
        hx, base_low_rank, tenants = ((f,) for f in found)
    else:
        got = exchange(packed)
        slot = row_list_entry[:, None] == jnp.arange(device_tenant_list.shape[1], dtype=jnp.int32)[None, :]
        row_tenant = jnp.sum(jnp.where(slot, device_tenant_list, 0), axis=1)
        everyone = lax.all_gather(hidden, "wide", axis=0, tiled=True)
        tenants = lax.all_gather(row_tenant, "wide", axis=0, tiled=True)
        tenants = jnp.broadcast_to(tenants[:, None], (rows, LANES))
        hx, base_low_rank = call(
            plain_rows_kernel,
            [jax.ShapeDtypeStruct((n, local_rows, LANES), F32)] * 2,
            [vmem()] * 5,
            [vmem()] * 2,
        )(everyone, tokens, down_factors, lax.dynamic_slice(everyone, (0, me * fa), (rows, fa)), tenants)

    if not small:
        masks, hx, base_low_rank = None, (hx,), (base_low_rank,)
        tenants = (tenants.reshape(n, local_rows, LANES),)
    part_shape = (n, HALF, 2 * (fa + fb) + (LANES if small else 0))
    my_tenant = lax.dynamic_slice(tenant_of_block, (me,), (1,))
    parts, tenants, *low_rank = call(
        functools.partial(block_kernel, small, masks),
        [jax.ShapeDtypeStruct(part_shape, BF16), jax.ShapeDtypeStruct((rows, LANES), jnp.int32)]
        + ([] if small else [jax.ShapeDtypeStruct((quarter, LANES), F32)]),
        [smem(), smem()] + [vmem()] * (3 + 3 * len(hx)),
        [vmem()] * (2 if small else 3),
        scratch=[pltpu.VMEM((RANK, width), BF16), pltpu.VMEM((RANK, features), BF16)]
        + [pltpu.VMEM((n, local_rows, LANES), t) for t in (F32, F32, jnp.int32)],
        flops=4 * RANK * BLOCK * n * (fa + fb),
        nbytes=2 * BLOCK * n * (fa + fb),
    )(my_tenant, me[None], tokens, query_output_gradient, got, *hx, *base_low_rank, *tenants)
    low_rank = [lax.psum(p, "wide") for p in low_rank]
    parts = exchange(parts)

    delta = call(
        functools.partial(delta_kernel, fa),
        jax.ShapeDtypeStruct((n, local_rows, fb), F32),
        [smem()] + [vmem()] * (3 + len(low_rank)),
        vmem(),
        flops=2 * rows * cols * fb,
        nbytes=2 * cols * fb,
    )(tenant_of_block, parts, up_factors_transposed, tenants, *low_rank)
    delta = exchange(delta)

    down_gradient, up_gradient = call(
        gradient_kernel,
        [jax.ShapeDtypeStruct((fa, cols), F32), jax.ShapeDtypeStruct((fb, cols), F32)],
        [smem(), vmem()],
        [vmem()] * 2,
        flops=2 * n * RANK * (fa + fb) * LANES,
        nbytes=4 * cols * (fa + fb),
    )(tenant_of_block, parts)
    attended = call(
        attention_kernel,
        jax.ShapeDtypeStruct((local_rows, HEADS * HEAD_DIM), BF16),
        [smem(), vmem(), vmem(), vmem(), vmem()],
        vmem(),
        flops=4 * HEADS * local_rows * cached_key_rows.shape[1] * HEAD_DIM,
        nbytes=4 * cached_key_rows.size,
    )(live_cache_length, delta, base_query_rows.astype(F32), cached_key_rows, cached_value_rows)
    return down_gradient, up_gradient, attended


def solution(mesh):
    placed = (
        P(("groups", "wide"), None),
        P(("groups", "wide"), None),
        P("wide", "groups"),
        P("wide", "groups"),
        P("groups"),
        P(("groups", "wide"), None),
        P(("groups", "wide")),
        P(("groups", "wide"), None),
        P(("groups", "wide"), None),
        P(("groups", "wide"), None, None),
        P(("groups", "wide"), None, None),
        P(("groups", "wide")),
    )
    return jax.shard_map(
        per_device,
        mesh=mesh,
        in_specs=placed,
        out_specs=(P("wide", "groups"), P("wide", "groups"), P(("groups", "wide"), None)),
        check_vma=False,
    )
```

```python
import functools

import jax
import jax.numpy as jnp
from jax import lax
from jax.experimental import pallas as pl
from jax.experimental.pallas import tpu as pltpu
from jax.sharding import PartitionSpec as P

HEAD_DIM = 128
HEADS = 32
KV_HEADS = 4
RANK = 32
TENANTS = 64
BLOCK = 128
ROWS_DEV = 4
LANES = 128
PER_TILE = LANES // RANK

adapter_scale = 2.0
learning_rate = 0.0002

F32 = jnp.float32
BF16 = jnp.bfloat16
VMEM_LIMIT = 24 * 1024 * 1024
ALL_VMEM = 58 * 1024 * 1024 + 768 * 1024


def vmem():
    return pl.BlockSpec(memory_space=pltpu.VMEM)


def smem():
    return pl.BlockSpec(memory_space=pltpu.SMEM)


def hbm():
    return pl.BlockSpec(memory_space=pltpu.HBM)


def call(kernel, out_shape, in_specs, out_specs, scratch=(), flops=0, nbytes=0, limit=VMEM_LIMIT):
    return pl.pallas_call(
        kernel,
        out_shape=out_shape,
        in_specs=in_specs,
        out_specs=out_specs,
        scratch_shapes=list(scratch),
        compiler_params=pltpu.CompilerParams(vmem_limit_bytes=limit),
        cost_estimate=pl.CostEstimate(flops=flops, bytes_accessed=nbytes, transcendentals=0),
    )


def each(count, body):
    if count <= 16:
        for j in range(count):
            body(j)
    else:
        pl.loop(0, count)(body)


def dot(a, b, ca, cb):
    return lax.dot_general(a, b, (((ca,), (cb,)), ((), ())), preferred_element_type=F32)


def quarter_indicator(quarter, value):
    lane = lax.broadcasted_iota(jnp.int32, (RANK, LANES), 1)
    row = lax.broadcasted_iota(jnp.int32, (RANK, LANES), 0)
    return jnp.where(lane - row == quarter * RANK, value, 0.0).astype(BF16)


def tile_of(tenant):
    return pl.ds(pl.multiple_of((tenant // PER_TILE) * LANES, LANES), LANES)


HALF = RANK // 2
CHUNKS = HALF // ROWS_DEV


def up_half(h, fa, fb):
    return slice(h * fb, (h + 1) * fb)


def down_half(h, fa, fb):
    return slice(2 * fb + h * fa, 2 * fb + (h + 1) * fa)


def pick_kernel(tenant_ref, b_ref, a_ref, o_ref, b_tab, a_tab, o_buf, t_ref, sem_t, sem_b, sem_a, sem_o):
    n = t_ref.shape[0]
    fa, fb = a_ref.shape[0], b_ref.shape[0]

    def loads(src, dst, sem):
        step = src.shape[0] // sem.shape[0]
        parts = [slice(c * step, (c + 1) * step) for c in range(sem.shape[0])]
        return [pltpu.make_async_copy(src.at[r], dst.at[r], sem.at[c]) for c, r in enumerate(parts)]

    first, second = loads(b_ref, b_tab, sem_b), loads(a_ref, a_tab, sem_a)
    tenants = pltpu.make_async_copy(tenant_ref, t_ref, sem_t)
    for load in [tenants] + first + second:
        load.start()

    def picked(j, table):
        t = t_ref[j]
        return dot(quarter_indicator(t % PER_TILE, 1.0), table[:, tile_of(t)], 1, 1).astype(BF16)

    def up_body(j):
        up = picked(j, b_tab)
        for h in range(2):
            o_buf[j, :, up_half(h, fa, fb)] = up[h * HALF : (h + 1) * HALF]

    def down_body(j):
        down = picked(j, a_tab)
        for h in range(2):
            o_buf[j, :, down_half(h, fa, fb)] = down[h * HALF : (h + 1) * HALF]
        pltpu.make_async_copy(o_buf.at[j], o_ref.at[j], sem_o.at[j]).start()

    def finish(j):
        pltpu.make_async_copy(o_buf.at[j], o_ref.at[j], sem_o.at[j]).wait()

    for load in [tenants] + first:
        load.wait()
    each(n, up_body)
    for load in second:
        load.wait()
    each(n, down_body)
    each(n, finish)


def rows_pack_kernel(list_ref, slot_ref, hidden_ref, o_ref):
    hidden = hidden_ref[...].astype(F32)
    size = hidden.shape[1] // CHUNKS
    main = jnp.concatenate([hidden[:, p * size : (p + 1) * size] for p in range(CHUNKS)], axis=0)
    row = lax.broadcasted_iota(jnp.int32, (HALF, LANES), 0) % ROWS_DEV
    mark = jnp.zeros((HALF, LANES), jnp.int32)
    for r in range(ROWS_DEV):
        mark = jnp.where(row == r, list_ref[0, slot_ref[r]], mark)
    o_ref[...] = jnp.concatenate([main, mark.astype(F32)], axis=1).astype(BF16)


def fold_rows(product, tenant):
    rows = product.shape[0]
    lane = lax.broadcasted_iota(jnp.int32, (rows, LANES), 1)
    total = jnp.zeros((rows, LANES), F32)
    for c in range(TENANTS // PER_TILE):
        mine = tenant == c * PER_TILE + lane // RANK
        total = total + jnp.where(mine, product[:, c * LANES : (c + 1) * LANES], 0.0)
    half = total + pltpu.roll(total, 2 * RANK, 1)
    return half + pltpu.roll(half, RANK, 1)


def rows_kernel(me_ref, h0_ref, h1_ref, x_ref, a_ref, hx_ref, base_ref, u_ref, sel):
    h = jnp.concatenate([r[k] for r in (h0_ref, h1_ref) for k in range(r.shape[0])], axis=0)
    size = h.shape[1] - LANES
    fa = a_ref.shape[0]
    part = lax.broadcasted_iota(jnp.int32, (h.shape[0], LANES), 0) % HALF // ROWS_DEV
    hx = jnp.zeros((h.shape[0], LANES), F32)
    for p in range(CHUNKS):
        hx = jnp.where(part == p, dot(h[:, :size], x_ref[:, p * size : (p + 1) * size], 1, 1), hx)
    per_chunk = size // fa
    for m in range(per_chunk):

        @pl.when(me_ref[0] % per_chunk == m)
        def _():
            sel[...] = h[:, m * fa : (m + 1) * fa]

    tenant = h[:, size:].astype(F32).astype(jnp.int32)
    base = fold_rows(dot(sel[...], a_ref[...], 1, 0), tenant)
    base = jnp.where(part == me_ref[0] // per_chunk, base, 0.0)
    for k in range(h.shape[0] // HALF):
        for value, dest in ((hx, hx_ref), (base, base_ref)):
            eight = value[k * HALF : k * HALF + 8] + value[k * HALF + 8 : (k + 1) * HALF]
            dest[k] = eight[:ROWS_DEV] + eight[ROWS_DEV:]
        u_ref[k] = tenant[k * HALF : k * HALF + ROWS_DEV]


def plain_rows_kernel(h_ref, x_ref, a_ref, hc_ref, u_ref, hx_ref, base_ref):
    hx = dot(h_ref[...], x_ref[...], 1, 1)
    base = fold_rows(dot(hc_ref[...], a_ref[...], 1, 0), u_ref[...])
    for d in range(hx_ref.shape[0]):
        hx_ref[d] = hx[d * ROWS_DEV : (d + 1) * ROWS_DEV]
        base_ref[d] = base[d * ROWS_DEV : (d + 1) * ROWS_DEV]


def block_kernel(ride, masks, t_ref, me_ref, x_ref, g_ref, r_ref, *refs):
    sets = (len(refs) - (7 if ride else 8)) // 3
    hx_sets, base_sets, u_sets = (refs[i * sets : (i + 1) * sets] for i in range(3))
    o_ref, u_ref = refs[3 * sets : 3 * sets + 2]
    wa_ref, wb_ref, sx, sb, su = refs[-5:]
    n = r_ref.shape[0]
    fa, fb = x_ref.shape[1] // n, g_ref.shape[1] // n
    for d in range(n):
        for h in range(2):
            rank = slice(h * HALF, (h + 1) * HALF)
            wb_ref[rank, d * fb : (d + 1) * fb] = r_ref[d, :, up_half(h, fa, fb)]
            wa_ref[rank, d * fa : (d + 1) * fa] = r_ref[d, :, down_half(h, fa, fb)]
    back = dot(wb_ref[...], g_ref[...], 1, 1).astype(BF16)
    down = dot(wa_ref[...], x_ref[...], 1, 1).astype(BF16)

    k = 0
    for hx_ref, base_ref, tile_ref in zip(hx_sets, base_sets, u_sets):
        for i in range(hx_ref.shape[0]):
            d = me_ref[0] ^ masks[k] if masks else i
            sx[d], sb[d], su[d] = hx_ref[i], base_ref[i], tile_ref[i]
            k += 1
    hx, base, tenant = (jnp.concatenate([v[d] for d in range(n)], axis=0) for v in (sx, sb, su))
    u_ref[...] = tenant
    high = hx.astype(BF16)
    low = (hx - high.astype(F32)).astype(BF16)
    wide_back = jnp.concatenate([back] * PER_TILE, axis=0)
    change = dot(high, wide_back, 1, 1) + dot(low, wide_back, 1, 1)
    mine = tenant == t_ref[0]
    full = base - jnp.where(mine, learning_rate * (adapter_scale * change), 0.0)
    quarter = full.shape[0] // PER_TILE
    spot = lax.broadcasted_iota(jnp.int32, (quarter, LANES), 1) // RANK
    packed = jnp.zeros((quarter, LANES), F32)
    for q in range(PER_TILE):
        packed = packed + jnp.where(spot == q, full[q * quarter : (q + 1) * quarter], 0.0)
    if not ride:
        refs[3 * sets + 2][...] = packed

    down_part = dot(back, x_ref[...], 1, 0).astype(BF16)
    up_part = dot(down, g_ref[...], 1, 0).astype(BF16)
    for d in range(n):
        for h in range(2):
            rank = slice(h * HALF, (h + 1) * HALF)
            o_ref[d, :, up_half(h, fa, fb)] = up_part[rank, d * fb : (d + 1) * fb]
            o_ref[d, :, down_half(h, fa, fb)] = down_part[rank, d * fa : (d + 1) * fa]
        if ride:
            o_ref[d, :, 2 * (fa + fb) :] = packed.astype(BF16)


def sum_by_tenant(t_ref, part_ref, cut, fa, fb, grad_ref):
    grad_ref[...] = jnp.zeros_like(grad_ref)

    def body(j):
        t = t_ref[j]
        part = jnp.concatenate([part_ref[j, :, cut(h, fa, fb)] for h in range(2)], axis=0)
        place = quarter_indicator(t % PER_TILE, adapter_scale)
        grad_ref[:, tile_of(t)] += dot(part, place, 0, 0)

    each(t_ref.shape[0], body)


def gradient_kernel(t_ref, part_ref, down_ref, up_ref):
    fa, fb = down_ref.shape[0], up_ref.shape[0]
    sum_by_tenant(t_ref, part_ref, down_half, fa, fb, down_ref)
    sum_by_tenant(t_ref, part_ref, up_half, fa, fb, up_ref)


def delta_kernel(fa, t_ref, part_ref, b_ref, u_ref, *refs):
    o_ref = refs[-1]
    n, fb = part_ref.shape[0], b_ref.shape[0]
    if len(refs) == 2:
        total = refs[0][...]
    else:
        total = part_ref[0, :, 2 * (fa + fb) :].astype(F32)
        for d in range(1, n):
            total = total + part_ref[d, :, 2 * (fa + fb) :].astype(F32)
    spot = lax.broadcasted_iota(jnp.int32, total.shape, 1) // RANK
    pieces = []
    for q in range(PER_TILE):
        one = jnp.where(spot == q, total, 0.0)
        half = one + pltpu.roll(one, 2 * RANK, 1)
        pieces.append(half + pltpu.roll(half, RANK, 1))
    adapted = jnp.concatenate(pieces, axis=0)
    quarter = lax.broadcasted_iota(jnp.int32, adapted.shape, 1) // RANK
    tenant = u_ref[...]
    spread = [
        jnp.where(tenant == c * PER_TILE + quarter, adapted, 0.0).astype(BF16) for c in range(TENANTS // PER_TILE)
    ]
    old = dot(jnp.concatenate(spread, axis=1), b_ref[...], 1, 1)
    matched = []
    for c in range(n // PER_TILE):
        block = jnp.zeros(adapted.shape, jnp.int32)
        for i in range(PER_TILE):
            block = jnp.where(quarter == i, t_ref[c * PER_TILE + i], block)
        matched.append(jnp.where(tenant == block, adapted, 0.0).astype(BF16))
    up = [part_ref[j, :, up_half(h, fa, fb)] for j in range(n) for h in range(2)]
    change = dot(jnp.concatenate(matched, axis=1), jnp.concatenate(up, axis=0), 1, 0)
    delta = adapter_scale * (old - learning_rate * (adapter_scale * change))
    for d in range(n):
        o_ref[d] = delta[d * ROWS_DEV : (d + 1) * ROWS_DEV]


def attention_kernel(len_ref, delta_ref, base_ref, k_ref, v_ref, o_ref):
    n = delta_ref.shape[0]
    delta = jnp.concatenate([delta_ref[d] for d in range(n)], axis=1)
    query = (base_ref[...] + delta).astype(BF16).astype(F32)
    group = HEADS // KV_HEADS
    cache = k_ref.shape[1]
    many = HEADS * ROWS_DEV
    empty = jnp.zeros((group * ROWS_DEV, HEAD_DIM), F32)
    heads = []
    for g in range(KV_HEADS):
        mine = [query[:, h * HEAD_DIM : (h + 1) * HEAD_DIM] for h in range(g * group, (g + 1) * group)]
        lanes = [empty] * KV_HEADS
        lanes[g] = jnp.concatenate(mine, axis=0)
        heads.append(jnp.concatenate(lanes, axis=1))
    heads = jnp.concatenate(heads, axis=0).astype(BF16)
    row = lax.broadcasted_iota(jnp.int32, (many, cache), 0) % ROWS_DEV
    length = jnp.zeros((many, cache), jnp.int32)
    scores = jnp.zeros((many, cache), F32)
    for r in range(ROWS_DEV):
        length = jnp.where(row == r, len_ref[r], length)
        scores = jnp.where(row == r, dot(heads, k_ref[r], 1, 1), scores)
    live = lax.broadcasted_iota(jnp.int32, (many, cache), 1) < length
    scores = jnp.where(live, scores / jnp.sqrt(F32(HEAD_DIM)), F32(-1e30))
    top = jnp.max(scores, axis=-1, keepdims=True)
    expo = jnp.where(live, jnp.exp(scores - top), 0.0)
    weights = (expo / jnp.sum(expo, axis=-1, keepdims=True)).astype(BF16)
    mixed = [dot(weights, v_ref[r], 1, 0) for r in range(ROWS_DEV)]
    outs = []
    rows = group * ROWS_DEV
    row = lax.broadcasted_iota(jnp.int32, (rows, HEAD_DIM), 0) % ROWS_DEV
    for g in range(KV_HEADS):
        part = jnp.zeros((rows, HEAD_DIM), F32)
        for r in range(ROWS_DEV):
            part = jnp.where(
                row == r, mixed[r][g * rows : (g + 1) * rows, g * HEAD_DIM : (g + 1) * HEAD_DIM], part
            )
        outs.extend(part[i * ROWS_DEV : (i + 1) * ROWS_DEV] for i in range(group))
    o_ref[...] = jnp.concatenate(outs, axis=1).astype(BF16)


def exchange(x):
    return lax.all_to_all(x, "wide", split_axis=0, concat_axis=0, tiled=True)


def partner(x, mask):
    return lax.ppermute(x, "wide", [(i, i ^ mask) for i in range(lax.axis_size("wide"))])


def per_device(
    tokens,
    query_output_gradient,
    down_factors,
    up_factors_transposed,
    tenant_of_block,
    device_tenant_list,
    row_list_entry,
    hidden,
    base_query_rows,
    cached_key_rows,
    cached_value_rows,
    live_cache_length,
):
    n = lax.axis_size("wide")
    me = lax.axis_index("wide").astype(jnp.int32)
    small = n == 16
    fa, cols = down_factors.shape
    fb = up_factors_transposed.shape[0]
    local_rows = hidden.shape[0]
    rows = local_rows * n
    quarter = rows // PER_TILE
    width = tokens.shape[1]
    features = query_output_gradient.shape[1]
    assert tokens.shape[0] == BLOCK and tenant_of_block.shape[0] == n

    shape = (n, HALF, 2 * (fa + fb))
    chunks = 4 if fa % 64 == 0 and fb % 64 == 0 else 1
    packed = call(
        pick_kernel,
        jax.ShapeDtypeStruct(shape, BF16),
        [hbm(), hbm(), hbm()],
        hbm(),
        scratch=[
            pltpu.VMEM(up_factors_transposed.shape, BF16),
            pltpu.VMEM(down_factors.shape, BF16),
            pltpu.VMEM(shape, BF16),
            pltpu.SMEM((n,), jnp.int32),
            pltpu.SemaphoreType.DMA,
            pltpu.SemaphoreType.DMA((chunks,)),
            pltpu.SemaphoreType.DMA((chunks,)),
            pltpu.SemaphoreType.DMA((n,)),
        ],
        flops=2 * RANK * LANES * n * (fa + fb),
        nbytes=2 * cols * (fa + fb),
        limit=ALL_VMEM,
    )(tenant_of_block, up_factors_transposed, down_factors)

    if small:
        held = call(
            rows_pack_kernel,
            jax.ShapeDtypeStruct((HALF, width // CHUNKS + LANES), BF16),
            [smem(), smem(), vmem()],
            vmem(),
            nbytes=4 * local_rows * width,
            limit=ALL_VMEM,
        )(device_tenant_list, row_list_entry, hidden)[None]
        held = jnp.concatenate([held, partner(held, n // 2)], axis=0)
        held, packed = lax.optimization_barrier((held, packed))
        got = exchange(packed)
        masks = [0, n // 2]
        bit = n // 4
        while bit > 1:
            held = lax.optimization_barrier(jnp.concatenate([held, partner(held, bit)], axis=0))
            masks = masks + [m ^ bit for m in masks]
            bit //= 2
        masks = masks + [m ^ 1 for m in masks]
        found = call(
            rows_kernel,
            [jax.ShapeDtypeStruct((n, local_rows, LANES), t) for t in (F32, F32, jnp.int32)],
            [smem()] + [vmem()] * 4,
            [vmem()] * 3,
            scratch=[pltpu.VMEM((n * HALF, fa), BF16)],
            flops=8 * rows * (BLOCK * width + fa * cols),
            nbytes=2 * BLOCK * width + 2 * fa * cols,
        )(me[None], held, partner(held, 1), tokens, down_factors)
        hx, base_low_rank, tenants = ((f,) for f in found)
    else:
        got = exchange(packed)
        slot = row_list_entry[:, None] == jnp.arange(device_tenant_list.shape[1], dtype=jnp.int32)[None, :]
        row_tenant = jnp.sum(jnp.where(slot, device_tenant_list, 0), axis=1)
        everyone = lax.all_gather(hidden, "wide", axis=0, tiled=True)
        tenants = lax.all_gather(row_tenant, "wide", axis=0, tiled=True)
        tenants = jnp.broadcast_to(tenants[:, None], (rows, LANES))
        hx, base_low_rank = call(
            plain_rows_kernel,
            [jax.ShapeDtypeStruct((n, local_rows, LANES), F32)] * 2,
            [vmem()] * 5,
            [vmem()] * 2,
        )(everyone, tokens, down_factors, lax.dynamic_slice(everyone, (0, me * fa), (rows, fa)), tenants)

    if not small:
        masks, hx, base_low_rank = None, (hx,), (base_low_rank,)
        tenants = (tenants.reshape(n, local_rows, LANES),)
    part_shape = (n, HALF, 2 * (fa + fb) + (LANES if small else 0))
    my_tenant = lax.dynamic_slice(tenant_of_block, (me,), (1,))
    parts, tenants, *low_rank = call(
        functools.partial(block_kernel, small, masks),
        [jax.ShapeDtypeStruct(part_shape, BF16), jax.ShapeDtypeStruct((rows, LANES), jnp.int32)]
        + ([] if small else [jax.ShapeDtypeStruct((quarter, LANES), F32)]),
        [smem(), smem()] + [vmem()] * (3 + 3 * len(hx)),
        [vmem()] * (2 if small else 3),
        scratch=[pltpu.VMEM((RANK, width), BF16), pltpu.VMEM((RANK, features), BF16)]
        + [pltpu.VMEM((n, local_rows, LANES), t) for t in (F32, F32, jnp.int32)],
        flops=4 * RANK * BLOCK * n * (fa + fb),
        nbytes=2 * BLOCK * n * (fa + fb),
    )(my_tenant, me[None], tokens, query_output_gradient, got, *hx, *base_low_rank, *tenants)
    low_rank = [lax.psum(p, "wide") for p in low_rank]
    parts = exchange(parts)

    delta = call(
        functools.partial(delta_kernel, fa),
        jax.ShapeDtypeStruct((n, local_rows, fb), F32),
        [smem()] + [vmem()] * (3 + len(low_rank)),
        vmem(),
        flops=2 * rows * cols * fb,
        nbytes=2 * cols * fb,
    )(tenant_of_block, parts, up_factors_transposed, tenants, *low_rank)
    delta = exchange(delta)

    down_gradient, up_gradient = call(
        gradient_kernel,
        [jax.ShapeDtypeStruct((fa, cols), F32), jax.ShapeDtypeStruct((fb, cols), F32)],
        [smem(), vmem()],
        [vmem()] * 2,
        flops=2 * n * RANK * (fa + fb) * LANES,
        nbytes=4 * cols * (fa + fb),
    )(tenant_of_block, parts)
    attended = call(
        attention_kernel,
        jax.ShapeDtypeStruct((local_rows, HEADS * HEAD_DIM), BF16),
        [smem(), vmem(), vmem(), vmem(), vmem()],
        vmem(),
        flops=4 * HEADS * local_rows * cached_key_rows.shape[1] * HEAD_DIM,
        nbytes=4 * cached_key_rows.size,
    )(live_cache_length, delta, base_query_rows.astype(F32), cached_key_rows, cached_value_rows)
    return down_gradient, up_gradient, attended


def solution(mesh):
    placed = (
        P(("groups", "wide"), None),
        P(("groups", "wide"), None),
        P("wide", "groups"),
        P("wide", "groups"),
        P("groups"),
        P(("groups", "wide"), None),
        P(("groups", "wide")),
        P(("groups", "wide"), None),
        P(("groups", "wide"), None),
        P(("groups", "wide"), None, None),
        P(("groups", "wide"), None, None),
        P(("groups", "wide")),
    )
    return jax.shard_map(
        per_device,
        mesh=mesh,
        in_specs=placed,
        out_specs=(P("wide", "groups"), P("wide", "groups"), P(("groups", "wide"), None)),
        check_vma=False,
    )
```

```python
import functools

import jax
import jax.numpy as jnp
from jax import lax
from jax.experimental import pallas as pl
from jax.experimental.pallas import tpu as pltpu
from jax.sharding import PartitionSpec as P

HEAD_DIM = 128
HEADS = 32
KV_HEADS = 4
RANK = 32
TENANTS = 64
BLOCK = 128
ROWS_DEV = 4
LANES = 128
PER_TILE = LANES // RANK

adapter_scale = 2.0
learning_rate = 0.0002

F32 = jnp.float32
BF16 = jnp.bfloat16
VMEM_LIMIT = 24 * 1024 * 1024
ALL_VMEM = 58 * 1024 * 1024 + 768 * 1024
ROWS_VMEM = 57 * 1024 * 1024 + 256 * 1024


def vmem():
    return pl.BlockSpec(memory_space=pltpu.VMEM)


def smem():
    return pl.BlockSpec(memory_space=pltpu.SMEM)


def hbm():
    return pl.BlockSpec(memory_space=pltpu.HBM)


def call(kernel, out_shape, in_specs, out_specs, scratch=(), flops=0, nbytes=0, limit=VMEM_LIMIT):
    return pl.pallas_call(
        kernel,
        out_shape=out_shape,
        in_specs=in_specs,
        out_specs=out_specs,
        scratch_shapes=list(scratch),
        compiler_params=pltpu.CompilerParams(vmem_limit_bytes=limit),
        cost_estimate=pl.CostEstimate(flops=flops, bytes_accessed=nbytes, transcendentals=0),
    )


def each(count, body):
    if count <= 16:
        for j in range(count):
            body(j)
    else:
        pl.loop(0, count)(body)


def dot(a, b, ca, cb):
    return lax.dot_general(a, b, (((ca,), (cb,)), ((), ())), preferred_element_type=F32)


def quarter_indicator(quarter, value):
    lane = lax.broadcasted_iota(jnp.int32, (RANK, LANES), 1)
    row = lax.broadcasted_iota(jnp.int32, (RANK, LANES), 0)
    return jnp.where(lane - row == quarter * RANK, value, 0.0).astype(BF16)


def tile_of(tenant):
    return pl.ds(pl.multiple_of((tenant // PER_TILE) * LANES, LANES), LANES)


HALF = RANK // 2
CHUNKS = HALF // ROWS_DEV


def up_half(h, fa, fb):
    return slice(h * fb, (h + 1) * fb)


def down_half(h, fa, fb):
    return slice(2 * fb + h * fa, 2 * fb + (h + 1) * fa)


def pick_kernel(tenant_ref, b_ref, a_ref, o_ref, b_tab, a_tab, o_buf, t_ref, sem_t, sem_b, sem_a, sem_o):
    n = t_ref.shape[0]
    fa, fb = a_ref.shape[0], b_ref.shape[0]

    def loads(src, dst, sem):
        step = src.shape[0] // sem.shape[0]
        parts = [slice(c * step, (c + 1) * step) for c in range(sem.shape[0])]
        return [pltpu.make_async_copy(src.at[r], dst.at[r], sem.at[c]) for c, r in enumerate(parts)]

    first, second = loads(b_ref, b_tab, sem_b), loads(a_ref, a_tab, sem_a)
    tenants = pltpu.make_async_copy(tenant_ref, t_ref, sem_t)
    for load in [tenants] + first + second:
        load.start()

    def picked(j, table):
        t = t_ref[j]
        return dot(quarter_indicator(t % PER_TILE, 1.0), table[:, tile_of(t)], 1, 1).astype(BF16)

    def up_body(j):
        up = picked(j, b_tab)
        for h in range(2):
            o_buf[j, :, up_half(h, fa, fb)] = up[h * HALF : (h + 1) * HALF]

    def down_body(j):
        down = picked(j, a_tab)
        for h in range(2):
            o_buf[j, :, down_half(h, fa, fb)] = down[h * HALF : (h + 1) * HALF]
        pltpu.make_async_copy(o_buf.at[j], o_ref.at[j], sem_o.at[j]).start()

    def finish(j):
        pltpu.make_async_copy(o_buf.at[j], o_ref.at[j], sem_o.at[j]).wait()

    for load in [tenants] + first:
        load.wait()
    each(n, up_body)
    for load in second:
        load.wait()
    each(n, down_body)
    each(n, finish)


def rows_pack_kernel(list_ref, slot_ref, hidden_ref, o_ref):
    hidden = hidden_ref[...].astype(F32)
    size = hidden.shape[1] // CHUNKS
    main = jnp.concatenate([hidden[:, p * size : (p + 1) * size] for p in range(CHUNKS)], axis=0)
    row = lax.broadcasted_iota(jnp.int32, (HALF, LANES), 0) % ROWS_DEV
    mark = jnp.zeros((HALF, LANES), jnp.int32)
    for r in range(ROWS_DEV):
        mark = jnp.where(row == r, list_ref[0, slot_ref[r]], mark)
    o_ref[...] = jnp.concatenate([main, mark.astype(F32)], axis=1).astype(BF16)


def fold_rows(product, tenant):
    rows = product.shape[0]
    lane = lax.broadcasted_iota(jnp.int32, (rows, LANES), 1)
    total = jnp.zeros((rows, LANES), F32)
    for c in range(TENANTS // PER_TILE):
        mine = tenant == c * PER_TILE + lane // RANK
        total = total + jnp.where(mine, product[:, c * LANES : (c + 1) * LANES], 0.0)
    half = total + pltpu.roll(total, 2 * RANK, 1)
    return half + pltpu.roll(half, RANK, 1)


def rows_kernel(me_ref, h0_ref, h1_ref, x_ref, a_ref, g_ref, hx_ref, base_ref, u_ref, g_out, sel, sem):
    copy = pltpu.make_async_copy(g_ref, g_out, sem)
    copy.start()
    h = jnp.concatenate([r[k] for r in (h0_ref, h1_ref) for k in range(r.shape[0])], axis=0)
    tiles = h.shape[0] // HALF
    size = h.shape[1] - LANES
    fa = a_ref.shape[0]

    def group(value, p):
        first = [k * HALF + p * ROWS_DEV for k in range(tiles)]
        return jnp.concatenate([value[f : f + ROWS_DEV] for f in first], axis=0)

    per_chunk = size // fa
    for m in range(per_chunk):

        @pl.when(me_ref[0] % per_chunk == m)
        def _():
            sel[...] = h[:, m * fa : (m + 1) * fa]

    wide = h.astype(F32)
    hx = jnp.zeros((tiles * ROWS_DEV, BLOCK), F32)
    for p in range(CHUNKS):
        chunk = group(wide[:, :size], p).astype(BF16)
        hx = hx + dot(chunk, x_ref[:, p * size : (p + 1) * size], 1, 1)
    tenant = group(wide[:, size:], 0).astype(jnp.int32)
    mine = sel[...].astype(F32)
    cols = group(mine, 0)
    for p in range(1, CHUNKS):
        cols = jnp.where(me_ref[0] // per_chunk == p, group(mine, p), cols)
    base = fold_rows(dot(cols.astype(BF16), a_ref[...], 1, 0), tenant)
    for k in range(tiles):
        rows = slice(k * ROWS_DEV, (k + 1) * ROWS_DEV)
        hx_ref[k], base_ref[k], u_ref[k] = hx[rows], base[rows], tenant[rows]
    copy.wait()


def plain_rows_kernel(h_ref, x_ref, a_ref, hc_ref, u_ref, hx_ref, base_ref):
    hx = dot(h_ref[...], x_ref[...], 1, 1)
    base = fold_rows(dot(hc_ref[...], a_ref[...], 1, 0), u_ref[...])
    for d in range(hx_ref.shape[0]):
        hx_ref[d] = hx[d * ROWS_DEV : (d + 1) * ROWS_DEV]
        base_ref[d] = base[d * ROWS_DEV : (d + 1) * ROWS_DEV]


def block_kernel(ride, masks, t_ref, me_ref, x_ref, g_ref, r_ref, *refs):
    sets = (len(refs) - (7 if ride else 8)) // 3
    hx_sets, base_sets, u_sets = (refs[i * sets : (i + 1) * sets] for i in range(3))
    o_ref, u_ref = refs[3 * sets : 3 * sets + 2]
    wa_ref, wb_ref, sx, sb, su = refs[-5:]
    n = r_ref.shape[0]
    fa, fb = x_ref.shape[1] // n, g_ref.shape[1] // n
    for d in range(n):
        for h in range(2):
            rank = slice(h * HALF, (h + 1) * HALF)
            wb_ref[rank, d * fb : (d + 1) * fb] = r_ref[d, :, up_half(h, fa, fb)]
            wa_ref[rank, d * fa : (d + 1) * fa] = r_ref[d, :, down_half(h, fa, fb)]
    back = dot(wb_ref[...], g_ref[...], 1, 1).astype(BF16)
    down = dot(wa_ref[...], x_ref[...], 1, 1).astype(BF16)

    k = 0
    for hx_ref, base_ref, tile_ref in zip(hx_sets, base_sets, u_sets):
        for i in range(hx_ref.shape[0]):
            d = me_ref[0] ^ masks[k] if masks else i
            sx[d], sb[d], su[d] = hx_ref[i], base_ref[i], tile_ref[i]
            k += 1
    hx, base, tenant = (jnp.concatenate([v[d] for d in range(n)], axis=0) for v in (sx, sb, su))
    u_ref[...] = tenant
    high = hx.astype(BF16)
    low = (hx - high.astype(F32)).astype(BF16)
    wide_back = jnp.concatenate([back] * PER_TILE, axis=0)
    change = dot(high, wide_back, 1, 1) + dot(low, wide_back, 1, 1)
    mine = tenant == t_ref[0]
    full = base - jnp.where(mine, learning_rate * (adapter_scale * change), 0.0)
    quarter = full.shape[0] // PER_TILE
    spot = lax.broadcasted_iota(jnp.int32, (quarter, LANES), 1) // RANK
    packed = jnp.zeros((quarter, LANES), F32)
    for q in range(PER_TILE):
        packed = packed + jnp.where(spot == q, full[q * quarter : (q + 1) * quarter], 0.0)
    if not ride:
        refs[3 * sets + 2][...] = packed

    down_part = dot(back, x_ref[...], 1, 0).astype(BF16)
    up_part = dot(down, g_ref[...], 1, 0).astype(BF16)
    for d in range(n):
        for h in range(2):
            rank = slice(h * HALF, (h + 1) * HALF)
            o_ref[d, :, up_half(h, fa, fb)] = up_part[rank, d * fb : (d + 1) * fb]
            o_ref[d, :, down_half(h, fa, fb)] = down_part[rank, d * fa : (d + 1) * fa]
        if ride:
            o_ref[d, :, 2 * (fa + fb) :] = packed.astype(BF16)


def sum_by_tenant(t_ref, part_ref, cut, fa, fb, grad_ref):
    grad_ref[...] = jnp.zeros_like(grad_ref)

    def body(j):
        t = t_ref[j]
        part = jnp.concatenate([part_ref[j, :, cut(h, fa, fb)] for h in range(2)], axis=0)
        place = quarter_indicator(t % PER_TILE, adapter_scale)
        grad_ref[:, tile_of(t)] += dot(part, place, 0, 0)

    each(t_ref.shape[0], body)


def gradient_kernel(t_ref, part_ref, down_ref, up_ref):
    fa, fb = down_ref.shape[0], up_ref.shape[0]
    sum_by_tenant(t_ref, part_ref, down_half, fa, fb, down_ref)
    sum_by_tenant(t_ref, part_ref, up_half, fa, fb, up_ref)


def delta_kernel(fa, t_ref, part_ref, b_ref, u_ref, *refs):
    o_ref = refs[-1]
    n, fb = part_ref.shape[0], b_ref.shape[0]
    if len(refs) == 2:
        total = refs[0][...]
    else:
        total = part_ref[0, :, 2 * (fa + fb) :].astype(F32)
        for d in range(1, n):
            total = total + part_ref[d, :, 2 * (fa + fb) :].astype(F32)
    spot = lax.broadcasted_iota(jnp.int32, total.shape, 1) // RANK
    pieces = []
    for q in range(PER_TILE):
        one = jnp.where(spot == q, total, 0.0)
        half = one + pltpu.roll(one, 2 * RANK, 1)
        pieces.append(half + pltpu.roll(half, RANK, 1))
    adapted = jnp.concatenate(pieces, axis=0)
    quarter = lax.broadcasted_iota(jnp.int32, adapted.shape, 1) // RANK
    tenant = u_ref[...]
    spread = [
        jnp.where(tenant == c * PER_TILE + quarter, adapted, 0.0).astype(BF16) for c in range(TENANTS // PER_TILE)
    ]
    old = dot(jnp.concatenate(spread, axis=1), b_ref[...], 1, 1)
    matched = []
    for c in range(n // PER_TILE):
        block = jnp.zeros(adapted.shape, jnp.int32)
        for i in range(PER_TILE):
            block = jnp.where(quarter == i, t_ref[c * PER_TILE + i], block)
        matched.append(jnp.where(tenant == block, adapted, 0.0).astype(BF16))
    up = [part_ref[j, :, up_half(h, fa, fb)] for j in range(n) for h in range(2)]
    change = dot(jnp.concatenate(matched, axis=1), jnp.concatenate(up, axis=0), 1, 0)
    delta = adapter_scale * (old - learning_rate * (adapter_scale * change))
    for d in range(n):
        o_ref[d] = delta[d * ROWS_DEV : (d + 1) * ROWS_DEV]


def attention_kernel(len_ref, delta_ref, base_ref, k_ref, v_ref, o_ref):
    n = delta_ref.shape[0]
    delta = jnp.concatenate([delta_ref[d] for d in range(n)], axis=1)
    query = (base_ref[...] + delta).astype(BF16).astype(F32)
    group = HEADS // KV_HEADS
    cache = k_ref.shape[1]
    many = HEADS * ROWS_DEV
    empty = jnp.zeros((group * ROWS_DEV, HEAD_DIM), F32)
    heads = []
    for g in range(KV_HEADS):
        mine = [query[:, h * HEAD_DIM : (h + 1) * HEAD_DIM] for h in range(g * group, (g + 1) * group)]
        lanes = [empty] * KV_HEADS
        lanes[g] = jnp.concatenate(mine, axis=0)
        heads.append(jnp.concatenate(lanes, axis=1))
    heads = jnp.concatenate(heads, axis=0).astype(BF16)
    row = lax.broadcasted_iota(jnp.int32, (many, cache), 0) % ROWS_DEV
    length = jnp.zeros((many, cache), jnp.int32)
    scores = jnp.zeros((many, cache), F32)
    for r in range(ROWS_DEV):
        length = jnp.where(row == r, len_ref[r], length)
        scores = jnp.where(row == r, dot(heads, k_ref[r], 1, 1), scores)
    live = lax.broadcasted_iota(jnp.int32, (many, cache), 1) < length
    scores = jnp.where(live, scores / jnp.sqrt(F32(HEAD_DIM)), F32(-1e30))
    top = jnp.max(scores, axis=-1, keepdims=True)
    expo = jnp.where(live, jnp.exp(scores - top), 0.0)
    weights = (expo / jnp.sum(expo, axis=-1, keepdims=True)).astype(BF16)
    mixed = [dot(weights, v_ref[r], 1, 0) for r in range(ROWS_DEV)]
    outs = []
    rows = group * ROWS_DEV
    row = lax.broadcasted_iota(jnp.int32, (rows, HEAD_DIM), 0) % ROWS_DEV
    for g in range(KV_HEADS):
        part = jnp.zeros((rows, HEAD_DIM), F32)
        for r in range(ROWS_DEV):
            part = jnp.where(
                row == r, mixed[r][g * rows : (g + 1) * rows, g * HEAD_DIM : (g + 1) * HEAD_DIM], part
            )
        outs.extend(part[i * ROWS_DEV : (i + 1) * ROWS_DEV] for i in range(group))
    o_ref[...] = jnp.concatenate(outs, axis=1).astype(BF16)


def exchange(x):
    return lax.all_to_all(x, "wide", split_axis=0, concat_axis=0, tiled=True)


def partner(x, mask):
    return lax.ppermute(x, "wide", [(i, i ^ mask) for i in range(lax.axis_size("wide"))])


def per_device(
    tokens,
    query_output_gradient,
    down_factors,
    up_factors_transposed,
    tenant_of_block,
    device_tenant_list,
    row_list_entry,
    hidden,
    base_query_rows,
    cached_key_rows,
    cached_value_rows,
    live_cache_length,
):
    n = lax.axis_size("wide")
    me = lax.axis_index("wide").astype(jnp.int32)
    small = n == 16
    fa, cols = down_factors.shape
    fb = up_factors_transposed.shape[0]
    local_rows = hidden.shape[0]
    rows = local_rows * n
    quarter = rows // PER_TILE
    width = tokens.shape[1]
    features = query_output_gradient.shape[1]
    assert tokens.shape[0] == BLOCK and tenant_of_block.shape[0] == n

    shape = (n, HALF, 2 * (fa + fb))
    chunks = 4 if fa % 64 == 0 and fb % 64 == 0 else 1
    packed = call(
        pick_kernel,
        jax.ShapeDtypeStruct(shape, BF16),
        [hbm(), hbm(), hbm()],
        hbm(),
        scratch=[
            pltpu.VMEM(up_factors_transposed.shape, BF16),
            pltpu.VMEM(down_factors.shape, BF16),
            pltpu.VMEM(shape, BF16),
            pltpu.SMEM((n,), jnp.int32),
            pltpu.SemaphoreType.DMA,
            pltpu.SemaphoreType.DMA((chunks,)),
            pltpu.SemaphoreType.DMA((chunks,)),
            pltpu.SemaphoreType.DMA((n,)),
        ],
        flops=2 * RANK * LANES * n * (fa + fb),
        nbytes=2 * cols * (fa + fb),
        limit=ALL_VMEM,
    )(tenant_of_block, up_factors_transposed, down_factors)

    if small:
        held = call(
            rows_pack_kernel,
            jax.ShapeDtypeStruct((HALF, width // CHUNKS + LANES), BF16),
            [smem(), smem(), vmem()],
            vmem(),
            nbytes=4 * local_rows * width,
            limit=ALL_VMEM,
        )(device_tenant_list, row_list_entry, hidden)[None]
        held = jnp.concatenate([held, partner(held, n // 2)], axis=0)
        held, packed = lax.optimization_barrier((held, packed))
        got = exchange(packed)
        masks = [0, n // 2]
        bit = n // 4
        while bit > 1:
            held = lax.optimization_barrier(jnp.concatenate([held, partner(held, bit)], axis=0))
            masks = masks + [m ^ bit for m in masks]
            bit //= 2
        masks = masks + [m ^ 1 for m in masks]
        *found, query_output_gradient = call(
            rows_kernel,
            [jax.ShapeDtypeStruct((n, local_rows, LANES), t) for t in (F32, F32, jnp.int32)]
            + [jax.ShapeDtypeStruct(query_output_gradient.shape, BF16)],
            [smem()] + [vmem()] * 4 + [hbm()],
            [vmem()] * 4,
            scratch=[pltpu.VMEM((n * HALF, fa), BF16), pltpu.SemaphoreType.DMA],
            limit=ROWS_VMEM,
            flops=2 * rows * (BLOCK * width + fa * cols),
            nbytes=2 * BLOCK * width + 2 * fa * cols,
        )(me[None], held, partner(held, 1), tokens, down_factors, query_output_gradient)
        hx, base_low_rank, tenants = ((f,) for f in found)
    else:
        got = exchange(packed)
        slot = row_list_entry[:, None] == jnp.arange(device_tenant_list.shape[1], dtype=jnp.int32)[None, :]
        row_tenant = jnp.sum(jnp.where(slot, device_tenant_list, 0), axis=1)
        everyone = lax.all_gather(hidden, "wide", axis=0, tiled=True)
        tenants = lax.all_gather(row_tenant, "wide", axis=0, tiled=True)
        tenants = jnp.broadcast_to(tenants[:, None], (rows, LANES))
        hx, base_low_rank = call(
            plain_rows_kernel,
            [jax.ShapeDtypeStruct((n, local_rows, LANES), F32)] * 2,
            [vmem()] * 5,
            [vmem()] * 2,
        )(everyone, tokens, down_factors, lax.dynamic_slice(everyone, (0, me * fa), (rows, fa)), tenants)

    if not small:
        masks, hx, base_low_rank = None, (hx,), (base_low_rank,)
        tenants = (tenants.reshape(n, local_rows, LANES),)
    part_shape = (n, HALF, 2 * (fa + fb) + (LANES if small else 0))
    my_tenant = lax.dynamic_slice(tenant_of_block, (me,), (1,))
    parts, tenants, *low_rank = call(
        functools.partial(block_kernel, small, masks),
        [jax.ShapeDtypeStruct(part_shape, BF16), jax.ShapeDtypeStruct((rows, LANES), jnp.int32)]
        + ([] if small else [jax.ShapeDtypeStruct((quarter, LANES), F32)]),
        [smem(), smem()] + [vmem()] * (3 + 3 * len(hx)),
        [vmem()] * (2 if small else 3),
        scratch=[pltpu.VMEM((RANK, width), BF16), pltpu.VMEM((RANK, features), BF16)]
        + [pltpu.VMEM((n, local_rows, LANES), t) for t in (F32, F32, jnp.int32)],
        flops=4 * RANK * BLOCK * n * (fa + fb),
        nbytes=2 * BLOCK * n * (fa + fb),
    )(my_tenant, me[None], tokens, query_output_gradient, got, *hx, *base_low_rank, *tenants)
    low_rank = [lax.psum(p, "wide") for p in low_rank]
    parts = exchange(parts)

    delta = call(
        functools.partial(delta_kernel, fa),
        jax.ShapeDtypeStruct((n, local_rows, fb), F32),
        [smem()] + [vmem()] * (3 + len(low_rank)),
        vmem(),
        flops=2 * rows * cols * fb,
        nbytes=2 * cols * fb,
    )(tenant_of_block, parts, up_factors_transposed, tenants, *low_rank)
    delta = exchange(delta)

    down_gradient, up_gradient = call(
        gradient_kernel,
        [jax.ShapeDtypeStruct((fa, cols), F32), jax.ShapeDtypeStruct((fb, cols), F32)],
        [smem(), vmem()],
        [vmem()] * 2,
        flops=2 * n * RANK * (fa + fb) * LANES,
        nbytes=4 * cols * (fa + fb),
    )(tenant_of_block, parts)
    attended = call(
        attention_kernel,
        jax.ShapeDtypeStruct((local_rows, HEADS * HEAD_DIM), BF16),
        [smem(), vmem(), vmem(), vmem(), vmem()],
        vmem(),
        flops=4 * HEADS * local_rows * cached_key_rows.shape[1] * HEAD_DIM,
        nbytes=4 * cached_key_rows.size,
    )(live_cache_length, delta, base_query_rows.astype(F32), cached_key_rows, cached_value_rows)
    return down_gradient, up_gradient, attended


def solution(mesh):
    placed = (
        P(("groups", "wide"), None),
        P(("groups", "wide"), None),
        P("wide", "groups"),
        P("wide", "groups"),
        P("groups"),
        P(("groups", "wide"), None),
        P(("groups", "wide")),
        P(("groups", "wide"), None),
        P(("groups", "wide"), None),
        P(("groups", "wide"), None, None),
        P(("groups", "wide"), None, None),
        P(("groups", "wide")),
    )
    return jax.shard_map(
        per_device,
        mesh=mesh,
        in_specs=placed,
        out_specs=(P("wide", "groups"), P("wide", "groups"), P(("groups", "wide"), None)),
        check_vma=False,
    )
```

```python
import functools

import jax
import jax.numpy as jnp
from jax import lax
from jax.experimental import pallas as pl
from jax.experimental.pallas import tpu as pltpu
from jax.sharding import PartitionSpec as P

HEAD_DIM = 128
HEADS = 32
KV_HEADS = 4
RANK = 32
TENANTS = 64
BLOCK = 128
ROWS_DEV = 4
LANES = 128
PER_TILE = LANES // RANK

adapter_scale = 2.0
learning_rate = 0.0002

F32 = jnp.float32
BF16 = jnp.bfloat16
VMEM_LIMIT = 24 * 1024 * 1024
ALL_VMEM = 58 * 1024 * 1024 + 768 * 1024


def vmem():
    return pl.BlockSpec(memory_space=pltpu.VMEM)


def smem():
    return pl.BlockSpec(memory_space=pltpu.SMEM)


def hbm():
    return pl.BlockSpec(memory_space=pltpu.HBM)


def call(kernel, out_shape, in_specs, out_specs, scratch=(), flops=0, nbytes=0, limit=VMEM_LIMIT):
    return pl.pallas_call(
        kernel,
        out_shape=out_shape,
        in_specs=in_specs,
        out_specs=out_specs,
        scratch_shapes=list(scratch),
        compiler_params=pltpu.CompilerParams(vmem_limit_bytes=limit),
        cost_estimate=pl.CostEstimate(flops=flops, bytes_accessed=nbytes, transcendentals=0),
    )


def each(count, body):
    if count <= 16:
        for j in range(count):
            body(j)
    else:
        pl.loop(0, count)(body)


def dot(a, b, ca, cb):
    return lax.dot_general(a, b, (((ca,), (cb,)), ((), ())), preferred_element_type=F32)


def quarter_indicator(quarter, value):
    lane = lax.broadcasted_iota(jnp.int32, (RANK, LANES), 1)
    row = lax.broadcasted_iota(jnp.int32, (RANK, LANES), 0)
    return jnp.where(lane - row == quarter * RANK, value, 0.0).astype(BF16)


def tile_of(tenant):
    return pl.ds(pl.multiple_of((tenant // PER_TILE) * LANES, LANES), LANES)


HALF = RANK // 2
CHUNKS = HALF // ROWS_DEV


def up_half(h, fa, fb):
    return slice(h * fb, (h + 1) * fb)


def down_half(h, fa, fb):
    return slice(2 * fb + h * fa, 2 * fb + (h + 1) * fa)


def pick_kernel(tenant_ref, b_ref, a_ref, o_ref, b_tab, a_tab, o_buf, t_ref, sem_t, sem_b, sem_a, sem_o):
    n = t_ref.shape[0]
    fa, fb = a_ref.shape[0], b_ref.shape[0]

    def loads(src, dst, sem):
        step = src.shape[0] // sem.shape[0]
        parts = [slice(c * step, (c + 1) * step) for c in range(sem.shape[0])]
        return [pltpu.make_async_copy(src.at[r], dst.at[r], sem.at[c]) for c, r in enumerate(parts)]

    first, second = loads(b_ref, b_tab, sem_b), loads(a_ref, a_tab, sem_a)
    tenants = pltpu.make_async_copy(tenant_ref, t_ref, sem_t)
    for load in [tenants] + first + second:
        load.start()

    def picked(j, table):
        t = t_ref[j]
        return dot(quarter_indicator(t % PER_TILE, 1.0), table[:, tile_of(t)], 1, 1).astype(BF16)

    def up_body(j):
        up = picked(j, b_tab)
        for h in range(2):
            o_buf[j, :, up_half(h, fa, fb)] = up[h * HALF : (h + 1) * HALF]

    def down_body(j):
        down = picked(j, a_tab)
        for h in range(2):
            o_buf[j, :, down_half(h, fa, fb)] = down[h * HALF : (h + 1) * HALF]
        pltpu.make_async_copy(o_buf.at[j], o_ref.at[j], sem_o.at[j]).start()

    def finish(j):
        pltpu.make_async_copy(o_buf.at[j], o_ref.at[j], sem_o.at[j]).wait()

    for load in [tenants] + first:
        load.wait()
    each(n, up_body)
    for load in second:
        load.wait()
    each(n, down_body)
    each(n, finish)


def rows_pack_kernel(list_ref, slot_ref, hidden_ref, o_ref):
    hidden = hidden_ref[...].astype(F32)
    size = hidden.shape[1] // CHUNKS
    main = jnp.concatenate([hidden[:, p * size : (p + 1) * size] for p in range(CHUNKS)], axis=0)
    row = lax.broadcasted_iota(jnp.int32, (HALF, LANES), 0) % ROWS_DEV
    mark = jnp.zeros((HALF, LANES), jnp.int32)
    for r in range(ROWS_DEV):
        mark = jnp.where(row == r, list_ref[0, slot_ref[r]], mark)
    o_ref[...] = jnp.concatenate([main, mark.astype(F32)], axis=1).astype(BF16)


def fold_rows(product, tenant):
    rows = product.shape[0]
    lane = lax.broadcasted_iota(jnp.int32, (rows, LANES), 1)
    total = jnp.zeros((rows, LANES), F32)
    for c in range(TENANTS // PER_TILE):
        mine = tenant == c * PER_TILE + lane // RANK
        total = total + jnp.where(mine, product[:, c * LANES : (c + 1) * LANES], 0.0)
    half = total + pltpu.roll(total, 2 * RANK, 1)
    return half + pltpu.roll(half, RANK, 1)


def rows_kernel(me_ref, h0_ref, h1_ref, x_ref, a_ref, hx_ref, base_ref, u_ref, sel):
    h = jnp.concatenate([r[k] for r in (h0_ref, h1_ref) for k in range(r.shape[0])], axis=0)
    tiles = h.shape[0] // HALF
    size = h.shape[1] - LANES
    fa = a_ref.shape[0]

    def group(value, p):
        first = [k * HALF + p * ROWS_DEV for k in range(tiles)]
        return jnp.concatenate([value[f : f + ROWS_DEV] for f in first], axis=0)

    per_chunk = size // fa
    for m in range(per_chunk):

        @pl.when(me_ref[0] % per_chunk == m)
        def _():
            sel[...] = h[:, m * fa : (m + 1) * fa]

    wide = h.astype(F32)
    hx = jnp.zeros((tiles * ROWS_DEV, BLOCK), F32)
    for p in range(CHUNKS):
        chunk = group(wide[:, :size], p).astype(BF16)
        hx = hx + dot(chunk, x_ref[:, p * size : (p + 1) * size], 1, 1)
    tenant = group(wide[:, size:], 0).astype(jnp.int32)
    mine = sel[...].astype(F32)
    cols = group(mine, 0)
    for p in range(1, CHUNKS):
        cols = jnp.where(me_ref[0] // per_chunk == p, group(mine, p), cols)
    base = fold_rows(dot(cols.astype(BF16), a_ref[...], 1, 0), tenant)
    for k in range(tiles):
        rows = slice(k * ROWS_DEV, (k + 1) * ROWS_DEV)
        hx_ref[k], base_ref[k], u_ref[k] = hx[rows], base[rows], tenant[rows]


def plain_rows_kernel(h_ref, x_ref, a_ref, hc_ref, u_ref, hx_ref, base_ref):
    hx = dot(h_ref[...], x_ref[...], 1, 1)
    base = fold_rows(dot(hc_ref[...], a_ref[...], 1, 0), u_ref[...])
    for d in range(hx_ref.shape[0]):
        hx_ref[d] = hx[d * ROWS_DEV : (d + 1) * ROWS_DEV]
        base_ref[d] = base[d * ROWS_DEV : (d + 1) * ROWS_DEV]


def block_kernel(ride, masks, t_ref, me_ref, x_ref, g_ref, r_ref, *refs):
    sets = (len(refs) - (7 if ride else 8)) // 3
    hx_sets, base_sets, u_sets = (refs[i * sets : (i + 1) * sets] for i in range(3))
    o_ref, u_ref = refs[3 * sets : 3 * sets + 2]
    wa_ref, wb_ref, sx, sb, su = refs[-5:]
    n = r_ref.shape[0]
    fa, fb = x_ref.shape[1] // n, g_ref.shape[1] // n
    for d in range(n):
        for h in range(2):
            rank = slice(h * HALF, (h + 1) * HALF)
            wb_ref[rank, d * fb : (d + 1) * fb] = r_ref[d, :, up_half(h, fa, fb)]
            wa_ref[rank, d * fa : (d + 1) * fa] = r_ref[d, :, down_half(h, fa, fb)]
    back = dot(wb_ref[...], g_ref[...], 1, 1).astype(BF16)
    down = dot(wa_ref[...], x_ref[...], 1, 1).astype(BF16)

    k = 0
    for hx_ref, base_ref, tile_ref in zip(hx_sets, base_sets, u_sets):
        for i in range(hx_ref.shape[0]):
            d = me_ref[0] ^ masks[k] if masks else i
            sx[d], sb[d], su[d] = hx_ref[i], base_ref[i], tile_ref[i]
            k += 1
    hx, base, tenant = (jnp.concatenate([v[d] for d in range(n)], axis=0) for v in (sx, sb, su))
    u_ref[...] = tenant
    high = hx.astype(BF16)
    low = (hx - high.astype(F32)).astype(BF16)
    wide_back = jnp.concatenate([back] * PER_TILE, axis=0)
    change = dot(high, wide_back, 1, 1) + dot(low, wide_back, 1, 1)
    mine = tenant == t_ref[0]
    full = base - jnp.where(mine, learning_rate * (adapter_scale * change), 0.0)
    quarter = full.shape[0] // PER_TILE
    spot = lax.broadcasted_iota(jnp.int32, (quarter, LANES), 1) // RANK
    packed = jnp.zeros((quarter, LANES), F32)
    for q in range(PER_TILE):
        packed = packed + jnp.where(spot == q, full[q * quarter : (q + 1) * quarter], 0.0)
    if not ride:
        refs[3 * sets + 2][...] = packed

    down_part = dot(back, x_ref[...], 1, 0).astype(BF16)
    up_part = dot(down, g_ref[...], 1, 0).astype(BF16)
    for d in range(n):
        for h in range(2):
            rank = slice(h * HALF, (h + 1) * HALF)
            o_ref[d, :, up_half(h, fa, fb)] = up_part[rank, d * fb : (d + 1) * fb]
            o_ref[d, :, down_half(h, fa, fb)] = down_part[rank, d * fa : (d + 1) * fa]
        if ride:
            o_ref[d, :, 2 * (fa + fb) :] = packed.astype(BF16)


def sum_by_tenant(t_ref, part_ref, cut, fa, fb, grad_ref):
    grad_ref[...] = jnp.zeros_like(grad_ref)

    def body(j):
        t = t_ref[j]
        part = jnp.concatenate([part_ref[j, :, cut(h, fa, fb)] for h in range(2)], axis=0)
        place = quarter_indicator(t % PER_TILE, adapter_scale)
        grad_ref[:, tile_of(t)] += dot(part, place, 0, 0)

    each(t_ref.shape[0], body)


def gradient_kernel(t_ref, part_ref, down_ref, up_ref):
    fa, fb = down_ref.shape[0], up_ref.shape[0]
    sum_by_tenant(t_ref, part_ref, down_half, fa, fb, down_ref)
    sum_by_tenant(t_ref, part_ref, up_half, fa, fb, up_ref)


def delta_kernel(fa, t_ref, part_ref, b_ref, u_ref, *refs):
    o_ref = refs[-1]
    n, fb = part_ref.shape[0], b_ref.shape[0]
    if len(refs) == 2:
        total = refs[0][...]
    else:
        total = part_ref[0, :, 2 * (fa + fb) :].astype(F32)
        for d in range(1, n):
            total = total + part_ref[d, :, 2 * (fa + fb) :].astype(F32)
    spot = lax.broadcasted_iota(jnp.int32, total.shape, 1) // RANK
    pieces = []
    for q in range(PER_TILE):
        one = jnp.where(spot == q, total, 0.0)
        half = one + pltpu.roll(one, 2 * RANK, 1)
        pieces.append(half + pltpu.roll(half, RANK, 1))
    adapted = jnp.concatenate(pieces, axis=0)
    quarter = lax.broadcasted_iota(jnp.int32, adapted.shape, 1) // RANK
    tenant = u_ref[...]
    spread = [
        jnp.where(tenant == c * PER_TILE + quarter, adapted, 0.0).astype(BF16) for c in range(TENANTS // PER_TILE)
    ]
    old = dot(jnp.concatenate(spread, axis=1), b_ref[...], 1, 1)
    matched = []
    for c in range(n // PER_TILE):
        block = jnp.zeros(adapted.shape, jnp.int32)
        for i in range(PER_TILE):
            block = jnp.where(quarter == i, t_ref[c * PER_TILE + i], block)
        matched.append(jnp.where(tenant == block, adapted, 0.0).astype(BF16))
    up = [part_ref[j, :, up_half(h, fa, fb)] for j in range(n) for h in range(2)]
    change = dot(jnp.concatenate(matched, axis=1), jnp.concatenate(up, axis=0), 1, 0)
    delta = adapter_scale * (old - learning_rate * (adapter_scale * change))
    for d in range(n):
        o_ref[d] = delta[d * ROWS_DEV : (d + 1) * ROWS_DEV]


def attention_kernel(len_ref, delta_ref, base_ref, k_ref, v_ref, o_ref):
    n = delta_ref.shape[0]
    delta = jnp.concatenate([delta_ref[d] for d in range(n)], axis=1)
    query = (base_ref[...] + delta).astype(BF16).astype(F32)
    group = HEADS // KV_HEADS
    cache = k_ref.shape[1]
    many = HEADS * ROWS_DEV
    empty = jnp.zeros((group * ROWS_DEV, HEAD_DIM), F32)
    heads = []
    for g in range(KV_HEADS):
        mine = [query[:, h * HEAD_DIM : (h + 1) * HEAD_DIM] for h in range(g * group, (g + 1) * group)]
        lanes = [empty] * KV_HEADS
        lanes[g] = jnp.concatenate(mine, axis=0)
        heads.append(jnp.concatenate(lanes, axis=1))
    heads = jnp.concatenate(heads, axis=0).astype(BF16)
    row = lax.broadcasted_iota(jnp.int32, (many, cache), 0) % ROWS_DEV
    length = jnp.zeros((many, cache), jnp.int32)
    scores = jnp.zeros((many, cache), F32)
    for r in range(ROWS_DEV):
        length = jnp.where(row == r, len_ref[r], length)
        scores = jnp.where(row == r, dot(heads, k_ref[r], 1, 1), scores)
    live = lax.broadcasted_iota(jnp.int32, (many, cache), 1) < length
    scores = jnp.where(live, scores / jnp.sqrt(F32(HEAD_DIM)), F32(-1e30))
    top = jnp.max(scores, axis=-1, keepdims=True)
    expo = jnp.where(live, jnp.exp(scores - top), 0.0)
    weights = (expo / jnp.sum(expo, axis=-1, keepdims=True)).astype(BF16)
    mixed = [dot(weights, v_ref[r], 1, 0) for r in range(ROWS_DEV)]
    outs = []
    rows = group * ROWS_DEV
    row = lax.broadcasted_iota(jnp.int32, (rows, HEAD_DIM), 0) % ROWS_DEV
    for g in range(KV_HEADS):
        part = jnp.zeros((rows, HEAD_DIM), F32)
        for r in range(ROWS_DEV):
            part = jnp.where(
                row == r, mixed[r][g * rows : (g + 1) * rows, g * HEAD_DIM : (g + 1) * HEAD_DIM], part
            )
        outs.extend(part[i * ROWS_DEV : (i + 1) * ROWS_DEV] for i in range(group))
    o_ref[...] = jnp.concatenate(outs, axis=1).astype(BF16)


def exchange(x):
    return lax.all_to_all(x, "wide", split_axis=0, concat_axis=0, tiled=True)


def partner(x, mask):
    return lax.ppermute(x, "wide", [(i, i ^ mask) for i in range(lax.axis_size("wide"))])


def per_device(
    tokens,
    query_output_gradient,
    down_factors,
    up_factors_transposed,
    tenant_of_block,
    device_tenant_list,
    row_list_entry,
    hidden,
    base_query_rows,
    cached_key_rows,
    cached_value_rows,
    live_cache_length,
):
    n = lax.axis_size("wide")
    me = lax.axis_index("wide").astype(jnp.int32)
    small = n == 16
    fa, cols = down_factors.shape
    fb = up_factors_transposed.shape[0]
    local_rows = hidden.shape[0]
    rows = local_rows * n
    quarter = rows // PER_TILE
    width = tokens.shape[1]
    features = query_output_gradient.shape[1]
    assert tokens.shape[0] == BLOCK and tenant_of_block.shape[0] == n

    shape = (n, HALF, 2 * (fa + fb))
    chunks = 4 if fa % 64 == 0 and fb % 64 == 0 else 1
    packed = call(
        pick_kernel,
        jax.ShapeDtypeStruct(shape, BF16),
        [hbm(), hbm(), hbm()],
        hbm(),
        scratch=[
            pltpu.VMEM(up_factors_transposed.shape, BF16),
            pltpu.VMEM(down_factors.shape, BF16),
            pltpu.VMEM(shape, BF16),
            pltpu.SMEM((n,), jnp.int32),
            pltpu.SemaphoreType.DMA,
            pltpu.SemaphoreType.DMA((chunks,)),
            pltpu.SemaphoreType.DMA((chunks,)),
            pltpu.SemaphoreType.DMA((n,)),
        ],
        flops=2 * RANK * LANES * n * (fa + fb),
        nbytes=2 * cols * (fa + fb),
        limit=ALL_VMEM,
    )(tenant_of_block, up_factors_transposed, down_factors)

    if small:
        held = call(
            rows_pack_kernel,
            jax.ShapeDtypeStruct((HALF, width // CHUNKS + LANES), BF16),
            [smem(), smem(), vmem()],
            vmem(),
            nbytes=4 * local_rows * width,
            limit=ALL_VMEM,
        )(device_tenant_list, row_list_entry, hidden)[None]
        held = jnp.concatenate([held, partner(held, n // 2)], axis=0)
        held, packed = lax.optimization_barrier((held, packed))
        got = exchange(packed)
        masks = [0, n // 2]
        bit = n // 4
        while bit > 1:
            held = lax.optimization_barrier(jnp.concatenate([held, partner(held, bit)], axis=0))
            masks = masks + [m ^ bit for m in masks]
            bit //= 2
        masks = masks + [m ^ 1 for m in masks]
        found = call(
            rows_kernel,
            [jax.ShapeDtypeStruct((n, local_rows, LANES), t) for t in (F32, F32, jnp.int32)],
            [smem()] + [vmem()] * 4,
            [vmem()] * 3,
            scratch=[pltpu.VMEM((n * HALF, fa), BF16)],
            flops=2 * rows * (BLOCK * width + fa * cols),
            nbytes=2 * BLOCK * width + 2 * fa * cols,
        )(me[None], held, partner(held, 1), tokens, down_factors)
        hx, base_low_rank, tenants = ((f,) for f in found)
    else:
        got = exchange(packed)
        slot = row_list_entry[:, None] == jnp.arange(device_tenant_list.shape[1], dtype=jnp.int32)[None, :]
        row_tenant = jnp.sum(jnp.where(slot, device_tenant_list, 0), axis=1)
        everyone = lax.all_gather(hidden, "wide", axis=0, tiled=True)
        tenants = lax.all_gather(row_tenant, "wide", axis=0, tiled=True)
        tenants = jnp.broadcast_to(tenants[:, None], (rows, LANES))
        hx, base_low_rank = call(
            plain_rows_kernel,
            [jax.ShapeDtypeStruct((n, local_rows, LANES), F32)] * 2,
            [vmem()] * 5,
            [vmem()] * 2,
        )(everyone, tokens, down_factors, lax.dynamic_slice(everyone, (0, me * fa), (rows, fa)), tenants)

    if not small:
        masks, hx, base_low_rank = None, (hx,), (base_low_rank,)
        tenants = (tenants.reshape(n, local_rows, LANES),)
    part_shape = (n, HALF, 2 * (fa + fb) + (LANES if small else 0))
    my_tenant = lax.dynamic_slice(tenant_of_block, (me,), (1,))
    parts, tenants, *low_rank = call(
        functools.partial(block_kernel, small, masks),
        [jax.ShapeDtypeStruct(part_shape, BF16), jax.ShapeDtypeStruct((rows, LANES), jnp.int32)]
        + ([] if small else [jax.ShapeDtypeStruct((quarter, LANES), F32)]),
        [smem(), smem()] + [vmem()] * (3 + 3 * len(hx)),
        [vmem()] * (2 if small else 3),
        scratch=[pltpu.VMEM((RANK, width), BF16), pltpu.VMEM((RANK, features), BF16)]
        + [pltpu.VMEM((n, local_rows, LANES), t) for t in (F32, F32, jnp.int32)],
        flops=4 * RANK * BLOCK * n * (fa + fb),
        nbytes=2 * BLOCK * n * (fa + fb),
    )(my_tenant, me[None], tokens, query_output_gradient, got, *hx, *base_low_rank, *tenants)
    low_rank = [lax.psum(p, "wide") for p in low_rank]
    parts = exchange(parts)

    delta = call(
        functools.partial(delta_kernel, fa),
        jax.ShapeDtypeStruct((n, local_rows, fb), F32),
        [smem()] + [vmem()] * (3 + len(low_rank)),
        vmem(),
        flops=2 * rows * cols * fb,
        nbytes=2 * cols * fb,
    )(tenant_of_block, parts, up_factors_transposed, tenants, *low_rank)
    delta = exchange(delta)

    down_gradient, up_gradient = call(
        gradient_kernel,
        [jax.ShapeDtypeStruct((fa, cols), F32), jax.ShapeDtypeStruct((fb, cols), F32)],
        [smem(), vmem()],
        [vmem()] * 2,
        flops=2 * n * RANK * (fa + fb) * LANES,
        nbytes=4 * cols * (fa + fb),
    )(tenant_of_block, parts)
    attended = call(
        attention_kernel,
        jax.ShapeDtypeStruct((local_rows, HEADS * HEAD_DIM), BF16),
        [smem(), vmem(), vmem(), vmem(), vmem()],
        vmem(),
        flops=4 * HEADS * local_rows * cached_key_rows.shape[1] * HEAD_DIM,
        nbytes=4 * cached_key_rows.size,
    )(live_cache_length, delta, base_query_rows.astype(F32), cached_key_rows, cached_value_rows)
    return down_gradient, up_gradient, attended


def solution(mesh):
    placed = (
        P(("groups", "wide"), None),
        P(("groups", "wide"), None),
        P("wide", "groups"),
        P("wide", "groups"),
        P("groups"),
        P(("groups", "wide"), None),
        P(("groups", "wide")),
        P(("groups", "wide"), None),
        P(("groups", "wide"), None),
        P(("groups", "wide"), None, None),
        P(("groups", "wide"), None, None),
        P(("groups", "wide")),
    )
    return jax.shard_map(
        per_device,
        mesh=mesh,
        in_specs=placed,
        out_specs=(P("wide", "groups"), P("wide", "groups"), P(("groups", "wide"), None)),
        check_vma=False,
    )
```

```python
import functools

import jax
import jax.numpy as jnp
from jax import lax
from jax.experimental import pallas as pl
from jax.experimental.pallas import tpu as pltpu
from jax.sharding import PartitionSpec as P

HEAD_DIM = 128
HEADS = 32
KV_HEADS = 4
RANK = 32
TENANTS = 64
BLOCK = 128
ROWS_DEV = 4
LANES = 128
PER_TILE = LANES // RANK

adapter_scale = 2.0
learning_rate = 0.0002

F32 = jnp.float32
BF16 = jnp.bfloat16
VMEM_LIMIT = 24 * 1024 * 1024
ALL_VMEM = 58 * 1024 * 1024 + 768 * 1024


def vmem():
    return pl.BlockSpec(memory_space=pltpu.VMEM)


def smem():
    return pl.BlockSpec(memory_space=pltpu.SMEM)


def hbm():
    return pl.BlockSpec(memory_space=pltpu.HBM)


def call(kernel, out_shape, in_specs, out_specs, scratch=(), flops=0, nbytes=0, limit=VMEM_LIMIT):
    return pl.pallas_call(
        kernel,
        out_shape=out_shape,
        in_specs=in_specs,
        out_specs=out_specs,
        scratch_shapes=list(scratch),
        compiler_params=pltpu.CompilerParams(vmem_limit_bytes=limit),
        cost_estimate=pl.CostEstimate(flops=flops, bytes_accessed=nbytes, transcendentals=0),
    )


def each(count, body):
    if count <= 16:
        for j in range(count):
            body(j)
    else:
        pl.loop(0, count)(body)


def dot(a, b, ca, cb):
    return lax.dot_general(a, b, (((ca,), (cb,)), ((), ())), preferred_element_type=F32)


def quarter_indicator(quarter, value):
    lane = lax.broadcasted_iota(jnp.int32, (RANK, LANES), 1)
    row = lax.broadcasted_iota(jnp.int32, (RANK, LANES), 0)
    return jnp.where(lane - row == quarter * RANK, value, 0.0).astype(BF16)


def tile_of(tenant):
    return pl.ds(pl.multiple_of((tenant // PER_TILE) * LANES, LANES), LANES)


HALF = RANK // 2
CHUNKS = HALF // ROWS_DEV


def up_half(h, fa, fb):
    return slice(h * fb, (h + 1) * fb)


def down_half(h, fa, fb):
    return slice(2 * fb + h * fa, 2 * fb + (h + 1) * fa)


def pick_kernel(tenant_ref, b_ref, a_ref, o_ref, b_tab, a_tab, o_buf, t_ref, sem_t, sem_b, sem_a, sem_o):
    n = t_ref.shape[0]
    fa, fb = a_ref.shape[0], b_ref.shape[0]

    def loads(src, dst, sem):
        step = src.shape[0] // sem.shape[0]
        parts = [slice(c * step, (c + 1) * step) for c in range(sem.shape[0])]
        return [pltpu.make_async_copy(src.at[r], dst.at[r], sem.at[c]) for c, r in enumerate(parts)]

    first, second = loads(b_ref, b_tab, sem_b), loads(a_ref, a_tab, sem_a)
    tenants = pltpu.make_async_copy(tenant_ref, t_ref, sem_t)
    for load in [tenants] + first + second:
        load.start()

    def picked(j, table):
        t = t_ref[j]
        return dot(quarter_indicator(t % PER_TILE, 1.0), table[:, tile_of(t)], 1, 1).astype(BF16)

    def up_body(j):
        up = picked(j, b_tab)
        for h in range(2):
            o_buf[j, :, up_half(h, fa, fb)] = up[h * HALF : (h + 1) * HALF]

    def down_body(j):
        down = picked(j, a_tab)
        for h in range(2):
            o_buf[j, :, down_half(h, fa, fb)] = down[h * HALF : (h + 1) * HALF]
        pltpu.make_async_copy(o_buf.at[j], o_ref.at[j], sem_o.at[j]).start()

    def finish(j):
        pltpu.make_async_copy(o_buf.at[j], o_ref.at[j], sem_o.at[j]).wait()

    for load in [tenants] + first:
        load.wait()
    each(n, up_body)
    for load in second:
        load.wait()
    each(n, down_body)
    each(n, finish)


def rows_pack_kernel(list_ref, slot_ref, hidden_ref, o_ref):
    hidden = hidden_ref[...].astype(F32)
    size = hidden.shape[1] // CHUNKS
    main = jnp.concatenate([hidden[:, p * size : (p + 1) * size] for p in range(CHUNKS)], axis=0)
    row = lax.broadcasted_iota(jnp.int32, (HALF, LANES), 0) % ROWS_DEV
    mark = jnp.zeros((HALF, LANES), jnp.int32)
    for r in range(ROWS_DEV):
        mark = jnp.where(row == r, list_ref[0, slot_ref[r]], mark)
    o_ref[...] = jnp.concatenate([main, mark.astype(F32)], axis=1).astype(BF16)


def fold_rows(product, tenant):
    rows = product.shape[0]
    lane = lax.broadcasted_iota(jnp.int32, (rows, LANES), 1)
    total = jnp.zeros((rows, LANES), F32)
    for c in range(TENANTS // PER_TILE):
        mine = tenant == c * PER_TILE + lane // RANK
        total = total + jnp.where(mine, product[:, c * LANES : (c + 1) * LANES], 0.0)
    half = total + pltpu.roll(total, 2 * RANK, 1)
    return half + pltpu.roll(half, RANK, 1)


def rows_kernel(me_ref, h0_ref, h1_ref, x_ref, a_ref, g_ref, hx_ref, base_ref, u_ref, g_out, sel, sem):
    copy = pltpu.make_async_copy(g_ref, g_out, sem)
    copy.start()
    h = jnp.concatenate([r[k] for r in (h0_ref, h1_ref) for k in range(r.shape[0])], axis=0)
    tiles = h.shape[0] // HALF
    size = h.shape[1] - LANES
    fa = a_ref.shape[0]

    def group(value, p):
        first = [k * HALF + p * ROWS_DEV for k in range(tiles)]
        return jnp.concatenate([value[f : f + ROWS_DEV] for f in first], axis=0)

    per_chunk = size // fa
    for m in range(per_chunk):

        @pl.when(me_ref[0] % per_chunk == m)
        def _():
            sel[...] = h[:, m * fa : (m + 1) * fa]

    wide = h.astype(F32)
    hx = jnp.zeros((tiles * ROWS_DEV, BLOCK), F32)
    for p in range(CHUNKS):
        chunk = group(wide[:, :size], p).astype(BF16)
        hx = hx + dot(chunk, x_ref[:, p * size : (p + 1) * size], 1, 1)
    tenant = group(wide[:, size:], 0).astype(jnp.int32)
    mine = sel[...].astype(F32)
    cols = group(mine, 0)
    for p in range(1, CHUNKS):
        cols = jnp.where(me_ref[0] // per_chunk == p, group(mine, p), cols)
    base = fold_rows(dot(cols.astype(BF16), a_ref[...], 1, 0), tenant)
    for k in range(tiles):
        rows = slice(k * ROWS_DEV, (k + 1) * ROWS_DEV)
        hx_ref[k], base_ref[k], u_ref[k] = hx[rows], base[rows], tenant[rows]
    copy.wait()


def plain_rows_kernel(h_ref, x_ref, a_ref, hc_ref, u_ref, hx_ref, base_ref):
    hx = dot(h_ref[...], x_ref[...], 1, 1)
    base = fold_rows(dot(hc_ref[...], a_ref[...], 1, 0), u_ref[...])
    for d in range(hx_ref.shape[0]):
        hx_ref[d] = hx[d * ROWS_DEV : (d + 1) * ROWS_DEV]
        base_ref[d] = base[d * ROWS_DEV : (d + 1) * ROWS_DEV]


def block_kernel(ride, masks, t_ref, me_ref, x_ref, g_ref, r_ref, *refs):
    sets = (len(refs) - (7 if ride else 8)) // 3
    hx_sets, base_sets, u_sets = (refs[i * sets : (i + 1) * sets] for i in range(3))
    o_ref, u_ref = refs[3 * sets : 3 * sets + 2]
    wa_ref, wb_ref, sx, sb, su = refs[-5:]
    n = r_ref.shape[0]
    fa, fb = x_ref.shape[1] // n, g_ref.shape[1] // n
    for d in range(n):
        for h in range(2):
            rank = slice(h * HALF, (h + 1) * HALF)
            wb_ref[rank, d * fb : (d + 1) * fb] = r_ref[d, :, up_half(h, fa, fb)]
            wa_ref[rank, d * fa : (d + 1) * fa] = r_ref[d, :, down_half(h, fa, fb)]
    back = dot(wb_ref[...], g_ref[...], 1, 1).astype(BF16)
    down = dot(wa_ref[...], x_ref[...], 1, 1).astype(BF16)

    k = 0
    for hx_ref, base_ref, tile_ref in zip(hx_sets, base_sets, u_sets):
        for i in range(hx_ref.shape[0]):
            d = me_ref[0] ^ masks[k] if masks else i
            sx[d], sb[d], su[d] = hx_ref[i], base_ref[i], tile_ref[i]
            k += 1
    hx, base, tenant = (jnp.concatenate([v[d] for d in range(n)], axis=0) for v in (sx, sb, su))
    u_ref[...] = tenant
    high = hx.astype(BF16)
    low = (hx - high.astype(F32)).astype(BF16)
    wide_back = jnp.concatenate([back] * PER_TILE, axis=0)
    change = dot(high, wide_back, 1, 1) + dot(low, wide_back, 1, 1)
    mine = tenant == t_ref[0]
    full = base - jnp.where(mine, learning_rate * (adapter_scale * change), 0.0)
    quarter = full.shape[0] // PER_TILE
    spot = lax.broadcasted_iota(jnp.int32, (quarter, LANES), 1) // RANK
    packed = jnp.zeros((quarter, LANES), F32)
    for q in range(PER_TILE):
        packed = packed + jnp.where(spot == q, full[q * quarter : (q + 1) * quarter], 0.0)
    if not ride:
        refs[3 * sets + 2][...] = packed

    down_part = dot(back, x_ref[...], 1, 0).astype(BF16)
    up_part = dot(down, g_ref[...], 1, 0).astype(BF16)
    for d in range(n):
        for h in range(2):
            rank = slice(h * HALF, (h + 1) * HALF)
            o_ref[d, :, up_half(h, fa, fb)] = up_part[rank, d * fb : (d + 1) * fb]
            o_ref[d, :, down_half(h, fa, fb)] = down_part[rank, d * fa : (d + 1) * fa]
        if ride:
            o_ref[d, :, 2 * (fa + fb) :] = packed.astype(BF16)


def sum_by_tenant(t_ref, part_ref, cut, fa, fb, grad_ref):
    grad_ref[...] = jnp.zeros_like(grad_ref)

    def body(j):
        t = t_ref[j]
        part = jnp.concatenate([part_ref[j, :, cut(h, fa, fb)] for h in range(2)], axis=0)
        place = quarter_indicator(t % PER_TILE, adapter_scale)
        grad_ref[:, tile_of(t)] += dot(part, place, 0, 0)

    each(t_ref.shape[0], body)


def gradient_kernel(t_ref, part_ref, down_ref, up_ref):
    fa, fb = down_ref.shape[0], up_ref.shape[0]
    sum_by_tenant(t_ref, part_ref, down_half, fa, fb, down_ref)
    sum_by_tenant(t_ref, part_ref, up_half, fa, fb, up_ref)


def delta_kernel(fa, t_ref, part_ref, b_ref, u_ref, *refs):
    o_ref = refs[-1]
    n, fb = part_ref.shape[0], b_ref.shape[0]
    if len(refs) == 2:
        total = refs[0][...]
    else:
        total = part_ref[0, :, 2 * (fa + fb) :].astype(F32)
        for d in range(1, n):
            total = total + part_ref[d, :, 2 * (fa + fb) :].astype(F32)
    spot = lax.broadcasted_iota(jnp.int32, total.shape, 1) // RANK
    pieces = []
    for q in range(PER_TILE):
        one = jnp.where(spot == q, total, 0.0)
        half = one + pltpu.roll(one, 2 * RANK, 1)
        pieces.append(half + pltpu.roll(half, RANK, 1))
    adapted = jnp.concatenate(pieces, axis=0)
    quarter = lax.broadcasted_iota(jnp.int32, adapted.shape, 1) // RANK
    tenant = u_ref[...]
    spread = [
        jnp.where(tenant == c * PER_TILE + quarter, adapted, 0.0).astype(BF16) for c in range(TENANTS // PER_TILE)
    ]
    old = dot(jnp.concatenate(spread, axis=1), b_ref[...], 1, 1)
    matched = []
    for c in range(n // PER_TILE):
        block = jnp.zeros(adapted.shape, jnp.int32)
        for i in range(PER_TILE):
            block = jnp.where(quarter == i, t_ref[c * PER_TILE + i], block)
        matched.append(jnp.where(tenant == block, adapted, 0.0).astype(BF16))
    up = [part_ref[j, :, up_half(h, fa, fb)] for j in range(n) for h in range(2)]
    change = dot(jnp.concatenate(matched, axis=1), jnp.concatenate(up, axis=0), 1, 0)
    delta = adapter_scale * (old - learning_rate * (adapter_scale * change))
    for d in range(n):
        o_ref[d] = delta[d * ROWS_DEV : (d + 1) * ROWS_DEV]


def attention_kernel(len_ref, delta_ref, base_ref, k_ref, v_ref, o_ref):
    n = delta_ref.shape[0]
    delta = jnp.concatenate([delta_ref[d] for d in range(n)], axis=1)
    query = (base_ref[...] + delta).astype(BF16).astype(F32)
    group = HEADS // KV_HEADS
    cache = k_ref.shape[1]
    many = HEADS * ROWS_DEV
    empty = jnp.zeros((group * ROWS_DEV, HEAD_DIM), F32)
    heads = []
    for g in range(KV_HEADS):
        mine = [query[:, h * HEAD_DIM : (h + 1) * HEAD_DIM] for h in range(g * group, (g + 1) * group)]
        lanes = [empty] * KV_HEADS
        lanes[g] = jnp.concatenate(mine, axis=0)
        heads.append(jnp.concatenate(lanes, axis=1))
    heads = jnp.concatenate(heads, axis=0).astype(BF16)
    row = lax.broadcasted_iota(jnp.int32, (many, cache), 0) % ROWS_DEV
    length = jnp.zeros((many, cache), jnp.int32)
    scores = jnp.zeros((many, cache), F32)
    for r in range(ROWS_DEV):
        length = jnp.where(row == r, len_ref[r], length)
        scores = jnp.where(row == r, dot(heads, k_ref[r], 1, 1), scores)
    live = lax.broadcasted_iota(jnp.int32, (many, cache), 1) < length
    scores = jnp.where(live, scores / jnp.sqrt(F32(HEAD_DIM)), F32(-1e30))
    top = jnp.max(scores, axis=-1, keepdims=True)
    expo = jnp.where(live, jnp.exp(scores - top), 0.0)
    weights = (expo / jnp.sum(expo, axis=-1, keepdims=True)).astype(BF16)
    mixed = [dot(weights, v_ref[r], 1, 0) for r in range(ROWS_DEV)]
    outs = []
    rows = group * ROWS_DEV
    row = lax.broadcasted_iota(jnp.int32, (rows, HEAD_DIM), 0) % ROWS_DEV
    for g in range(KV_HEADS):
        part = jnp.zeros((rows, HEAD_DIM), F32)
        for r in range(ROWS_DEV):
            part = jnp.where(
                row == r, mixed[r][g * rows : (g + 1) * rows, g * HEAD_DIM : (g + 1) * HEAD_DIM], part
            )
        outs.extend(part[i * ROWS_DEV : (i + 1) * ROWS_DEV] for i in range(group))
    o_ref[...] = jnp.concatenate(outs, axis=1).astype(BF16)


def exchange(x):
    return lax.all_to_all(x, "wide", split_axis=0, concat_axis=0, tiled=True)


def partner(x, mask):
    return lax.ppermute(x, "wide", [(i, i ^ mask) for i in range(lax.axis_size("wide"))])


def per_device(
    tokens,
    query_output_gradient,
    down_factors,
    up_factors_transposed,
    tenant_of_block,
    device_tenant_list,
    row_list_entry,
    hidden,
    base_query_rows,
    cached_key_rows,
    cached_value_rows,
    live_cache_length,
):
    n = lax.axis_size("wide")
    me = lax.axis_index("wide").astype(jnp.int32)
    small = n == 16
    fa, cols = down_factors.shape
    fb = up_factors_transposed.shape[0]
    local_rows = hidden.shape[0]
    rows = local_rows * n
    quarter = rows // PER_TILE
    width = tokens.shape[1]
    features = query_output_gradient.shape[1]
    assert tokens.shape[0] == BLOCK and tenant_of_block.shape[0] == n

    shape = (n, HALF, 2 * (fa + fb))
    chunks = 4 if fa % 64 == 0 and fb % 64 == 0 else 1
    packed = call(
        pick_kernel,
        jax.ShapeDtypeStruct(shape, BF16),
        [hbm(), hbm(), hbm()],
        hbm(),
        scratch=[
            pltpu.VMEM(up_factors_transposed.shape, BF16),
            pltpu.VMEM(down_factors.shape, BF16),
            pltpu.VMEM(shape, BF16),
            pltpu.SMEM((n,), jnp.int32),
            pltpu.SemaphoreType.DMA,
            pltpu.SemaphoreType.DMA((chunks,)),
            pltpu.SemaphoreType.DMA((chunks,)),
            pltpu.SemaphoreType.DMA((n,)),
        ],
        flops=2 * RANK * LANES * n * (fa + fb),
        nbytes=2 * cols * (fa + fb),
        limit=ALL_VMEM,
    )(tenant_of_block, up_factors_transposed, down_factors)

    if small:
        held = call(
            rows_pack_kernel,
            jax.ShapeDtypeStruct((HALF, width // CHUNKS + LANES), BF16),
            [smem(), smem(), vmem()],
            vmem(),
            nbytes=4 * local_rows * width,
            limit=ALL_VMEM,
        )(device_tenant_list, row_list_entry, hidden)[None]
        held = jnp.concatenate([held, partner(held, n // 2)], axis=0)
        held, packed = lax.optimization_barrier((held, packed))
        got = exchange(packed)
        masks = [0, n // 2]
        bit = n // 4
        while bit > 1:
            held = lax.optimization_barrier(jnp.concatenate([held, partner(held, bit)], axis=0))
            masks = masks + [m ^ bit for m in masks]
            bit //= 2
        masks = masks + [m ^ 1 for m in masks]
        *found, query_output_gradient = call(
            rows_kernel,
            [jax.ShapeDtypeStruct((n, local_rows, LANES), t) for t in (F32, F32, jnp.int32)]
            + [jax.ShapeDtypeStruct(query_output_gradient.shape, BF16)],
            [smem()] + [vmem()] * 4 + [hbm()],
            [vmem()] * 4,
            scratch=[pltpu.VMEM((n * HALF, fa), BF16), pltpu.SemaphoreType.DMA],
            flops=2 * rows * (BLOCK * width + fa * cols),
            nbytes=2 * BLOCK * width + 2 * fa * cols,
        )(me[None], held, partner(held, 1), tokens, down_factors, query_output_gradient)
        hx, base_low_rank, tenants = ((f,) for f in found)
    else:
        got = exchange(packed)
        slot = row_list_entry[:, None] == jnp.arange(device_tenant_list.shape[1], dtype=jnp.int32)[None, :]
        row_tenant = jnp.sum(jnp.where(slot, device_tenant_list, 0), axis=1)
        everyone = lax.all_gather(hidden, "wide", axis=0, tiled=True)
        tenants = lax.all_gather(row_tenant, "wide", axis=0, tiled=True)
        tenants = jnp.broadcast_to(tenants[:, None], (rows, LANES))
        hx, base_low_rank = call(
            plain_rows_kernel,
            [jax.ShapeDtypeStruct((n, local_rows, LANES), F32)] * 2,
            [vmem()] * 5,
            [vmem()] * 2,
        )(everyone, tokens, down_factors, lax.dynamic_slice(everyone, (0, me * fa), (rows, fa)), tenants)

    if not small:
        masks, hx, base_low_rank = None, (hx,), (base_low_rank,)
        tenants = (tenants.reshape(n, local_rows, LANES),)
    part_shape = (n, HALF, 2 * (fa + fb) + (LANES if small else 0))
    my_tenant = lax.dynamic_slice(tenant_of_block, (me,), (1,))
    parts, tenants, *low_rank = call(
        functools.partial(block_kernel, small, masks),
        [jax.ShapeDtypeStruct(part_shape, BF16), jax.ShapeDtypeStruct((rows, LANES), jnp.int32)]
        + ([] if small else [jax.ShapeDtypeStruct((quarter, LANES), F32)]),
        [smem(), smem()] + [vmem()] * (3 + 3 * len(hx)),
        [vmem()] * (2 if small else 3),
        scratch=[pltpu.VMEM((RANK, width), BF16), pltpu.VMEM((RANK, features), BF16)]
        + [pltpu.VMEM((n, local_rows, LANES), t) for t in (F32, F32, jnp.int32)],
        flops=4 * RANK * BLOCK * n * (fa + fb),
        nbytes=2 * BLOCK * n * (fa + fb),
    )(my_tenant, me[None], tokens, query_output_gradient, got, *hx, *base_low_rank, *tenants)
    low_rank = [lax.psum(p, "wide") for p in low_rank]
    parts = exchange(parts)

    delta = call(
        functools.partial(delta_kernel, fa),
        jax.ShapeDtypeStruct((n, local_rows, fb), F32),
        [smem()] + [vmem()] * (3 + len(low_rank)),
        vmem(),
        flops=2 * rows * cols * fb,
        nbytes=2 * cols * fb,
    )(tenant_of_block, parts, up_factors_transposed, tenants, *low_rank)
    delta = exchange(delta)

    down_gradient, up_gradient = call(
        gradient_kernel,
        [jax.ShapeDtypeStruct((fa, cols), F32), jax.ShapeDtypeStruct((fb, cols), F32)],
        [smem(), vmem()],
        [vmem()] * 2,
        flops=2 * n * RANK * (fa + fb) * LANES,
        nbytes=4 * cols * (fa + fb),
    )(tenant_of_block, parts)
    attended = call(
        attention_kernel,
        jax.ShapeDtypeStruct((local_rows, HEADS * HEAD_DIM), BF16),
        [smem(), vmem(), vmem(), vmem(), vmem()],
        vmem(),
        flops=4 * HEADS * local_rows * cached_key_rows.shape[1] * HEAD_DIM,
        nbytes=4 * cached_key_rows.size,
    )(live_cache_length, delta, base_query_rows.astype(F32), cached_key_rows, cached_value_rows)
    return down_gradient, up_gradient, attended


def solution(mesh):
    placed = (
        P(("groups", "wide"), None),
        P(("groups", "wide"), None),
        P("wide", "groups"),
        P("wide", "groups"),
        P("groups"),
        P(("groups", "wide"), None),
        P(("groups", "wide")),
        P(("groups", "wide"), None),
        P(("groups", "wide"), None),
        P(("groups", "wide"), None, None),
        P(("groups", "wide"), None, None),
        P(("groups", "wide")),
    )
    return jax.shard_map(
        per_device,
        mesh=mesh,
        in_specs=placed,
        out_specs=(P("wide", "groups"), P("wide", "groups"), P(("groups", "wide"), None)),
        check_vma=False,
    )
```

```python
import functools

import jax
import jax.numpy as jnp
from jax import lax
from jax.experimental import pallas as pl
from jax.experimental.pallas import tpu as pltpu
from jax.sharding import PartitionSpec as P

HEAD_DIM = 128
HEADS = 32
KV_HEADS = 4
RANK = 32
TENANTS = 64
BLOCK = 128
ROWS_DEV = 4
LANES = 128
PER_TILE = LANES // RANK

adapter_scale = 2.0
learning_rate = 0.0002

F32 = jnp.float32
BF16 = jnp.bfloat16
VMEM_LIMIT = 24 * 1024 * 1024
ALL_VMEM = 58 * 1024 * 1024 + 768 * 1024
BLOCK_VMEM = 59 * 1024 * 1024 + 512 * 1024


def vmem():
    return pl.BlockSpec(memory_space=pltpu.VMEM)


def smem():
    return pl.BlockSpec(memory_space=pltpu.SMEM)


def hbm():
    return pl.BlockSpec(memory_space=pltpu.HBM)


def call(kernel, out_shape, in_specs, out_specs, scratch=(), flops=0, nbytes=0, limit=VMEM_LIMIT):
    return pl.pallas_call(
        kernel,
        out_shape=out_shape,
        in_specs=in_specs,
        out_specs=out_specs,
        scratch_shapes=list(scratch),
        compiler_params=pltpu.CompilerParams(vmem_limit_bytes=limit),
        cost_estimate=pl.CostEstimate(flops=flops, bytes_accessed=nbytes, transcendentals=0),
    )


def each(count, body):
    if count <= 16:
        for j in range(count):
            body(j)
    else:
        pl.loop(0, count)(body)


def dot(a, b, ca, cb):
    return lax.dot_general(a, b, (((ca,), (cb,)), ((), ())), preferred_element_type=F32)


def quarter_indicator(quarter, value):
    lane = lax.broadcasted_iota(jnp.int32, (RANK, LANES), 1)
    row = lax.broadcasted_iota(jnp.int32, (RANK, LANES), 0)
    return jnp.where(lane - row == quarter * RANK, value, 0.0).astype(BF16)


def tile_of(tenant):
    return pl.ds(pl.multiple_of((tenant // PER_TILE) * LANES, LANES), LANES)


HALF = RANK // 2
CHUNKS = HALF // ROWS_DEV


def up_half(h, fa, fb):
    return slice(h * fb, (h + 1) * fb)


def down_half(h, fa, fb):
    return slice(2 * fb + h * fa, 2 * fb + (h + 1) * fa)


def pick_kernel(tenant_ref, b_ref, a_ref, o_ref, b_tab, a_tab, o_buf, t_ref, sem_t, sem_b, sem_a, sem_o):
    n = t_ref.shape[0]
    fa, fb = a_ref.shape[0], b_ref.shape[0]

    def loads(src, dst, sem):
        step = src.shape[0] // sem.shape[0]
        parts = [slice(c * step, (c + 1) * step) for c in range(sem.shape[0])]
        return [pltpu.make_async_copy(src.at[r], dst.at[r], sem.at[c]) for c, r in enumerate(parts)]

    first, second = loads(b_ref, b_tab, sem_b), loads(a_ref, a_tab, sem_a)
    tenants = pltpu.make_async_copy(tenant_ref, t_ref, sem_t)
    for load in [tenants] + first + second:
        load.start()

    def picked(j, table):
        t = t_ref[j]
        return dot(quarter_indicator(t % PER_TILE, 1.0), table[:, tile_of(t)], 1, 1).astype(BF16)

    def up_body(j):
        up = picked(j, b_tab)
        for h in range(2):
            o_buf[j, :, up_half(h, fa, fb)] = up[h * HALF : (h + 1) * HALF]

    def down_body(j):
        down = picked(j, a_tab)
        for h in range(2):
            o_buf[j, :, down_half(h, fa, fb)] = down[h * HALF : (h + 1) * HALF]
        pltpu.make_async_copy(o_buf.at[j], o_ref.at[j], sem_o.at[j]).start()

    def finish(j):
        pltpu.make_async_copy(o_buf.at[j], o_ref.at[j], sem_o.at[j]).wait()

    for load in [tenants] + first:
        load.wait()
    each(n, up_body)
    for load in second:
        load.wait()
    each(n, down_body)
    each(n, finish)


def rows_pack_kernel(list_ref, slot_ref, hidden_ref, o_ref):
    hidden = hidden_ref[...].astype(F32)
    size = hidden.shape[1] // CHUNKS
    main = jnp.concatenate([hidden[:, p * size : (p + 1) * size] for p in range(CHUNKS)], axis=0)
    row = lax.broadcasted_iota(jnp.int32, (HALF, LANES), 0) % ROWS_DEV
    mark = jnp.zeros((HALF, LANES), jnp.int32)
    for r in range(ROWS_DEV):
        mark = jnp.where(row == r, list_ref[0, slot_ref[r]], mark)
    o_ref[...] = jnp.concatenate([main, mark.astype(F32)], axis=1).astype(BF16)


def fold_rows(product, tenant):
    rows = product.shape[0]
    lane = lax.broadcasted_iota(jnp.int32, (rows, LANES), 1)
    total = jnp.zeros((rows, LANES), F32)
    for c in range(TENANTS // PER_TILE):
        mine = tenant == c * PER_TILE + lane // RANK
        total = total + jnp.where(mine, product[:, c * LANES : (c + 1) * LANES], 0.0)
    half = total + pltpu.roll(total, 2 * RANK, 1)
    return half + pltpu.roll(half, RANK, 1)


def rows_kernel(me_ref, h0_ref, h1_ref, x_ref, a_ref, hx_ref, base_ref, u_ref, sel):
    h = jnp.concatenate([r[k] for r in (h0_ref, h1_ref) for k in range(r.shape[0])], axis=0)
    tiles = h.shape[0] // HALF
    size = h.shape[1] - LANES
    fa = a_ref.shape[0]

    def group(value, p):
        first = [k * HALF + p * ROWS_DEV for k in range(tiles)]
        return jnp.concatenate([value[f : f + ROWS_DEV] for f in first], axis=0)

    per_chunk = size // fa
    for m in range(per_chunk):

        @pl.when(me_ref[0] % per_chunk == m)
        def _():
            sel[...] = h[:, m * fa : (m + 1) * fa]

    wide = h.astype(F32)
    hx = jnp.zeros((tiles * ROWS_DEV, BLOCK), F32)
    for p in range(CHUNKS):
        chunk = group(wide[:, :size], p).astype(BF16)
        hx = hx + dot(chunk, x_ref[:, p * size : (p + 1) * size], 1, 1)
    tenant = group(wide[:, size:], 0).astype(jnp.int32)
    mine = sel[...].astype(F32)
    cols = group(mine, 0)
    for p in range(1, CHUNKS):
        cols = jnp.where(me_ref[0] // per_chunk == p, group(mine, p), cols)
    base = fold_rows(dot(cols.astype(BF16), a_ref[...], 1, 0), tenant)
    for k in range(tiles):
        rows = slice(k * ROWS_DEV, (k + 1) * ROWS_DEV)
        hx_ref[k], base_ref[k], u_ref[k] = hx[rows], base[rows], tenant[rows]


def plain_rows_kernel(h_ref, x_ref, a_ref, hc_ref, u_ref, hx_ref, base_ref):
    hx = dot(h_ref[...], x_ref[...], 1, 1)
    base = fold_rows(dot(hc_ref[...], a_ref[...], 1, 0), u_ref[...])
    for d in range(hx_ref.shape[0]):
        hx_ref[d] = hx[d * ROWS_DEV : (d + 1) * ROWS_DEV]
        base_ref[d] = base[d * ROWS_DEV : (d + 1) * ROWS_DEV]


def block_kernel(ride, masks, t_ref, me_ref, x_ref, g_hbm, r_ref, *refs):
    sets = (len(refs) - (9 if ride else 10)) // 3
    hx_sets, base_sets, u_sets = (refs[i * sets : (i + 1) * sets] for i in range(3))
    o_ref, u_ref = refs[3 * sets : 3 * sets + 2]
    wa_ref, wb_ref, sx, sb, su, g_ref, sem = refs[-7:]
    step = g_ref.shape[0] // sem.shape[0]
    loads = []
    for c in range(sem.shape[0]):
        part = slice(c * step, (c + 1) * step)
        loads.append(pltpu.make_async_copy(g_hbm.at[part], g_ref.at[part], sem.at[c]))
        loads[-1].start()
    n = r_ref.shape[0]
    fa, fb = x_ref.shape[1] // n, g_ref.shape[1] // n
    for d in range(n):
        for h in range(2):
            rank = slice(h * HALF, (h + 1) * HALF)
            wb_ref[rank, d * fb : (d + 1) * fb] = r_ref[d, :, up_half(h, fa, fb)]
            wa_ref[rank, d * fa : (d + 1) * fa] = r_ref[d, :, down_half(h, fa, fb)]
    down = dot(wa_ref[...], x_ref[...], 1, 1).astype(BF16)
    for load in loads:
        load.wait()
    back = dot(wb_ref[...], g_ref[...], 1, 1).astype(BF16)

    k = 0
    for hx_ref, base_ref, tile_ref in zip(hx_sets, base_sets, u_sets):
        for i in range(hx_ref.shape[0]):
            d = me_ref[0] ^ masks[k] if masks else i
            sx[d], sb[d], su[d] = hx_ref[i], base_ref[i], tile_ref[i]
            k += 1
    hx, base, tenant = (jnp.concatenate([v[d] for d in range(n)], axis=0) for v in (sx, sb, su))
    u_ref[...] = tenant
    high = hx.astype(BF16)
    low = (hx - high.astype(F32)).astype(BF16)
    wide_back = jnp.concatenate([back] * PER_TILE, axis=0)
    change = dot(high, wide_back, 1, 1) + dot(low, wide_back, 1, 1)
    mine = tenant == t_ref[0]
    full = base - jnp.where(mine, learning_rate * (adapter_scale * change), 0.0)
    quarter = full.shape[0] // PER_TILE
    spot = lax.broadcasted_iota(jnp.int32, (quarter, LANES), 1) // RANK
    packed = jnp.zeros((quarter, LANES), F32)
    for q in range(PER_TILE):
        packed = packed + jnp.where(spot == q, full[q * quarter : (q + 1) * quarter], 0.0)
    if not ride:
        refs[3 * sets + 2][...] = packed

    down_part = dot(back, x_ref[...], 1, 0).astype(BF16)
    up_part = dot(down, g_ref[...], 1, 0).astype(BF16)
    for d in range(n):
        for h in range(2):
            rank = slice(h * HALF, (h + 1) * HALF)
            o_ref[d, :, up_half(h, fa, fb)] = up_part[rank, d * fb : (d + 1) * fb]
            o_ref[d, :, down_half(h, fa, fb)] = down_part[rank, d * fa : (d + 1) * fa]
        if ride:
            o_ref[d, :, 2 * (fa + fb) :] = packed.astype(BF16)


def sum_by_tenant(t_ref, part_ref, cut, fa, fb, grad_ref):
    grad_ref[...] = jnp.zeros_like(grad_ref)

    def body(j):
        t = t_ref[j]
        part = jnp.concatenate([part_ref[j, :, cut(h, fa, fb)] for h in range(2)], axis=0)
        place = quarter_indicator(t % PER_TILE, adapter_scale)
        grad_ref[:, tile_of(t)] += dot(part, place, 0, 0)

    each(t_ref.shape[0], body)


def gradient_kernel(t_ref, part_ref, down_ref, up_ref):
    fa, fb = down_ref.shape[0], up_ref.shape[0]
    sum_by_tenant(t_ref, part_ref, down_half, fa, fb, down_ref)
    sum_by_tenant(t_ref, part_ref, up_half, fa, fb, up_ref)


def delta_kernel(fa, t_ref, part_ref, b_ref, u_ref, *refs):
    o_ref = refs[-1]
    n, fb = part_ref.shape[0], b_ref.shape[0]
    if len(refs) == 2:
        total = refs[0][...]
    else:
        total = part_ref[0, :, 2 * (fa + fb) :].astype(F32)
        for d in range(1, n):
            total = total + part_ref[d, :, 2 * (fa + fb) :].astype(F32)
    spot = lax.broadcasted_iota(jnp.int32, total.shape, 1) // RANK
    pieces = []
    for q in range(PER_TILE):
        one = jnp.where(spot == q, total, 0.0)
        half = one + pltpu.roll(one, 2 * RANK, 1)
        pieces.append(half + pltpu.roll(half, RANK, 1))
    adapted = jnp.concatenate(pieces, axis=0)
    quarter = lax.broadcasted_iota(jnp.int32, adapted.shape, 1) // RANK
    tenant = u_ref[...]
    spread = [
        jnp.where(tenant == c * PER_TILE + quarter, adapted, 0.0).astype(BF16) for c in range(TENANTS // PER_TILE)
    ]
    old = dot(jnp.concatenate(spread, axis=1), b_ref[...], 1, 1)
    matched = []
    for c in range(n // PER_TILE):
        block = jnp.zeros(adapted.shape, jnp.int32)
        for i in range(PER_TILE):
            block = jnp.where(quarter == i, t_ref[c * PER_TILE + i], block)
        matched.append(jnp.where(tenant == block, adapted, 0.0).astype(BF16))
    up = [part_ref[j, :, up_half(h, fa, fb)] for j in range(n) for h in range(2)]
    change = dot(jnp.concatenate(matched, axis=1), jnp.concatenate(up, axis=0), 1, 0)
    delta = adapter_scale * (old - learning_rate * (adapter_scale * change))
    for d in range(n):
        o_ref[d] = delta[d * ROWS_DEV : (d + 1) * ROWS_DEV]


def attention_kernel(len_ref, delta_ref, base_ref, k_ref, v_ref, o_ref):
    n = delta_ref.shape[0]
    delta = jnp.concatenate([delta_ref[d] for d in range(n)], axis=1)
    query = (base_ref[...] + delta).astype(BF16).astype(F32)
    group = HEADS // KV_HEADS
    cache = k_ref.shape[1]
    many = HEADS * ROWS_DEV
    empty = jnp.zeros((group * ROWS_DEV, HEAD_DIM), F32)
    heads = []
    for g in range(KV_HEADS):
        mine = [query[:, h * HEAD_DIM : (h + 1) * HEAD_DIM] for h in range(g * group, (g + 1) * group)]
        lanes = [empty] * KV_HEADS
        lanes[g] = jnp.concatenate(mine, axis=0)
        heads.append(jnp.concatenate(lanes, axis=1))
    heads = jnp.concatenate(heads, axis=0).astype(BF16)
    row = lax.broadcasted_iota(jnp.int32, (many, cache), 0) % ROWS_DEV
    length = jnp.zeros((many, cache), jnp.int32)
    scores = jnp.zeros((many, cache), F32)
    for r in range(ROWS_DEV):
        length = jnp.where(row == r, len_ref[r], length)
        scores = jnp.where(row == r, dot(heads, k_ref[r], 1, 1), scores)
    live = lax.broadcasted_iota(jnp.int32, (many, cache), 1) < length
    scores = jnp.where(live, scores / jnp.sqrt(F32(HEAD_DIM)), F32(-1e30))
    top = jnp.max(scores, axis=-1, keepdims=True)
    expo = jnp.where(live, jnp.exp(scores - top), 0.0)
    weights = (expo / jnp.sum(expo, axis=-1, keepdims=True)).astype(BF16)
    mixed = [dot(weights, v_ref[r], 1, 0) for r in range(ROWS_DEV)]
    outs = []
    rows = group * ROWS_DEV
    row = lax.broadcasted_iota(jnp.int32, (rows, HEAD_DIM), 0) % ROWS_DEV
    for g in range(KV_HEADS):
        part = jnp.zeros((rows, HEAD_DIM), F32)
        for r in range(ROWS_DEV):
            part = jnp.where(
                row == r, mixed[r][g * rows : (g + 1) * rows, g * HEAD_DIM : (g + 1) * HEAD_DIM], part
            )
        outs.extend(part[i * ROWS_DEV : (i + 1) * ROWS_DEV] for i in range(group))
    o_ref[...] = jnp.concatenate(outs, axis=1).astype(BF16)


def exchange(x):
    return lax.all_to_all(x, "wide", split_axis=0, concat_axis=0, tiled=True)


def partner(x, mask):
    return lax.ppermute(x, "wide", [(i, i ^ mask) for i in range(lax.axis_size("wide"))])


def per_device(
    tokens,
    query_output_gradient,
    down_factors,
    up_factors_transposed,
    tenant_of_block,
    device_tenant_list,
    row_list_entry,
    hidden,
    base_query_rows,
    cached_key_rows,
    cached_value_rows,
    live_cache_length,
):
    n = lax.axis_size("wide")
    me = lax.axis_index("wide").astype(jnp.int32)
    small = n == 16
    fa, cols = down_factors.shape
    fb = up_factors_transposed.shape[0]
    local_rows = hidden.shape[0]
    rows = local_rows * n
    quarter = rows // PER_TILE
    width = tokens.shape[1]
    features = query_output_gradient.shape[1]
    assert tokens.shape[0] == BLOCK and tenant_of_block.shape[0] == n

    shape = (n, HALF, 2 * (fa + fb))
    chunks = 4 if fa % 64 == 0 and fb % 64 == 0 else 1
    packed = call(
        pick_kernel,
        jax.ShapeDtypeStruct(shape, BF16),
        [hbm(), hbm(), hbm()],
        hbm(),
        scratch=[
            pltpu.VMEM(up_factors_transposed.shape, BF16),
            pltpu.VMEM(down_factors.shape, BF16),
            pltpu.VMEM(shape, BF16),
            pltpu.SMEM((n,), jnp.int32),
            pltpu.SemaphoreType.DMA,
            pltpu.SemaphoreType.DMA((chunks,)),
            pltpu.SemaphoreType.DMA((chunks,)),
            pltpu.SemaphoreType.DMA((n,)),
        ],
        flops=2 * RANK * LANES * n * (fa + fb),
        nbytes=2 * cols * (fa + fb),
        limit=ALL_VMEM,
    )(tenant_of_block, up_factors_transposed, down_factors)

    if small:
        held = call(
            rows_pack_kernel,
            jax.ShapeDtypeStruct((HALF, width // CHUNKS + LANES), BF16),
            [smem(), smem(), vmem()],
            vmem(),
            nbytes=4 * local_rows * width,
            limit=ALL_VMEM,
        )(device_tenant_list, row_list_entry, hidden)[None]
        held = jnp.concatenate([held, partner(held, n // 2)], axis=0)
        held, packed = lax.optimization_barrier((held, packed))
        got = exchange(packed)
        masks = [0, n // 2]
        bit = n // 4
        while bit > 1:
            held = lax.optimization_barrier(jnp.concatenate([held, partner(held, bit)], axis=0))
            masks = masks + [m ^ bit for m in masks]
            bit //= 2
        masks = masks + [m ^ 1 for m in masks]
        found = call(
            rows_kernel,
            [jax.ShapeDtypeStruct((n, local_rows, LANES), t) for t in (F32, F32, jnp.int32)],
            [smem()] + [vmem()] * 4,
            [vmem()] * 3,
            scratch=[pltpu.VMEM((n * HALF, fa), BF16)],
            flops=2 * rows * (BLOCK * width + fa * cols),
            nbytes=2 * BLOCK * width + 2 * fa * cols,
        )(me[None], held, partner(held, 1), tokens, down_factors)
        hx, base_low_rank, tenants = ((f,) for f in found)
    else:
        got = exchange(packed)
        slot = row_list_entry[:, None] == jnp.arange(device_tenant_list.shape[1], dtype=jnp.int32)[None, :]
        row_tenant = jnp.sum(jnp.where(slot, device_tenant_list, 0), axis=1)
        everyone = lax.all_gather(hidden, "wide", axis=0, tiled=True)
        tenants = lax.all_gather(row_tenant, "wide", axis=0, tiled=True)
        tenants = jnp.broadcast_to(tenants[:, None], (rows, LANES))
        hx, base_low_rank = call(
            plain_rows_kernel,
            [jax.ShapeDtypeStruct((n, local_rows, LANES), F32)] * 2,
            [vmem()] * 5,
            [vmem()] * 2,
        )(everyone, tokens, down_factors, lax.dynamic_slice(everyone, (0, me * fa), (rows, fa)), tenants)

    if not small:
        masks, hx, base_low_rank = None, (hx,), (base_low_rank,)
        tenants = (tenants.reshape(n, local_rows, LANES),)
    part_shape = (n, HALF, 2 * (fa + fb) + (LANES if small else 0))
    my_tenant = lax.dynamic_slice(tenant_of_block, (me,), (1,))
    parts, tenants, *low_rank = call(
        functools.partial(block_kernel, small, masks),
        [jax.ShapeDtypeStruct(part_shape, BF16), jax.ShapeDtypeStruct((rows, LANES), jnp.int32)]
        + ([] if small else [jax.ShapeDtypeStruct((quarter, LANES), F32)]),
        [smem(), smem(), vmem(), hbm()] + [vmem()] * (1 + 3 * len(hx)),
        [vmem()] * (2 if small else 3),
        scratch=[pltpu.VMEM((RANK, width), BF16), pltpu.VMEM((RANK, features), BF16)]
        + [pltpu.VMEM((n, local_rows, LANES), t) for t in (F32, F32, jnp.int32)]
        + [pltpu.VMEM(query_output_gradient.shape, BF16), pltpu.SemaphoreType.DMA((4,))],
        limit=BLOCK_VMEM,
        flops=4 * RANK * BLOCK * n * (fa + fb),
        nbytes=2 * BLOCK * n * (fa + fb),
    )(my_tenant, me[None], tokens, query_output_gradient, got, *hx, *base_low_rank, *tenants)
    low_rank = [lax.psum(p, "wide") for p in low_rank]
    parts = exchange(parts)

    delta = call(
        functools.partial(delta_kernel, fa),
        jax.ShapeDtypeStruct((n, local_rows, fb), F32),
        [smem()] + [vmem()] * (3 + len(low_rank)),
        vmem(),
        flops=2 * rows * cols * fb,
        nbytes=2 * cols * fb,
    )(tenant_of_block, parts, up_factors_transposed, tenants, *low_rank)
    delta = exchange(delta)

    down_gradient, up_gradient = call(
        gradient_kernel,
        [jax.ShapeDtypeStruct((fa, cols), F32), jax.ShapeDtypeStruct((fb, cols), F32)],
        [smem(), vmem()],
        [vmem()] * 2,
        flops=2 * n * RANK * (fa + fb) * LANES,
        nbytes=4 * cols * (fa + fb),
    )(tenant_of_block, parts)
    attended = call(
        attention_kernel,
        jax.ShapeDtypeStruct((local_rows, HEADS * HEAD_DIM), BF16),
        [smem(), vmem(), vmem(), vmem(), vmem()],
        vmem(),
        flops=4 * HEADS * local_rows * cached_key_rows.shape[1] * HEAD_DIM,
        nbytes=4 * cached_key_rows.size,
    )(live_cache_length, delta, base_query_rows.astype(F32), cached_key_rows, cached_value_rows)
    return down_gradient, up_gradient, attended


def solution(mesh):
    placed = (
        P(("groups", "wide"), None),
        P(("groups", "wide"), None),
        P("wide", "groups"),
        P("wide", "groups"),
        P("groups"),
        P(("groups", "wide"), None),
        P(("groups", "wide")),
        P(("groups", "wide"), None),
        P(("groups", "wide"), None),
        P(("groups", "wide"), None, None),
        P(("groups", "wide"), None, None),
        P(("groups", "wide")),
    )
    return jax.shard_map(
        per_device,
        mesh=mesh,
        in_specs=placed,
        out_specs=(P("wide", "groups"), P("wide", "groups"), P(("groups", "wide"), None)),
        check_vma=False,
    )
```

```python
import functools

import jax
import jax.numpy as jnp
from jax import lax
from jax.experimental import pallas as pl
from jax.experimental.pallas import tpu as pltpu
from jax.sharding import PartitionSpec as P

HEAD_DIM = 128
HEADS = 32
KV_HEADS = 4
RANK = 32
TENANTS = 64
BLOCK = 128
ROWS_DEV = 4
LANES = 128
PER_TILE = LANES // RANK

adapter_scale = 2.0
learning_rate = 0.0002

F32 = jnp.float32
BF16 = jnp.bfloat16
VMEM_LIMIT = 24 * 1024 * 1024
ALL_VMEM = 58 * 1024 * 1024 + 768 * 1024
PICK_VMEM = 50 * 1024 * 1024


def vmem():
    return pl.BlockSpec(memory_space=pltpu.VMEM)


def smem():
    return pl.BlockSpec(memory_space=pltpu.SMEM)


def hbm():
    return pl.BlockSpec(memory_space=pltpu.HBM)


def call(kernel, out_shape, in_specs, out_specs, scratch=(), flops=0, nbytes=0, limit=VMEM_LIMIT):
    return pl.pallas_call(
        kernel,
        out_shape=out_shape,
        in_specs=in_specs,
        out_specs=out_specs,
        scratch_shapes=list(scratch),
        compiler_params=pltpu.CompilerParams(vmem_limit_bytes=limit),
        cost_estimate=pl.CostEstimate(flops=flops, bytes_accessed=nbytes, transcendentals=0),
    )


def each(count, body):
    if count <= 16:
        for j in range(count):
            body(j)
    else:
        pl.loop(0, count)(body)


def dot(a, b, ca, cb):
    return lax.dot_general(a, b, (((ca,), (cb,)), ((), ())), preferred_element_type=F32)


def quarter_indicator(quarter, value):
    lane = lax.broadcasted_iota(jnp.int32, (RANK, LANES), 1)
    row = lax.broadcasted_iota(jnp.int32, (RANK, LANES), 0)
    return jnp.where(lane - row == quarter * RANK, value, 0.0).astype(BF16)


def tile_of(tenant):
    return pl.ds(pl.multiple_of((tenant // PER_TILE) * LANES, LANES), LANES)


HALF = RANK // 2
CHUNKS = HALF // ROWS_DEV


def up_half(h, fa, fb):
    return slice(h * fb, (h + 1) * fb)


def down_half(h, fa, fb):
    return slice(2 * fb + h * fa, 2 * fb + (h + 1) * fa)


def pick_kernel(tenant_ref, b_ref, a_ref, o_ref, b_tab, a_tab, o_buf, t_ref, sem_t, sem_b, sem_a, sem_o):
    n = t_ref.shape[0]
    fa, fb = a_ref.shape[0], b_ref.shape[0]

    def loads(src, dst, sem):
        step = src.shape[0] // sem.shape[0]
        parts = [slice(c * step, (c + 1) * step) for c in range(sem.shape[0])]
        return [pltpu.make_async_copy(src.at[r], dst.at[r], sem.at[c]) for c, r in enumerate(parts)]

    first, second = loads(b_ref, b_tab, sem_b), loads(a_ref, a_tab, sem_a)
    tenants = pltpu.make_async_copy(tenant_ref, t_ref, sem_t)
    for load in [tenants] + first + second:
        load.start()

    def picked(j, table):
        t = t_ref[j]
        return dot(quarter_indicator(t % PER_TILE, 1.0), table[:, tile_of(t)], 1, 1).astype(BF16)

    def up_body(j):
        up = picked(j, b_tab)
        for h in range(2):
            o_buf[j, :, up_half(h, fa, fb)] = up[h * HALF : (h + 1) * HALF]

    def down_body(j):
        down = picked(j, a_tab)
        for h in range(2):
            o_buf[j, :, down_half(h, fa, fb)] = down[h * HALF : (h + 1) * HALF]
        pltpu.make_async_copy(o_buf.at[j], o_ref.at[j], sem_o.at[j]).start()

    def finish(j):
        pltpu.make_async_copy(o_buf.at[j], o_ref.at[j], sem_o.at[j]).wait()

    for load in [tenants] + first:
        load.wait()
    each(n, up_body)
    for load in second:
        load.wait()
    each(n, down_body)
    each(n, finish)


def rows_pack_kernel(list_ref, slot_ref, hidden_ref, o_ref):
    hidden = hidden_ref[...].astype(F32)
    size = hidden.shape[1] // CHUNKS
    main = jnp.concatenate([hidden[:, p * size : (p + 1) * size] for p in range(CHUNKS)], axis=0)
    row = lax.broadcasted_iota(jnp.int32, (HALF, LANES), 0) % ROWS_DEV
    mark = jnp.zeros((HALF, LANES), jnp.int32)
    for r in range(ROWS_DEV):
        mark = jnp.where(row == r, list_ref[0, slot_ref[r]], mark)
    o_ref[...] = jnp.concatenate([main, mark.astype(F32)], axis=1).astype(BF16)


def fold_rows(product, tenant):
    rows = product.shape[0]
    lane = lax.broadcasted_iota(jnp.int32, (rows, LANES), 1)
    total = jnp.zeros((rows, LANES), F32)
    for c in range(TENANTS // PER_TILE):
        mine = tenant == c * PER_TILE + lane // RANK
        total = total + jnp.where(mine, product[:, c * LANES : (c + 1) * LANES], 0.0)
    half = total + pltpu.roll(total, 2 * RANK, 1)
    return half + pltpu.roll(half, RANK, 1)


def rows_kernel(me_ref, h0_ref, h1_ref, x_ref, a_ref, hx_ref, base_ref, u_ref, sel):
    h = jnp.concatenate([r[k] for r in (h0_ref, h1_ref) for k in range(r.shape[0])], axis=0)
    tiles = h.shape[0] // HALF
    size = h.shape[1] - LANES
    fa = a_ref.shape[0]

    def group(value, p):
        first = [k * HALF + p * ROWS_DEV for k in range(tiles)]
        return jnp.concatenate([value[f : f + ROWS_DEV] for f in first], axis=0)

    per_chunk = size // fa
    for m in range(per_chunk):

        @pl.when(me_ref[0] % per_chunk == m)
        def _():
            sel[...] = h[:, m * fa : (m + 1) * fa]

    wide = h.astype(F32)
    hx = jnp.zeros((tiles * ROWS_DEV, BLOCK), F32)
    for p in range(CHUNKS):
        chunk = group(wide[:, :size], p).astype(BF16)
        hx = hx + dot(chunk, x_ref[:, p * size : (p + 1) * size], 1, 1)
    tenant = group(wide[:, size:], 0).astype(jnp.int32)
    mine = sel[...].astype(F32)
    cols = group(mine, 0)
    for p in range(1, CHUNKS):
        cols = jnp.where(me_ref[0] // per_chunk == p, group(mine, p), cols)
    base = fold_rows(dot(cols.astype(BF16), a_ref[...], 1, 0), tenant)
    for k in range(tiles):
        rows = slice(k * ROWS_DEV, (k + 1) * ROWS_DEV)
        hx_ref[k], base_ref[k], u_ref[k] = hx[rows], base[rows], tenant[rows]


def plain_rows_kernel(h_ref, x_ref, a_ref, hc_ref, u_ref, hx_ref, base_ref):
    hx = dot(h_ref[...], x_ref[...], 1, 1)
    base = fold_rows(dot(hc_ref[...], a_ref[...], 1, 0), u_ref[...])
    for d in range(hx_ref.shape[0]):
        hx_ref[d] = hx[d * ROWS_DEV : (d + 1) * ROWS_DEV]
        base_ref[d] = base[d * ROWS_DEV : (d + 1) * ROWS_DEV]


def block_kernel(ride, masks, t_ref, me_ref, x_ref, g_ref, r_ref, *refs):
    sets = (len(refs) - (7 if ride else 8)) // 3
    hx_sets, base_sets, u_sets = (refs[i * sets : (i + 1) * sets] for i in range(3))
    o_ref, u_ref = refs[3 * sets : 3 * sets + 2]
    wa_ref, wb_ref, sx, sb, su = refs[-5:]
    n = r_ref.shape[0]
    fa, fb = x_ref.shape[1] // n, g_ref.shape[1] // n
    for d in range(n):
        for h in range(2):
            rank = slice(h * HALF, (h + 1) * HALF)
            wb_ref[rank, d * fb : (d + 1) * fb] = r_ref[d, :, up_half(h, fa, fb)]
            wa_ref[rank, d * fa : (d + 1) * fa] = r_ref[d, :, down_half(h, fa, fb)]
    back = dot(wb_ref[...], g_ref[...], 1, 1).astype(BF16)
    down = dot(wa_ref[...], x_ref[...], 1, 1).astype(BF16)

    k = 0
    for hx_ref, base_ref, tile_ref in zip(hx_sets, base_sets, u_sets):
        for i in range(hx_ref.shape[0]):
            d = me_ref[0] ^ masks[k] if masks else i
            sx[d], sb[d], su[d] = hx_ref[i], base_ref[i], tile_ref[i]
            k += 1
    hx, base, tenant = (jnp.concatenate([v[d] for d in range(n)], axis=0) for v in (sx, sb, su))
    u_ref[...] = tenant
    high = hx.astype(BF16)
    low = (hx - high.astype(F32)).astype(BF16)
    wide_back = jnp.concatenate([back] * PER_TILE, axis=0)
    change = dot(high, wide_back, 1, 1) + dot(low, wide_back, 1, 1)
    mine = tenant == t_ref[0]
    full = base - jnp.where(mine, learning_rate * (adapter_scale * change), 0.0)
    quarter = full.shape[0] // PER_TILE
    spot = lax.broadcasted_iota(jnp.int32, (quarter, LANES), 1) // RANK
    packed = jnp.zeros((quarter, LANES), F32)
    for q in range(PER_TILE):
        packed = packed + jnp.where(spot == q, full[q * quarter : (q + 1) * quarter], 0.0)
    if not ride:
        refs[3 * sets + 2][...] = packed

    down_part = dot(back, x_ref[...], 1, 0).astype(BF16)
    up_part = dot(down, g_ref[...], 1, 0).astype(BF16)
    for d in range(n):
        for h in range(2):
            rank = slice(h * HALF, (h + 1) * HALF)
            o_ref[d, :, up_half(h, fa, fb)] = up_part[rank, d * fb : (d + 1) * fb]
            o_ref[d, :, down_half(h, fa, fb)] = down_part[rank, d * fa : (d + 1) * fa]
        if ride:
            o_ref[d, :, 2 * (fa + fb) :] = packed.astype(BF16)


def sum_by_tenant(t_ref, part_ref, cut, fa, fb, grad_ref):
    grad_ref[...] = jnp.zeros_like(grad_ref)

    def body(j):
        t = t_ref[j]
        part = jnp.concatenate([part_ref[j, :, cut(h, fa, fb)] for h in range(2)], axis=0)
        place = quarter_indicator(t % PER_TILE, adapter_scale)
        grad_ref[:, tile_of(t)] += dot(part, place, 0, 0)

    each(t_ref.shape[0], body)


def gradient_kernel(t_ref, part_ref, down_ref, up_ref):
    fa, fb = down_ref.shape[0], up_ref.shape[0]
    sum_by_tenant(t_ref, part_ref, down_half, fa, fb, down_ref)
    sum_by_tenant(t_ref, part_ref, up_half, fa, fb, up_ref)


def delta_kernel(fa, t_ref, part_ref, b_ref, u_ref, *refs):
    o_ref = refs[-1]
    n, fb = part_ref.shape[0], b_ref.shape[0]
    if len(refs) == 2:
        total = refs[0][...]
    else:
        total = part_ref[0, :, 2 * (fa + fb) :].astype(F32)
        for d in range(1, n):
            total = total + part_ref[d, :, 2 * (fa + fb) :].astype(F32)
    spot = lax.broadcasted_iota(jnp.int32, total.shape, 1) // RANK
    pieces = []
    for q in range(PER_TILE):
        one = jnp.where(spot == q, total, 0.0)
        half = one + pltpu.roll(one, 2 * RANK, 1)
        pieces.append(half + pltpu.roll(half, RANK, 1))
    adapted = jnp.concatenate(pieces, axis=0)
    quarter = lax.broadcasted_iota(jnp.int32, adapted.shape, 1) // RANK
    tenant = u_ref[...]
    spread = [
        jnp.where(tenant == c * PER_TILE + quarter, adapted, 0.0).astype(BF16) for c in range(TENANTS // PER_TILE)
    ]
    old = dot(jnp.concatenate(spread, axis=1), b_ref[...], 1, 1)
    matched = []
    for c in range(n // PER_TILE):
        block = jnp.zeros(adapted.shape, jnp.int32)
        for i in range(PER_TILE):
            block = jnp.where(quarter == i, t_ref[c * PER_TILE + i], block)
        matched.append(jnp.where(tenant == block, adapted, 0.0).astype(BF16))
    up = [part_ref[j, :, up_half(h, fa, fb)] for j in range(n) for h in range(2)]
    change = dot(jnp.concatenate(matched, axis=1), jnp.concatenate(up, axis=0), 1, 0)
    delta = adapter_scale * (old - learning_rate * (adapter_scale * change))
    for d in range(n):
        o_ref[d] = delta[d * ROWS_DEV : (d + 1) * ROWS_DEV]


def attention_kernel(len_ref, delta_ref, base_ref, k_ref, v_ref, o_ref):
    n = delta_ref.shape[0]
    delta = jnp.concatenate([delta_ref[d] for d in range(n)], axis=1)
    query = (base_ref[...] + delta).astype(BF16).astype(F32)
    group = HEADS // KV_HEADS
    cache = k_ref.shape[1]
    many = HEADS * ROWS_DEV
    empty = jnp.zeros((group * ROWS_DEV, HEAD_DIM), F32)
    heads = []
    for g in range(KV_HEADS):
        mine = [query[:, h * HEAD_DIM : (h + 1) * HEAD_DIM] for h in range(g * group, (g + 1) * group)]
        lanes = [empty] * KV_HEADS
        lanes[g] = jnp.concatenate(mine, axis=0)
        heads.append(jnp.concatenate(lanes, axis=1))
    heads = jnp.concatenate(heads, axis=0).astype(BF16)
    row = lax.broadcasted_iota(jnp.int32, (many, cache), 0) % ROWS_DEV
    length = jnp.zeros((many, cache), jnp.int32)
    scores = jnp.zeros((many, cache), F32)
    for r in range(ROWS_DEV):
        length = jnp.where(row == r, len_ref[r], length)
        scores = jnp.where(row == r, dot(heads, k_ref[r], 1, 1), scores)
    live = lax.broadcasted_iota(jnp.int32, (many, cache), 1) < length
    scores = jnp.where(live, scores / jnp.sqrt(F32(HEAD_DIM)), F32(-1e30))
    top = jnp.max(scores, axis=-1, keepdims=True)
    expo = jnp.where(live, jnp.exp(scores - top), 0.0)
    weights = (expo / jnp.sum(expo, axis=-1, keepdims=True)).astype(BF16)
    mixed = [dot(weights, v_ref[r], 1, 0) for r in range(ROWS_DEV)]
    outs = []
    rows = group * ROWS_DEV
    row = lax.broadcasted_iota(jnp.int32, (rows, HEAD_DIM), 0) % ROWS_DEV
    for g in range(KV_HEADS):
        part = jnp.zeros((rows, HEAD_DIM), F32)
        for r in range(ROWS_DEV):
            part = jnp.where(
                row == r, mixed[r][g * rows : (g + 1) * rows, g * HEAD_DIM : (g + 1) * HEAD_DIM], part
            )
        outs.extend(part[i * ROWS_DEV : (i + 1) * ROWS_DEV] for i in range(group))
    o_ref[...] = jnp.concatenate(outs, axis=1).astype(BF16)


def exchange(x):
    return lax.all_to_all(x, "wide", split_axis=0, concat_axis=0, tiled=True)


def partner(x, mask):
    return lax.ppermute(x, "wide", [(i, i ^ mask) for i in range(lax.axis_size("wide"))])


def per_device(
    tokens,
    query_output_gradient,
    down_factors,
    up_factors_transposed,
    tenant_of_block,
    device_tenant_list,
    row_list_entry,
    hidden,
    base_query_rows,
    cached_key_rows,
    cached_value_rows,
    live_cache_length,
):
    n = lax.axis_size("wide")
    me = lax.axis_index("wide").astype(jnp.int32)
    small = n == 16
    fa, cols = down_factors.shape
    fb = up_factors_transposed.shape[0]
    local_rows = hidden.shape[0]
    rows = local_rows * n
    quarter = rows // PER_TILE
    width = tokens.shape[1]
    features = query_output_gradient.shape[1]
    assert tokens.shape[0] == BLOCK and tenant_of_block.shape[0] == n

    shape = (n, HALF, 2 * (fa + fb))
    chunks = 4 if fa % 64 == 0 and fb % 64 == 0 else 1
    packed = call(
        pick_kernel,
        jax.ShapeDtypeStruct(shape, BF16),
        [hbm(), hbm(), hbm()],
        hbm(),
        scratch=[
            pltpu.VMEM(up_factors_transposed.shape, BF16),
            pltpu.VMEM(down_factors.shape, BF16),
            pltpu.VMEM(shape, BF16),
            pltpu.SMEM((n,), jnp.int32),
            pltpu.SemaphoreType.DMA,
            pltpu.SemaphoreType.DMA((chunks,)),
            pltpu.SemaphoreType.DMA((chunks,)),
            pltpu.SemaphoreType.DMA((n,)),
        ],
        flops=2 * RANK * LANES * n * (fa + fb),
        nbytes=2 * cols * (fa + fb),
        limit=PICK_VMEM,
    )(tenant_of_block, up_factors_transposed, down_factors)

    if small:
        held = call(
            rows_pack_kernel,
            jax.ShapeDtypeStruct((HALF, width // CHUNKS + LANES), BF16),
            [smem(), smem(), vmem()],
            vmem(),
            nbytes=4 * local_rows * width,
            limit=ALL_VMEM,
        )(device_tenant_list, row_list_entry, hidden)[None]
        held = jnp.concatenate([held, partner(held, n // 2)], axis=0)
        held, packed = lax.optimization_barrier((held, packed))
        got = exchange(packed)
        masks = [0, n // 2]
        bit = n // 4
        while bit > 1:
            held = lax.optimization_barrier(jnp.concatenate([held, partner(held, bit)], axis=0))
            masks = masks + [m ^ bit for m in masks]
            bit //= 2
        masks = masks + [m ^ 1 for m in masks]
        found = call(
            rows_kernel,
            [jax.ShapeDtypeStruct((n, local_rows, LANES), t) for t in (F32, F32, jnp.int32)],
            [smem()] + [vmem()] * 4,
            [vmem()] * 3,
            scratch=[pltpu.VMEM((n * HALF, fa), BF16)],
            flops=2 * rows * (BLOCK * width + fa * cols),
            nbytes=2 * BLOCK * width + 2 * fa * cols,
        )(me[None], held, partner(held, 1), tokens, down_factors)
        hx, base_low_rank, tenants = ((f,) for f in found)
    else:
        got = exchange(packed)
        slot = row_list_entry[:, None] == jnp.arange(device_tenant_list.shape[1], dtype=jnp.int32)[None, :]
        row_tenant = jnp.sum(jnp.where(slot, device_tenant_list, 0), axis=1)
        everyone = lax.all_gather(hidden, "wide", axis=0, tiled=True)
        tenants = lax.all_gather(row_tenant, "wide", axis=0, tiled=True)
        tenants = jnp.broadcast_to(tenants[:, None], (rows, LANES))
        hx, base_low_rank = call(
            plain_rows_kernel,
            [jax.ShapeDtypeStruct((n, local_rows, LANES), F32)] * 2,
            [vmem()] * 5,
            [vmem()] * 2,
        )(everyone, tokens, down_factors, lax.dynamic_slice(everyone, (0, me * fa), (rows, fa)), tenants)

    if not small:
        masks, hx, base_low_rank = None, (hx,), (base_low_rank,)
        tenants = (tenants.reshape(n, local_rows, LANES),)
    part_shape = (n, HALF, 2 * (fa + fb) + (LANES if small else 0))
    my_tenant = lax.dynamic_slice(tenant_of_block, (me,), (1,))
    parts, tenants, *low_rank = call(
        functools.partial(block_kernel, small, masks),
        [jax.ShapeDtypeStruct(part_shape, BF16), jax.ShapeDtypeStruct((rows, LANES), jnp.int32)]
        + ([] if small else [jax.ShapeDtypeStruct((quarter, LANES), F32)]),
        [smem(), smem()] + [vmem()] * (3 + 3 * len(hx)),
        [vmem()] * (2 if small else 3),
        scratch=[pltpu.VMEM((RANK, width), BF16), pltpu.VMEM((RANK, features), BF16)]
        + [pltpu.VMEM((n, local_rows, LANES), t) for t in (F32, F32, jnp.int32)],
        flops=4 * RANK * BLOCK * n * (fa + fb),
        nbytes=2 * BLOCK * n * (fa + fb),
    )(my_tenant, me[None], tokens, query_output_gradient, got, *hx, *base_low_rank, *tenants)
    low_rank = [lax.psum(p, "wide") for p in low_rank]
    parts = exchange(parts)

    delta = call(
        functools.partial(delta_kernel, fa),
        jax.ShapeDtypeStruct((n, local_rows, fb), F32),
        [smem()] + [vmem()] * (3 + len(low_rank)),
        vmem(),
        flops=2 * rows * cols * fb,
        nbytes=2 * cols * fb,
    )(tenant_of_block, parts, up_factors_transposed, tenants, *low_rank)
    delta = exchange(delta)

    down_gradient, up_gradient = call(
        gradient_kernel,
        [jax.ShapeDtypeStruct((fa, cols), F32), jax.ShapeDtypeStruct((fb, cols), F32)],
        [smem(), vmem()],
        [vmem()] * 2,
        flops=2 * n * RANK * (fa + fb) * LANES,
        nbytes=4 * cols * (fa + fb),
    )(tenant_of_block, parts)
    attended = call(
        attention_kernel,
        jax.ShapeDtypeStruct((local_rows, HEADS * HEAD_DIM), BF16),
        [smem(), vmem(), vmem(), vmem(), vmem()],
        vmem(),
        flops=4 * HEADS * local_rows * cached_key_rows.shape[1] * HEAD_DIM,
        nbytes=4 * cached_key_rows.size,
    )(live_cache_length, delta, base_query_rows.astype(F32), cached_key_rows, cached_value_rows)
    return down_gradient, up_gradient, attended


def solution(mesh):
    placed = (
        P(("groups", "wide"), None),
        P(("groups", "wide"), None),
        P("wide", "groups"),
        P("wide", "groups"),
        P("groups"),
        P(("groups", "wide"), None),
        P(("groups", "wide")),
        P(("groups", "wide"), None),
        P(("groups", "wide"), None),
        P(("groups", "wide"), None, None),
        P(("groups", "wide"), None, None),
        P(("groups", "wide")),
    )
    return jax.shard_map(
        per_device,
        mesh=mesh,
        in_specs=placed,
        out_specs=(P("wide", "groups"), P("wide", "groups"), P(("groups", "wide"), None)),
        check_vma=False,
    )
```

```python
import functools

import jax
import jax.numpy as jnp
from jax import lax
from jax.experimental import pallas as pl
from jax.experimental.pallas import tpu as pltpu
from jax.sharding import PartitionSpec as P

HEAD_DIM = 128
HEADS = 32
KV_HEADS = 4
RANK = 32
TENANTS = 64
BLOCK = 128
ROWS_DEV = 4
LANES = 128
PER_TILE = LANES // RANK

adapter_scale = 2.0
learning_rate = 0.0002

F32 = jnp.float32
BF16 = jnp.bfloat16
VMEM_LIMIT = 24 * 1024 * 1024
ALL_VMEM = 58 * 1024 * 1024 + 768 * 1024


def vmem():
    return pl.BlockSpec(memory_space=pltpu.VMEM)


def smem():
    return pl.BlockSpec(memory_space=pltpu.SMEM)


def hbm():
    return pl.BlockSpec(memory_space=pltpu.HBM)


def call(kernel, out_shape, in_specs, out_specs, scratch=(), flops=0, nbytes=0, limit=VMEM_LIMIT):
    return pl.pallas_call(
        kernel,
        out_shape=out_shape,
        in_specs=in_specs,
        out_specs=out_specs,
        scratch_shapes=list(scratch),
        compiler_params=pltpu.CompilerParams(vmem_limit_bytes=limit),
        cost_estimate=pl.CostEstimate(flops=flops, bytes_accessed=nbytes, transcendentals=0),
    )


def each(count, body):
    if count <= 16:
        for j in range(count):
            body(j)
    else:
        pl.loop(0, count)(body)


def dot(a, b, ca, cb):
    return lax.dot_general(a, b, (((ca,), (cb,)), ((), ())), preferred_element_type=F32)


def quarter_indicator(quarter, value):
    lane = lax.broadcasted_iota(jnp.int32, (RANK, LANES), 1)
    row = lax.broadcasted_iota(jnp.int32, (RANK, LANES), 0)
    return jnp.where(lane - row == quarter * RANK, value, 0.0).astype(BF16)


def tile_of(tenant):
    return pl.ds(pl.multiple_of((tenant // PER_TILE) * LANES, LANES), LANES)


HALF = RANK // 2
CHUNKS = HALF // ROWS_DEV


def up_half(h, fa, fb):
    return slice(h * fb, (h + 1) * fb)


def down_half(h, fa, fb):
    return slice(2 * fb + h * fa, 2 * fb + (h + 1) * fa)


def pick_kernel(tenant_ref, b_ref, a_ref, o_ref, b_tab, a_tab, o_buf, t_ref, sem_t, sem_b, sem_a, sem_o):
    n = t_ref.shape[0]
    fa, fb = a_ref.shape[0], b_ref.shape[0]

    def loads(src, dst, sem):
        step = src.shape[0] // sem.shape[0]
        parts = [slice(c * step, (c + 1) * step) for c in range(sem.shape[0])]
        return [pltpu.make_async_copy(src.at[r], dst.at[r], sem.at[c]) for c, r in enumerate(parts)]

    first, second = loads(b_ref, b_tab, sem_b), loads(a_ref, a_tab, sem_a)
    tenants = pltpu.make_async_copy(tenant_ref, t_ref, sem_t)
    for load in [tenants] + first + second:
        load.start()

    def picked(j, table):
        t = t_ref[j]
        return dot(quarter_indicator(t % PER_TILE, 1.0), table[:, tile_of(t)], 1, 1).astype(BF16)

    def up_body(j):
        up = picked(j, b_tab)
        for h in range(2):
            o_buf[j, :, up_half(h, fa, fb)] = up[h * HALF : (h + 1) * HALF]

    def down_body(j):
        down = picked(j, a_tab)
        for h in range(2):
            o_buf[j, :, down_half(h, fa, fb)] = down[h * HALF : (h + 1) * HALF]
        pltpu.make_async_copy(o_buf.at[j], o_ref.at[j], sem_o.at[j]).start()

    def finish(j):
        pltpu.make_async_copy(o_buf.at[j], o_ref.at[j], sem_o.at[j]).wait()

    for load in [tenants] + first:
        load.wait()
    each(n, up_body)
    for load in second:
        load.wait()
    each(n, down_body)
    each(n, finish)


def rows_pack_kernel(list_ref, slot_ref, hidden_ref, o_ref):
    hidden = hidden_ref[...].astype(F32)
    size = hidden.shape[1] // CHUNKS
    main = jnp.concatenate([hidden[:, p * size : (p + 1) * size] for p in range(CHUNKS)], axis=0)
    row = lax.broadcasted_iota(jnp.int32, (HALF, LANES), 0) % ROWS_DEV
    mark = jnp.zeros((HALF, LANES), jnp.int32)
    for r in range(ROWS_DEV):
        mark = jnp.where(row == r, list_ref[0, slot_ref[r]], mark)
    o_ref[...] = jnp.concatenate([main, mark.astype(F32)], axis=1).astype(BF16)


def fold_rows(product, tenant):
    rows = product.shape[0]
    lane = lax.broadcasted_iota(jnp.int32, (rows, LANES), 1)
    total = jnp.zeros((rows, LANES), F32)
    for c in range(TENANTS // PER_TILE):
        mine = tenant == c * PER_TILE + lane // RANK
        total = total + jnp.where(mine, product[:, c * LANES : (c + 1) * LANES], 0.0)
    half = total + pltpu.roll(total, 2 * RANK, 1)
    return half + pltpu.roll(half, RANK, 1)


def rows_kernel(me_ref, h0_ref, h1_ref, x_ref, a_ref, hx_ref, base_ref, u_ref, sel):
    h = jnp.concatenate([r[k] for r in (h0_ref, h1_ref) for k in range(r.shape[0])], axis=0)
    tiles = h.shape[0] // HALF
    size = h.shape[1] - LANES
    fa = a_ref.shape[0]

    def group(value, p):
        first = [k * HALF + p * ROWS_DEV for k in range(tiles)]
        return jnp.concatenate([value[f : f + ROWS_DEV] for f in first], axis=0)

    per_chunk = size // fa
    for m in range(per_chunk):

        @pl.when(me_ref[0] % per_chunk == m)
        def _():
            sel[...] = h[:, m * fa : (m + 1) * fa]

    wide = h.astype(F32)
    hx = jnp.zeros((tiles * ROWS_DEV, BLOCK), F32)
    for p in range(CHUNKS):
        chunk = group(wide[:, :size], p).astype(BF16)
        hx = hx + dot(chunk, x_ref[:, p * size : (p + 1) * size], 1, 1)
    tenant = group(wide[:, size:], 0).astype(jnp.int32)
    mine = sel[...].astype(F32)
    cols = group(mine, 0)
    for p in range(1, CHUNKS):
        cols = jnp.where(me_ref[0] // per_chunk == p, group(mine, p), cols)
    base = fold_rows(dot(cols.astype(BF16), a_ref[...], 1, 0), tenant)
    for k in range(tiles):
        rows = slice(k * ROWS_DEV, (k + 1) * ROWS_DEV)
        hx_ref[k], base_ref[k], u_ref[k] = hx[rows], base[rows], tenant[rows]


def plain_rows_kernel(h_ref, x_ref, a_ref, hc_ref, u_ref, hx_ref, base_ref):
    hx = dot(h_ref[...], x_ref[...], 1, 1)
    base = fold_rows(dot(hc_ref[...], a_ref[...], 1, 0), u_ref[...])
    for d in range(hx_ref.shape[0]):
        hx_ref[d] = hx[d * ROWS_DEV : (d + 1) * ROWS_DEV]
        base_ref[d] = base[d * ROWS_DEV : (d + 1) * ROWS_DEV]


def block_kernel(ride, masks, t_ref, me_ref, x_ref, g_ref, r_ref, *refs):
    sets = (len(refs) - (7 if ride else 8)) // 3
    hx_sets, base_sets, u_sets = (refs[i * sets : (i + 1) * sets] for i in range(3))
    o_ref, u_ref = refs[3 * sets : 3 * sets + 2]
    wa_ref, wb_ref, sx, sb, su = refs[-5:]
    n = r_ref.shape[0]
    fa, fb = x_ref.shape[1] // n, g_ref.shape[1] // n
    for d in range(n):
        for h in range(2):
            rank = slice(h * HALF, (h + 1) * HALF)
            wb_ref[rank, d * fb : (d + 1) * fb] = r_ref[d, :, up_half(h, fa, fb)]
            wa_ref[rank, d * fa : (d + 1) * fa] = r_ref[d, :, down_half(h, fa, fb)]
    back = dot(wb_ref[...], g_ref[...], 1, 1).astype(BF16)
    down = dot(wa_ref[...], x_ref[...], 1, 1).astype(BF16)

    k = 0
    for hx_ref, base_ref, tile_ref in zip(hx_sets, base_sets, u_sets):
        for i in range(hx_ref.shape[0]):
            d = me_ref[0] ^ masks[k] if masks else i
            sx[d], sb[d], su[d] = hx_ref[i], base_ref[i], tile_ref[i]
            k += 1
    hx, base, tenant = (jnp.concatenate([v[d] for d in range(n)], axis=0) for v in (sx, sb, su))
    u_ref[...] = tenant
    high = hx.astype(BF16)
    low = (hx - high.astype(F32)).astype(BF16)
    wide_back = jnp.concatenate([back] * PER_TILE, axis=0)
    change = dot(high, wide_back, 1, 1) + dot(low, wide_back, 1, 1)
    mine = tenant == t_ref[0]
    full = base - jnp.where(mine, learning_rate * (adapter_scale * change), 0.0)
    quarter = full.shape[0] // PER_TILE
    spot = lax.broadcasted_iota(jnp.int32, (quarter, LANES), 1) // RANK
    packed = jnp.zeros((quarter, LANES), F32)
    for q in range(PER_TILE):
        packed = packed + jnp.where(spot == q, full[q * quarter : (q + 1) * quarter], 0.0)
    if not ride:
        refs[3 * sets + 2][...] = packed

    down_part = dot(back, x_ref[...], 1, 0).astype(BF16)
    up_part = dot(down, g_ref[...], 1, 0).astype(BF16)
    for d in range(n):
        for h in range(2):
            rank = slice(h * HALF, (h + 1) * HALF)
            o_ref[d, :, up_half(h, fa, fb)] = up_part[rank, d * fb : (d + 1) * fb]
            o_ref[d, :, down_half(h, fa, fb)] = down_part[rank, d * fa : (d + 1) * fa]
        if ride:
            o_ref[d, :, 2 * (fa + fb) :] = packed.astype(BF16)


def sum_by_tenant(t_ref, part_ref, cut, fa, fb, grad_ref):
    grad_ref[...] = jnp.zeros_like(grad_ref)

    def body(j):
        t = t_ref[j]
        part = jnp.concatenate([part_ref[j, :, cut(h, fa, fb)] for h in range(2)], axis=0)
        place = quarter_indicator(t % PER_TILE, adapter_scale)
        grad_ref[:, tile_of(t)] += dot(part, place, 0, 0)

    each(t_ref.shape[0], body)


def gradient_kernel(t_ref, part_ref, down_ref, up_ref):
    fa, fb = down_ref.shape[0], up_ref.shape[0]
    sum_by_tenant(t_ref, part_ref, down_half, fa, fb, down_ref)
    sum_by_tenant(t_ref, part_ref, up_half, fa, fb, up_ref)


def delta_kernel(fa, t_ref, part_ref, b_ref, u_ref, *refs):
    o_ref = refs[-1]
    n, fb = part_ref.shape[0], b_ref.shape[0]
    if len(refs) == 2:
        total = refs[0][...]
    else:
        total = part_ref[0, :, 2 * (fa + fb) :].astype(F32)
        for d in range(1, n):
            total = total + part_ref[d, :, 2 * (fa + fb) :].astype(F32)
    spot = lax.broadcasted_iota(jnp.int32, total.shape, 1) // RANK
    pieces = []
    for q in range(PER_TILE):
        one = jnp.where(spot == q, total, 0.0)
        half = one + pltpu.roll(one, 2 * RANK, 1)
        pieces.append(half + pltpu.roll(half, RANK, 1))
    adapted = jnp.concatenate(pieces, axis=0)
    quarter = lax.broadcasted_iota(jnp.int32, adapted.shape, 1) // RANK
    tenant = u_ref[...]
    spread = [
        jnp.where(tenant == c * PER_TILE + quarter, adapted, 0.0).astype(BF16) for c in range(TENANTS // PER_TILE)
    ]
    old = dot(jnp.concatenate(spread, axis=1), b_ref[...], 1, 1)
    matched = []
    for c in range(n // PER_TILE):
        block = jnp.zeros(adapted.shape, jnp.int32)
        for i in range(PER_TILE):
            block = jnp.where(quarter == i, t_ref[c * PER_TILE + i], block)
        matched.append(jnp.where(tenant == block, adapted, 0.0).astype(BF16))
    up = [part_ref[j, :, up_half(h, fa, fb)] for j in range(n) for h in range(2)]
    change = dot(jnp.concatenate(matched, axis=1), jnp.concatenate(up, axis=0), 1, 0)
    delta = adapter_scale * (old - learning_rate * (adapter_scale * change))
    for d in range(n):
        o_ref[d] = delta[d * ROWS_DEV : (d + 1) * ROWS_DEV].astype(BF16)


def attention_kernel(len_ref, delta_ref, base_ref, k_ref, v_ref, o_ref):
    n = delta_ref.shape[0]
    delta = jnp.concatenate([delta_ref[d].astype(F32) for d in range(n)], axis=1)
    query = (base_ref[...] + delta).astype(BF16).astype(F32)
    group = HEADS // KV_HEADS
    cache = k_ref.shape[1]
    many = HEADS * ROWS_DEV
    empty = jnp.zeros((group * ROWS_DEV, HEAD_DIM), F32)
    heads = []
    for g in range(KV_HEADS):
        mine = [query[:, h * HEAD_DIM : (h + 1) * HEAD_DIM] for h in range(g * group, (g + 1) * group)]
        lanes = [empty] * KV_HEADS
        lanes[g] = jnp.concatenate(mine, axis=0)
        heads.append(jnp.concatenate(lanes, axis=1))
    heads = jnp.concatenate(heads, axis=0).astype(BF16)
    row = lax.broadcasted_iota(jnp.int32, (many, cache), 0) % ROWS_DEV
    length = jnp.zeros((many, cache), jnp.int32)
    scores = jnp.zeros((many, cache), F32)
    for r in range(ROWS_DEV):
        length = jnp.where(row == r, len_ref[r], length)
        scores = jnp.where(row == r, dot(heads, k_ref[r], 1, 1), scores)
    live = lax.broadcasted_iota(jnp.int32, (many, cache), 1) < length
    scores = jnp.where(live, scores / jnp.sqrt(F32(HEAD_DIM)), F32(-1e30))
    top = jnp.max(scores, axis=-1, keepdims=True)
    expo = jnp.where(live, jnp.exp(scores - top), 0.0)
    weights = (expo / jnp.sum(expo, axis=-1, keepdims=True)).astype(BF16)
    mixed = [dot(weights, v_ref[r], 1, 0) for r in range(ROWS_DEV)]
    outs = []
    rows = group * ROWS_DEV
    row = lax.broadcasted_iota(jnp.int32, (rows, HEAD_DIM), 0) % ROWS_DEV
    for g in range(KV_HEADS):
        part = jnp.zeros((rows, HEAD_DIM), F32)
        for r in range(ROWS_DEV):
            part = jnp.where(
                row == r, mixed[r][g * rows : (g + 1) * rows, g * HEAD_DIM : (g + 1) * HEAD_DIM], part
            )
        outs.extend(part[i * ROWS_DEV : (i + 1) * ROWS_DEV] for i in range(group))
    o_ref[...] = jnp.concatenate(outs, axis=1).astype(BF16)


def exchange(x):
    return lax.all_to_all(x, "wide", split_axis=0, concat_axis=0, tiled=True)


def partner(x, mask):
    return lax.ppermute(x, "wide", [(i, i ^ mask) for i in range(lax.axis_size("wide"))])


def per_device(
    tokens,
    query_output_gradient,
    down_factors,
    up_factors_transposed,
    tenant_of_block,
    device_tenant_list,
    row_list_entry,
    hidden,
    base_query_rows,
    cached_key_rows,
    cached_value_rows,
    live_cache_length,
):
    n = lax.axis_size("wide")
    me = lax.axis_index("wide").astype(jnp.int32)
    small = n == 16
    fa, cols = down_factors.shape
    fb = up_factors_transposed.shape[0]
    local_rows = hidden.shape[0]
    rows = local_rows * n
    quarter = rows // PER_TILE
    width = tokens.shape[1]
    features = query_output_gradient.shape[1]
    assert tokens.shape[0] == BLOCK and tenant_of_block.shape[0] == n

    shape = (n, HALF, 2 * (fa + fb))
    chunks = 4 if fa % 64 == 0 and fb % 64 == 0 else 1
    packed = call(
        pick_kernel,
        jax.ShapeDtypeStruct(shape, BF16),
        [hbm(), hbm(), hbm()],
        hbm(),
        scratch=[
            pltpu.VMEM(up_factors_transposed.shape, BF16),
            pltpu.VMEM(down_factors.shape, BF16),
            pltpu.VMEM(shape, BF16),
            pltpu.SMEM((n,), jnp.int32),
            pltpu.SemaphoreType.DMA,
            pltpu.SemaphoreType.DMA((chunks,)),
            pltpu.SemaphoreType.DMA((chunks,)),
            pltpu.SemaphoreType.DMA((n,)),
        ],
        flops=2 * RANK * LANES * n * (fa + fb),
        nbytes=2 * cols * (fa + fb),
        limit=ALL_VMEM,
    )(tenant_of_block, up_factors_transposed, down_factors)

    if small:
        held = call(
            rows_pack_kernel,
            jax.ShapeDtypeStruct((HALF, width // CHUNKS + LANES), BF16),
            [smem(), smem(), vmem()],
            vmem(),
            nbytes=4 * local_rows * width,
            limit=ALL_VMEM,
        )(device_tenant_list, row_list_entry, hidden)[None]
        held = jnp.concatenate([held, partner(held, n // 2)], axis=0)
        held, packed = lax.optimization_barrier((held, packed))
        got = exchange(packed)
        masks = [0, n // 2]
        bit = n // 4
        while bit > 1:
            held = lax.optimization_barrier(jnp.concatenate([held, partner(held, bit)], axis=0))
            masks = masks + [m ^ bit for m in masks]
            bit //= 2
        masks = masks + [m ^ 1 for m in masks]
        found = call(
            rows_kernel,
            [jax.ShapeDtypeStruct((n, local_rows, LANES), t) for t in (F32, F32, jnp.int32)],
            [smem()] + [vmem()] * 4,
            [vmem()] * 3,
            scratch=[pltpu.VMEM((n * HALF, fa), BF16)],
            flops=2 * rows * (BLOCK * width + fa * cols),
            nbytes=2 * BLOCK * width + 2 * fa * cols,
        )(me[None], held, partner(held, 1), tokens, down_factors)
        hx, base_low_rank, tenants = ((f,) for f in found)
    else:
        got = exchange(packed)
        slot = row_list_entry[:, None] == jnp.arange(device_tenant_list.shape[1], dtype=jnp.int32)[None, :]
        row_tenant = jnp.sum(jnp.where(slot, device_tenant_list, 0), axis=1)
        everyone = lax.all_gather(hidden, "wide", axis=0, tiled=True)
        tenants = lax.all_gather(row_tenant, "wide", axis=0, tiled=True)
        tenants = jnp.broadcast_to(tenants[:, None], (rows, LANES))
        hx, base_low_rank = call(
            plain_rows_kernel,
            [jax.ShapeDtypeStruct((n, local_rows, LANES), F32)] * 2,
            [vmem()] * 5,
            [vmem()] * 2,
        )(everyone, tokens, down_factors, lax.dynamic_slice(everyone, (0, me * fa), (rows, fa)), tenants)

    if not small:
        masks, hx, base_low_rank = None, (hx,), (base_low_rank,)
        tenants = (tenants.reshape(n, local_rows, LANES),)
    part_shape = (n, HALF, 2 * (fa + fb) + (LANES if small else 0))
    my_tenant = lax.dynamic_slice(tenant_of_block, (me,), (1,))
    parts, tenants, *low_rank = call(
        functools.partial(block_kernel, small, masks),
        [jax.ShapeDtypeStruct(part_shape, BF16), jax.ShapeDtypeStruct((rows, LANES), jnp.int32)]
        + ([] if small else [jax.ShapeDtypeStruct((quarter, LANES), F32)]),
        [smem(), smem()] + [vmem()] * (3 + 3 * len(hx)),
        [vmem()] * (2 if small else 3),
        scratch=[pltpu.VMEM((RANK, width), BF16), pltpu.VMEM((RANK, features), BF16)]
        + [pltpu.VMEM((n, local_rows, LANES), t) for t in (F32, F32, jnp.int32)],
        flops=4 * RANK * BLOCK * n * (fa + fb),
        nbytes=2 * BLOCK * n * (fa + fb),
    )(my_tenant, me[None], tokens, query_output_gradient, got, *hx, *base_low_rank, *tenants)
    low_rank = [lax.psum(p, "wide") for p in low_rank]
    parts = exchange(parts)

    delta = call(
        functools.partial(delta_kernel, fa),
        jax.ShapeDtypeStruct((n, local_rows, fb), BF16),
        [smem()] + [vmem()] * (3 + len(low_rank)),
        vmem(),
        flops=2 * rows * cols * fb,
        nbytes=2 * cols * fb,
    )(tenant_of_block, parts, up_factors_transposed, tenants, *low_rank)
    delta = exchange(delta)

    down_gradient, up_gradient = call(
        gradient_kernel,
        [jax.ShapeDtypeStruct((fa, cols), F32), jax.ShapeDtypeStruct((fb, cols), F32)],
        [smem(), vmem()],
        [vmem()] * 2,
        flops=2 * n * RANK * (fa + fb) * LANES,
        nbytes=4 * cols * (fa + fb),
    )(tenant_of_block, parts)
    attended = call(
        attention_kernel,
        jax.ShapeDtypeStruct((local_rows, HEADS * HEAD_DIM), BF16),
        [smem(), vmem(), vmem(), vmem(), vmem()],
        vmem(),
        flops=4 * HEADS * local_rows * cached_key_rows.shape[1] * HEAD_DIM,
        nbytes=4 * cached_key_rows.size,
    )(live_cache_length, delta, base_query_rows.astype(F32), cached_key_rows, cached_value_rows)
    return down_gradient, up_gradient, attended


def solution(mesh):
    placed = (
        P(("groups", "wide"), None),
        P(("groups", "wide"), None),
        P("wide", "groups"),
        P("wide", "groups"),
        P("groups"),
        P(("groups", "wide"), None),
        P(("groups", "wide")),
        P(("groups", "wide"), None),
        P(("groups", "wide"), None),
        P(("groups", "wide"), None, None),
        P(("groups", "wide"), None, None),
        P(("groups", "wide")),
    )
    return jax.shard_map(
        per_device,
        mesh=mesh,
        in_specs=placed,
        out_specs=(P("wide", "groups"), P("wide", "groups"), P(("groups", "wide"), None)),
        check_vma=False,
    )
```
